32 devices in a mesh: groups: 2 (over x), blk: 8 (over z, y), rep: 2 (over core).
Axes of the slice: x: 2, y: 2, z: 4, core: 2. Of those that a mesh axis runs over, the one named last changes fastest.
Arguments:
- projections: bfloat16 [512, 8, 36, 1024], P(('groups', 'blk', 'rep')), parts along dimension 0, may hold values from -6 to 6
- images: bfloat16 [512, 36, 1024], P(('groups', 'blk', 'rep')), parts along dimension 0, may hold values from -6 to 6
- transfer: bfloat16 [512, 36, 1024], P(('groups', 'blk', 'rep')), parts along dimension 0, may hold values from -1 to 1
- pose_weights: float32 [512, 8], P(('groups', 'blk', 'rep')), parts along dimension 0, may hold values from 0 to 1
- pose_of: int32 [512, 8], P(('groups', 'blk', 'rep')), parts along dimension 0, may hold values from 0 to 511
- pose_blocks: int32 [1024, 36], P('groups'), parts along dimension 0, may hold values from 0 to 63
- pose_tiles: int32 [1024, 36], P('groups'), parts along dimension 0, may hold values from 0 to 15
- weight_bank: float32 [16, 32, 1024], replicated, may hold values from -0.18 to 0.18
Outputs:
- map_gradient: float32 [128, 32, 1024], P(('groups', 'blk')), parts along dimension 0
The draws below stay inside these ranges and needn't reach their ends.
There are 2 independent parts, one for each index of `groups`. The reference program is written for one: setup_inputs(seed, part) draws one part's arguments, and reference() takes and returns one part's arrays. A program takes and returns all parts, laid end to end along the dimension named above; an argument that names none is the same for every part. Nothing has to cross between parts.
All inputs are finite; a program needn't handle non-finite values.
Results may differ from the reference program's by a relative error of at most 0.0003.
Values sent between devices are 32-bit elements; how exact they have to be, the bound alone decides.
No kernel may reach another device: no remote copies, remote signals or barrier semaphores. Data moves between devices by JAX's collectives and lax.ppermute only.
A program may use at most 128 MiB of HBM per device.

```python
import math
import jax
import jax.numpy as jnp
import numpy as np
from jax import lax

BD = 32
BQ = 1024
TILES = 36
K = 8
NW = 16
NPOSE = 512
PART_DEV = 16
PARTICLES = 256
NBLK = 64


def with_ends(array, stream_key, least, high):
    longest = array.shape.index(max(array.shape))
    spots = []
    for shift in (0, 1):
        where = [jax.random.randint(jax.random.fold_in(stream_key, axis), (), 0, length) for axis, length in enumerate(array.shape)]
        where[longest] = (where[longest] + shift) % array.shape[longest]
        spots.append(tuple(where))
    return array.at[spots[0]].set(least).at[spots[1]].set(high)


def level_of(stream_key, extent, shards, least, largest):
    def one(position, parts):
        draws = jax.random.uniform(jax.random.fold_in(jax.random.fold_in(stream_key, 6), position), (parts,), jnp.float32, least / len(shards), largest / len(shards))
        return jnp.repeat(jnp.exp(draws), extent[position] // parts).reshape((-1,) + (1,) * (len(extent) - position - 1))

    gain = one(*shards[0])
    for cut in shards[1:]:
        gain = gain * one(*cut)
    return gain


def rank_table(number_of, slope):
    weights = [(1 << 20) // math.isqrt(rank ** slope) + 1 for rank in range(1, number_of + 1)]
    width = 1 + sum(weights) // (1 << 30)
    return np.cumsum(np.array([max(1, weight // width) for weight in weights]))


def ranked(key, dims, number_of, skew):
    table = rank_table(number_of, skew)
    lot = jax.random.randint(jax.random.fold_in(key, 1), dims, 0, int(table[number_of - 1]))
    standing = jnp.searchsorted(jnp.asarray(table, jnp.int32), lot, side="right")
    return jax.random.permutation(jax.random.fold_in(key, 2), number_of)[standing].astype(jnp.int32)


def bell_draw(key, shape, width, most, split=(), kind=jnp.bfloat16):
    array = jax.random.normal(key, shape, jnp.float32) * width
    if len(split) > 0:
        array = level_of(key, shape, split, -0.22, 0.18) * array
    return jnp.clip(array, min=-most, max=most).astype(kind)


def setup_inputs(seed: int = 0, part: int = 0) -> dict:
    streams_of = jax.random.split(jax.random.key(seed), 9)
    part_keys = jax.random.split(jax.random.fold_in(streams_of[8], part), 9)
    return {
        "projections": bell_draw(part_keys[0], (PARTICLES, K, TILES, BQ), 1.0, 6.0, ((0, 16),)),
        "images": bell_draw(part_keys[1], (PARTICLES, TILES, BQ), 1.0, 6.0, ((0, 16),)),
        "transfer": jnp.clip(jax.random.uniform(part_keys[2], (PARTICLES, TILES, BQ), jnp.float32, -1.0, 1.0) * level_of(part_keys[2], (PARTICLES, TILES, BQ), ((0, 16),), -0.4, 0.0), -1.0, 1.0).astype(jnp.bfloat16),
        "pose_weights": jnp.clip(1.0 * jax.random.uniform(part_keys[3], (PARTICLES, K), jnp.float32) ** level_of(part_keys[3], (PARTICLES, K), ((0, 16),), -0.2, 0.2), 0.0, 1.0),
        "pose_of": with_ends(jax.random.randint(part_keys[4], (PARTICLES, K), 0, NPOSE), jax.random.fold_in(part_keys[4], 1), 0, NPOSE - 1).astype(jnp.int32),
        "pose_blocks": with_ends(ranked(part_keys[5], (NPOSE, TILES), NBLK, 1), jax.random.fold_in(part_keys[5], 3), 0, NBLK - 1).astype(jnp.int32),
        "pose_tiles": with_ends(jax.random.randint(part_keys[6], (NPOSE, TILES), 0, NW), jax.random.fold_in(part_keys[6], 1), 0, NW - 1).astype(jnp.int32),
        "weight_bank": bell_draw(streams_of[7], (NW, BD, BQ), 0.03, 0.18, (), jnp.float32),
    }


def reference(projections, images, transfer, pose_weights, pose_of, pose_blocks, pose_tiles, weight_bank):
    groups_count = PARTICLES // PART_DEV

    def add_group(carry, inputs):
        proj_part, image_part, transfer_part, weight_part, pose_part = inputs
        transfer_f = transfer_part.astype(jnp.float32)[:, None]
        residual = transfer_f * proj_part.astype(jnp.float32) - image_part.astype(jnp.float32)[:, None]
        contrib = weight_part[:, :, None, None] * transfer_f * residual
        block_ids = pose_blocks[pose_part]
        tile_ids = pose_tiles[pose_part]
        segment = (block_ids * NW + tile_ids).reshape(-1).astype(jnp.int32)
        summed = jax.ops.segment_sum(contrib.reshape(-1, BQ), segment, num_segments=NBLK * NW)
        return carry + summed, None

    stacked = (
        projections.reshape(groups_count, PART_DEV, K, TILES, BQ),
        images.reshape(groups_count, PART_DEV, TILES, BQ),
        transfer.reshape(groups_count, PART_DEV, TILES, BQ),
        pose_weights.reshape(groups_count, PART_DEV, K),
        pose_of.reshape(groups_count, PART_DEV, K),
    )
    start_sums = jnp.zeros((NBLK * NW, BQ), jnp.float32)
    tile_sums, unused = lax.scan(add_group, start_sums, stacked)
    tile_sums = tile_sums.reshape(NBLK, NW, BQ)
    return jnp.einsum("tzq,btq->bzq", weight_bank, tile_sums, precision=lax.Precision.HIGHEST)
```

```python
import functools

import jax
import jax.numpy as jnp
from jax import lax
from jax.experimental import pallas as pl
from jax.experimental.pallas import tpu as pltpu
from jax.sharding import PartitionSpec as P

NB_DEV = 8
LANES = 128
SUB = 8
MIB = 1 << 20
UNROLL = 4


def accumulate_kernel(
    bank_size, n_acc,
    proj_hbm, img_hbm, tra_hbm, w_smem, pose_hbm, blocks_hbm, tiles_hbm,
    out_hbm,
    proj, img, tra, pose, blocks, tiles, idx_v, idx_s, square, cross, *rest,
):
    parts, accs = rest[:UNROLL], rest[UNROLL : UNROLL + n_acc]
    proj_sem, small_sem, table_sem, idx_sem, out_sem = rest[UNROLL + n_acc :]
    n_part, n_tile, n_pose, n_cell = proj.shape
    n_col = n_cell // LANES
    n_table = blocks.shape[1]
    n_row = accs[0].shape[0]

    table_copies = [
        pltpu.make_async_copy(src, dst, table_sem.at[i])
        for i, (src, dst) in enumerate(((pose_hbm, pose), (blocks_hbm, blocks), (tiles_hbm, tiles)))
    ]
    small_copies = [
        pltpu.make_async_copy(img_hbm, img, small_sem.at[0]),
        pltpu.make_async_copy(tra_hbm, tra, small_sem.at[1]),
    ]
    for copy in table_copies + small_copies:
        copy.start()

    def proj_copy(p):
        return pltpu.make_async_copy(proj_hbm.at[p], proj.at[p], proj_sem.at[p])

    for p in range(n_part):
        proj_copy(p).start()

    for copy in table_copies:
        copy.wait()
    lane = lax.broadcasted_iota(jnp.int32, (n_pose, n_table), 1)
    chosen = jnp.concatenate(
        [(pose[:, p : p + 1] == lane).astype(jnp.float32) for p in range(n_part)], axis=0
    ).astype(jnp.bfloat16)

    def look_up(table):
        return lax.dot_general(
            chosen, table[...].astype(jnp.float32).astype(jnp.bfloat16),
            (((1,), (1,)), ((), ())), preferred_element_type=jnp.float32,
        )

    idx_v[:, :n_tile] = ((look_up(blocks) * bank_size + look_up(tiles)) * SUB).astype(jnp.int32)
    idx_copy = pltpu.make_async_copy(idx_v, idx_s, idx_sem)
    idx_copy.start()

    zero = jnp.zeros((8 * SUB, LANES), jnp.float32)

    @pl.loop(0, n_row // (8 * SUB))
    def _(i):
        rows = pl.ds(pl.multiple_of(i * (8 * SUB), 8 * SUB), 8 * SUB)
        for acc in accs:
            acc[rows, :] = zero

    for copy in small_copies:
        copy.wait()

    @pl.loop(0, n_tile)
    def _(j):
        for c in range(n_col):
            cols = slice(c * LANES, (c + 1) * LANES)
            rows = slice(c * n_part, (c + 1) * n_part)
            t = tra[j, :, cols].astype(jnp.float32)
            square[j, rows, :] = t * t
            cross[j, rows, :] = t * img[j, :, cols].astype(jnp.float32)

    idx_copy.wait()

    @pl.loop(0, n_part)
    def _(p):
        proj_copy(p).wait()
        weights = [jnp.full((n_col, LANES), w_smem[k, p], jnp.float32) for k in range(n_pose)]

        @pl.loop(0, n_tile // UNROLL)
        def _(i):
            for u, part in enumerate(parts):
                j = i * UNROLL + u
                for c in range(n_col):
                    x = proj[p, j, :, c * LANES : (c + 1) * LANES].astype(jnp.float32)
                    part[c * n_pose : (c + 1) * n_pose, :] = x
                cell = pl.ds(p, n_col, stride=n_part)
                tt = square[j, cell, :]
                ti = cross[j, cell, :]
                for k in range(n_pose):
                    x = part[pl.ds(k, n_col, stride=n_pose), :]
                    row = pl.ds(pl.multiple_of(idx_s[p * n_pose + k, j], SUB), SUB)
                    acc = accs[k % n_acc]
                    acc[row, :] += (tt * x - ti) * weights[k]

    chunk = 64 * SUB
    n_chunk = n_row // chunk
    step = chunk // 16

    def out_copy(i):
        rows = pl.ds(pl.multiple_of(i * chunk, chunk), chunk)
        return pltpu.make_async_copy(accs[0].at[rows, :], out_hbm.at[rows, :], out_sem.at[i])

    @pl.loop(0, n_chunk)
    def _(i):
        @pl.loop(0, chunk // step)
        def _(h):
            rows = pl.ds(pl.multiple_of(i * chunk + h * step, step), step)
            total = accs[0][rows, :]
            for acc in accs[1:]:
                total += acc[rows, :]
            accs[0][rows, :] = total
        out_copy(i).start()

    @pl.loop(0, n_chunk)
    def _(i):
        out_copy(i).wait()


def accumulate(projections, images, transfer, pose_weights, pose_of, pose_blocks, pose_tiles, total, bank_size):
    n_part, n_pose, n_tile, n_cell = projections.shape
    n_col = n_cell // LANES
    n_acc = 4 if total * n_cell * 4 * 4 <= 16 * MIB else 2
    n_row = total * n_col
    n_idx = n_part * n_pose
    projections = jnp.transpose(projections, (0, 2, 1, 3))
    images, transfer = jnp.transpose(images, (1, 0, 2)), jnp.transpose(transfer, (1, 0, 2))
    anywhere = pl.BlockSpec(memory_space=pl.ANY)
    return pl.pallas_call(
        functools.partial(accumulate_kernel, bank_size, n_acc),
        out_shape=jax.ShapeDtypeStruct((n_row, LANES), jnp.float32),
        in_specs=[anywhere] * 3 + [pl.BlockSpec(memory_space=pltpu.SMEM)] + [anywhere] * 3,
        out_specs=anywhere,
        scratch_shapes=[
            pltpu.VMEM(projections.shape, jnp.bfloat16),
            pltpu.VMEM(images.shape, jnp.bfloat16),
            pltpu.VMEM(transfer.shape, jnp.bfloat16),
            pltpu.VMEM((n_pose, n_part), jnp.int32),
            pltpu.VMEM(pose_blocks.shape[::-1], jnp.int32),
            pltpu.VMEM(pose_tiles.shape[::-1], jnp.int32),
            pltpu.VMEM((n_idx, LANES), jnp.int32),
            pltpu.SMEM((n_idx, LANES), jnp.int32),
            pltpu.VMEM((n_tile, n_col * n_part, LANES), jnp.float32),
            pltpu.VMEM((n_tile, n_col * n_part, LANES), jnp.float32),
        ]
        + [pltpu.VMEM((n_pose * n_col, LANES), jnp.float32)] * UNROLL
        + [pltpu.VMEM((n_row, LANES), jnp.float32)] * n_acc
        + [
            pltpu.SemaphoreType.DMA((n_part,)),
            pltpu.SemaphoreType.DMA((2,)),
            pltpu.SemaphoreType.DMA((3,)),
            pltpu.SemaphoreType.DMA,
            pltpu.SemaphoreType.DMA((n_row // (64 * SUB),)),
        ],
        compiler_params=pltpu.CompilerParams(vmem_limit_bytes=60 * MIB),
        name="accumulate",
    )(projections, images, transfer, pose_weights.T, pose_of.T, pose_blocks.T, pose_tiles.T)


def bank_kernel(sums, bank, out):
    bank_size, n_z, n_cell = bank.shape
    n_blk = out.shape[0]
    group = 2 * SUB

    for c in range(n_cell // LANES):
        cols = slice(c * LANES, (c + 1) * LANES)

        @pl.loop(0, n_z // group)
        def _(g):
            rows = pl.ds(pl.multiple_of(g * group, group), group)
            weights = [bank[t, rows, cols] for t in range(bank_size)]
            for b in range(n_blk):
                total = weights[0] * sums[b * bank_size, c : c + 1, :]
                for t in range(1, bank_size):
                    total += weights[t] * sums[b * bank_size + t, c : c + 1, :]
                out[b, rows, cols] = total


def apply_bank(sums, weight_bank, n_blk):
    bank_size, n_z, n_cell = weight_bank.shape
    vmem = pl.BlockSpec(memory_space=pltpu.VMEM)
    return pl.pallas_call(
        bank_kernel,
        out_shape=jax.ShapeDtypeStruct((n_blk, n_z, n_cell), jnp.float32),
        in_specs=[vmem, vmem],
        out_specs=vmem,
        compiler_params=pltpu.CompilerParams(vmem_limit_bytes=32 * MIB),
        name="apply_bank",
    )(sums, weight_bank)


def body(
    projections, images, transfer, pose_weights, pose_of, pose_blocks, pose_tiles, weight_bank
):
    bank_size = weight_bank.shape[0]
    n_cell = projections.shape[-1]
    total = NB_DEV * lax.axis_size("blk") * bank_size
    sums = accumulate(
        projections, images, transfer, pose_weights, pose_of, pose_blocks, pose_tiles, total, bank_size
    )
    sums = sums.reshape(total, n_cell // LANES, LANES)
    owned = lax.psum_scatter(sums, ("blk", "rep"), scatter_dimension=0, tiled=True)
    owned = lax.all_gather(owned, "rep", axis=0, tiled=True)
    return apply_bank(owned, weight_bank, NB_DEV)


def solution(mesh):
    placed = (
        P(("groups", "blk", "rep"), None, None, None),
        P(("groups", "blk", "rep"), None, None),
        P(("groups", "blk", "rep"), None, None),
        P(("groups", "blk", "rep"), None),
        P(("groups", "blk", "rep"), None),
        P("groups", None),
        P("groups", None),
        P(),
    )
    return jax.shard_map(
        body,
        mesh=mesh,
        in_specs=placed,
        out_specs=P(("groups", "blk"), None, None),
        check_vma=False,
    )
```

```python
import functools

import jax
import jax.numpy as jnp
from jax import lax
from jax.experimental import pallas as pl
from jax.experimental.pallas import tpu as pltpu
from jax.sharding import PartitionSpec as P

NB_DEV = 8
LANES = 128
SUB = 8
MIB = 1 << 20
N_ACC = 4
N_CHUNK = 4


def accumulate_kernel(
    bank_size, n_owner, n_chunk,
    rep_smem, proj_hbm, img_hbm, tra_hbm, w_smem, pose_hbm, blocks_hbm, tiles_hbm,
    *rest,
):
    outs, rest = rest[: 2 * n_chunk], rest[2 * n_chunk :]
    proj, img, tra, pose, blocks, tiles, idx_v, idx_s, square, cross = rest[:10]
    accs = rest[10 : 10 + N_ACC]
    proj_sem, small_sem, table_sem, idx_sem, out_sem = rest[10 + N_ACC :]
    n_pose, n_part = pose.shape
    n_tile, n_table = blocks.shape
    n_row = accs[0].shape[0]
    group = 4 * SUB * SUB

    table_copies = [
        pltpu.make_async_copy(src, dst, table_sem.at[i])
        for i, (src, dst) in enumerate(((pose_hbm, pose), (blocks_hbm, blocks), (tiles_hbm, tiles)))
    ]
    small_copies = [
        pltpu.make_async_copy(img_hbm, img, small_sem.at[0]),
        pltpu.make_async_copy(tra_hbm, tra, small_sem.at[1]),
    ]
    for copy in table_copies + small_copies:
        copy.start()

    def proj_copy(p):
        return pltpu.make_async_copy(proj_hbm.at[p], proj.at[p], proj_sem.at[p])

    for p in range(n_part):
        proj_copy(p).start()

    for copy in table_copies:
        copy.wait()
    lane = lax.broadcasted_iota(jnp.int32, (n_pose, n_table), 1)
    chosen = jnp.concatenate(
        [(pose[:, p : p + 1] == lane).astype(jnp.float32) for p in range(n_part)], axis=0
    ).astype(jnp.bfloat16)

    def look_up(table):
        return lax.dot_general(
            chosen, table[...].astype(jnp.float32).astype(jnp.bfloat16),
            (((1,), (1,)), ((), ())), preferred_element_type=jnp.float32,
        )

    idx_v[:, :n_tile] = ((look_up(blocks) * bank_size + look_up(tiles)) * SUB).astype(jnp.int32)
    idx_copy = pltpu.make_async_copy(idx_v, idx_s, idx_sem)
    idx_copy.start()

    zero = jnp.zeros((8 * SUB, LANES), jnp.float32)

    @pl.loop(0, n_row // (8 * SUB))
    def _(i):
        rows = pl.ds(pl.multiple_of(i * (8 * SUB), 8 * SUB), 8 * SUB)
        for acc in accs:
            acc[rows, :] = zero

    to = lax.broadcasted_iota(jnp.int32, (group, group), 0)
    fro = lax.broadcasted_iota(jnp.int32, (group, group), 1)
    swapped = (fro // 64) * 64 + (fro % 8) * 8 + (fro // 8) % 8
    swap = (to == swapped).astype(jnp.float32).astype(jnp.bfloat16)

    def regroup(left, right):
        both = jnp.concatenate([left, right], axis=1)
        return jnp.dot(swap, both, preferred_element_type=jnp.float32)

    for copy in small_copies:
        copy.wait()

    @pl.loop(0, tra.shape[0] // group)
    def _(i):
        rows = pl.ds(pl.multiple_of(i * group, group), group)
        both = regroup(tra[rows, :], img[rows, :])
        t = both[:, :LANES]
        square[rows, :] = t * t
        cross[rows, :] = t * both[:, LANES:]

    idx_copy.wait()

    @pl.loop(0, n_part // 2)
    def _(q):
        proj_copy(2 * q).wait()
        proj_copy(2 * q + 1).wait()
        weights = [
            [jnp.full((SUB, LANES), w_smem[k, 2 * q + h], jnp.float32) for k in range(n_pose)]
            for h in range(2)
        ]

        @pl.loop(0, n_tile // 4)
        def _(i):
            rows = pl.ds(pl.multiple_of(i * group, group), group)
            x = regroup(proj[2 * q, rows, :], proj[2 * q + 1, rows, :])
            for u in range(4):
                j = i * 4 + u
                for h in range(2):
                    p = 2 * q + h
                    cell = pl.ds(pl.multiple_of((j * n_part + p) * SUB, SUB), SUB)
                    tt = square[cell, :]
                    ti = cross[cell, :]

                    def term(k):
                        first = (u * n_pose + k) * SUB
                        value = x[first : first + SUB, h * LANES : (h + 1) * LANES]
                        return (tt * value - ti) * weights[h][k]

                    for k in range(N_ACC):
                        acc = accs[k]
                        at = idx_s[p * n_pose + k, j]
                        at2 = idx_s[p * n_pose + k + N_ACC, j]
                        here = pl.ds(pl.multiple_of(at, SUB), SUB)
                        here2 = pl.ds(pl.multiple_of(at2, SUB), SUB)
                        same = jnp.where(at == at2, 1.0, 0.0)
                        one, two = term(k), term(k + N_ACC)
                        old, old2 = acc[here, :], acc[here2, :]
                        acc[here, :] = old + one
                        acc[here2, :] = old2 + (two + same * one)

    rep = rep_smem[0]
    piece = n_row // (n_owner * 2 * n_chunk)
    step = 4 * SUB

    for c in range(n_chunk):
        for side in range(2):
            out = outs[2 * c + side]
            half = rep if side else 1 - rep

            def out_copy(o, first):
                return pltpu.make_async_copy(
                    accs[0].at[pl.ds(first, piece), :], out.at[o], out_sem.at[(2 * c + side) * n_owner + o]
                )

            @pl.loop(0, n_owner)
            def _(o):
                first = pl.multiple_of(((o * 2 + half) * n_chunk + c) * piece, piece)

                @pl.loop(0, piece // step)
                def _(h):
                    rows = pl.ds(pl.multiple_of(first + h * step, step), step)
                    total = accs[0][rows, :]
                    for acc in accs[1:]:
                        total += acc[rows, :]
                    accs[0][rows, :] = total

                out_copy(o, first).start()

    for c in range(n_chunk):
        for side in range(2):

            @pl.loop(0, n_owner)
            def _(o):
                pltpu.make_async_copy(
                    accs[0].at[pl.ds(0, piece), :],
                    outs[2 * c + side].at[o],
                    out_sem.at[(2 * c + side) * n_owner + o],
                ).wait()


def tiles_in_order(array):
    lead = array.shape[:-2]
    rows, cells = array.shape[-2:]
    array = array.reshape(lead + (rows // SUB, SUB, cells // LANES, LANES))
    return jnp.swapaxes(array, -3, -2)


def accumulate(
    projections, images, transfer, pose_weights, pose_of, pose_blocks, pose_tiles,
    bank_size, n_owner, n_chunk, rep,
):
    n_part, n_pose, n_tile, n_cell = projections.shape
    assert n_cell == SUB * LANES and n_pose == SUB and n_pose == 2 * N_ACC
    n_row = n_owner * NB_DEV * bank_size * SUB
    n_idx = n_part * n_pose
    piece = n_row // (n_owner * 2 * n_chunk)
    projections = tiles_in_order(jnp.transpose(projections, (0, 2, 1, 3)))
    projections = projections.reshape(n_part, n_tile * n_pose * SUB, LANES)
    images = tiles_in_order(jnp.transpose(images, (1, 0, 2))).reshape(n_tile * n_part * SUB, LANES)
    transfer = tiles_in_order(jnp.transpose(transfer, (1, 0, 2))).reshape(n_tile * n_part * SUB, LANES)
    anywhere = pl.BlockSpec(memory_space=pl.ANY)
    smem = pl.BlockSpec(memory_space=pltpu.SMEM)
    return pl.pallas_call(
        functools.partial(accumulate_kernel, bank_size, n_owner, n_chunk),
        out_shape=[jax.ShapeDtypeStruct((n_owner, piece, LANES), jnp.float32)] * (2 * n_chunk),
        in_specs=[smem] + [anywhere] * 3 + [smem] + [anywhere] * 3,
        out_specs=[anywhere] * (2 * n_chunk),
        scratch_shapes=[
            pltpu.VMEM(projections.shape, jnp.bfloat16),
            pltpu.VMEM(images.shape, jnp.bfloat16),
            pltpu.VMEM(transfer.shape, jnp.bfloat16),
            pltpu.VMEM((n_pose, n_part), jnp.int32),
            pltpu.VMEM(pose_blocks.shape[::-1], jnp.int32),
            pltpu.VMEM(pose_tiles.shape[::-1], jnp.int32),
            pltpu.VMEM((n_idx, LANES), jnp.int32),
            pltpu.SMEM((n_idx, LANES), jnp.int32),
            pltpu.VMEM(transfer.shape, jnp.float32),
            pltpu.VMEM(transfer.shape, jnp.float32),
        ]
        + [pltpu.VMEM((n_row, LANES), jnp.float32)] * N_ACC
        + [
            pltpu.SemaphoreType.DMA((n_part,)),
            pltpu.SemaphoreType.DMA((2,)),
            pltpu.SemaphoreType.DMA((3,)),
            pltpu.SemaphoreType.DMA,
            pltpu.SemaphoreType.DMA((2 * n_chunk * n_owner,)),
        ],
        compiler_params=pltpu.CompilerParams(vmem_limit_bytes=60 * MIB),
        name="accumulate",
    )(rep, projections, images, transfer, pose_weights.T, pose_of.T, pose_blocks.T, pose_tiles.T)


def bank_kernel(sums, bank, out):
    bank_size, n_z, n_cell = bank.shape
    n_blk = out.shape[0]
    group = 2 * SUB

    for c in range(n_cell // LANES):
        cols = slice(c * LANES, (c + 1) * LANES)

        @pl.loop(0, n_z // group)
        def _(g):
            rows = pl.ds(pl.multiple_of(g * group, group), group)
            weights = [bank[t, rows, cols] for t in range(bank_size)]
            for b in range(n_blk):
                total = weights[0] * sums[b * bank_size, c : c + 1, :]
                for t in range(1, bank_size):
                    total += weights[t] * sums[b * bank_size + t, c : c + 1, :]
                out[b, rows, cols] = total


def apply_bank(sums, weight_bank, n_blk):
    bank_size, n_z, n_cell = weight_bank.shape
    vmem = pl.BlockSpec(memory_space=pltpu.VMEM)
    return pl.pallas_call(
        bank_kernel,
        out_shape=jax.ShapeDtypeStruct((n_blk, n_z, n_cell), jnp.float32),
        in_specs=[vmem, vmem],
        out_specs=vmem,
        compiler_params=pltpu.CompilerParams(vmem_limit_bytes=32 * MIB),
        name="apply_bank",
    )(sums, weight_bank)


def body(
    projections, images, transfer, pose_weights, pose_of, pose_blocks, pose_tiles, weight_bank
):
    bank_size = weight_bank.shape[0]
    n_blk = lax.axis_size("blk")
    n_far = n_blk // 2
    here = lax.axis_index("blk")
    far, near = here // 2, here % 2
    rep = lax.axis_index("rep").astype(jnp.int32).reshape(1)
    outs = accumulate(
        projections, images, transfer, pose_weights, pose_of, pose_blocks, pose_tiles,
        bank_size, n_blk, N_CHUNK, rep,
    )
    swap_rep = [(0, 1), (1, 0)]
    swap_near = [(i, i ^ 1) for i in range(n_blk)]

    def pick(array, index, axis):
        return lax.dynamic_index_in_dim(array, index, axis, keepdims=False)

    owned = []
    for c in range(N_CHUNK):
        sent, kept = outs[2 * c], outs[2 * c + 1]
        got = lax.ppermute(sent, "rep", swap_rep)
        shape = (n_far, 2) + sent.shape[1:]
        got, kept = got.reshape(shape), kept.reshape(shape)
        away = pick(kept, 1 - near, 1) + pick(got, 1 - near, 1)
        stay = pick(kept, near, 1) + pick(got, near, 1)
        stay = stay + lax.ppermute(away, "blk", swap_near)
        total = pick(stay, far, 0)
        for d in range(1, n_far):
            pairs = [(i, i ^ (2 * d)) for i in range(n_blk)]
            total = total + lax.ppermute(pick(stay, far ^ d, 0), "blk", pairs)
        owned.append(total)
    owned = jnp.concatenate(owned, axis=0)
    owned = lax.all_gather(owned, "rep", axis=0, tiled=True)
    owned = owned.reshape(NB_DEV * bank_size, SUB, LANES)
    return apply_bank(owned, weight_bank, NB_DEV)


def solution(mesh):
    placed = (
        P(("groups", "blk", "rep"), None, None, None),
        P(("groups", "blk", "rep"), None, None),
        P(("groups", "blk", "rep"), None, None),
        P(("groups", "blk", "rep"), None),
        P(("groups", "blk", "rep"), None),
        P("groups", None),
        P("groups", None),
        P(),
    )
    return jax.shard_map(
        body,
        mesh=mesh,
        in_specs=placed,
        out_specs=P(("groups", "blk"), None, None),
        check_vma=False,
    )
```

```python
import functools

import jax
import jax.numpy as jnp
from jax import lax
from jax.experimental import pallas as pl
from jax.experimental.pallas import tpu as pltpu
from jax.sharding import PartitionSpec as P

NB_DEV = 8
LANES = 128
SUB = 8
MIB = 1 << 20
N_ACC = 4
UNROLL = 4
STRIDE = 9
PARTS = ((1, True), (2, False), (1, False))


def accumulate_kernel(
    bank_size, n_owner, sizes,
    rep_smem, proj_hbm, img_hbm, tra_hbm, w_smem, pose_hbm, blocks_hbm, tiles_hbm,
    *rest,
):
    n_chunk = len(sizes)
    outs, rest = rest[: 2 * n_chunk], rest[2 * n_chunk :]
    proj, img, tra, pose, blocks, tiles, idx_v, idx_s, square, cross = rest[:10]
    parts, rest = rest[10 : 10 + UNROLL], rest[10 + UNROLL :]
    accs = rest[:N_ACC]
    proj_sem, small_sem, table_sem, idx_sem, out_sem = rest[N_ACC:]
    n_pose, n_part = pose.shape
    n_tile, n_table = blocks.shape
    n_row = accs[0].shape[0]

    table_copies = [
        pltpu.make_async_copy(src, dst, table_sem.at[i])
        for i, (src, dst) in enumerate(((pose_hbm, pose), (blocks_hbm, blocks), (tiles_hbm, tiles)))
    ]
    small_copies = [
        pltpu.make_async_copy(img_hbm, img, small_sem.at[0]),
        pltpu.make_async_copy(tra_hbm, tra, small_sem.at[1]),
    ]
    for copy in table_copies + small_copies:
        copy.start()

    def proj_copy(p):
        return pltpu.make_async_copy(proj_hbm.at[p], proj.at[p], proj_sem.at[p])

    for p in range(n_part):
        proj_copy(p).start()

    for copy in table_copies:
        copy.wait()
    lane = lax.broadcasted_iota(jnp.int32, (n_pose, n_table), 1)
    chosen = jnp.concatenate(
        [(pose[:, p : p + 1] == lane).astype(jnp.float32) for p in range(n_part)], axis=0
    ).astype(jnp.bfloat16)

    def look_up(table):
        return lax.dot_general(
            chosen, table[...].astype(jnp.float32).astype(jnp.bfloat16),
            (((1,), (1,)), ((), ())), preferred_element_type=jnp.float32,
        )

    idx_v[:, :n_tile] = ((look_up(blocks) * bank_size + look_up(tiles)) * SUB).astype(jnp.int32)
    idx_copy = pltpu.make_async_copy(idx_v, idx_s, idx_sem)
    idx_copy.start()

    zero = jnp.zeros((8 * SUB, LANES), jnp.float32)

    @pl.loop(0, n_row // (8 * SUB))
    def _(i):
        rows = pl.ds(pl.multiple_of(i * (8 * SUB), 8 * SUB), 8 * SUB)
        for acc in accs:
            acc[rows, :] = zero

    for copy in small_copies:
        copy.wait()

    def stage_in(part, tiles_of, first):
        for c in range(0, SUB, 2):
            pair = tiles_of[pl.ds(pl.multiple_of(first + c * SUB, 2 * SUB), 2 * SUB), :].astype(jnp.float32)
            part[c * STRIDE : c * STRIDE + SUB, :] = pair[:SUB]
            part[(c + 1) * STRIDE : (c + 1) * STRIDE + SUB, :] = pair[SUB:]

    def row_of(part, k):
        return part[pl.ds(k, SUB, stride=STRIDE), :]

    @pl.loop(0, tra.shape[0] // (2 * SUB * SUB))
    def _(i):
        for u in range(2):
            first = (i * 2 + u) * (SUB * SUB)
            stage_in(parts[2 * u], tra, first)
            stage_in(parts[2 * u + 1], img, first)
            for k in range(SUB):
                rows = pl.ds(pl.multiple_of(first + k * SUB, SUB), SUB)
                t = row_of(parts[2 * u], k)
                square[rows, :] = t * t
                cross[rows, :] = t * row_of(parts[2 * u + 1], k)

    idx_copy.wait()

    @pl.loop(0, n_part)
    def _(p):
        proj_copy(p).wait()
        weights = [jnp.full((SUB, LANES), w_smem[k, p], jnp.float32) for k in range(n_pose)]

        @pl.loop(0, n_tile // UNROLL)
        def _(i):
            for u, part in enumerate(parts):
                j = i * UNROLL + u
                stage_in(part, proj.at[p], j * (SUB * SUB))
                cell = pl.ds(pl.multiple_of((j * n_part + p) * SUB, SUB), SUB)
                tt = square[cell, :]
                ti = cross[cell, :]
                for k in range(N_ACC):
                    acc = accs[k]
                    at = idx_s[p * n_pose + k, j]
                    at2 = idx_s[p * n_pose + k + N_ACC, j]
                    here = pl.ds(pl.multiple_of(at, SUB), SUB)
                    here2 = pl.ds(pl.multiple_of(at2, SUB), SUB)
                    same = jnp.where(at == at2, 1.0, 0.0)
                    one = (tt * row_of(part, k) - ti) * weights[k]
                    two = (tt * row_of(part, k + N_ACC) - ti) * weights[k + N_ACC]
                    old, old2 = acc[here, :], acc[here2, :]
                    acc[here, :] = old + one
                    acc[here2, :] = old2 + (two + same * one)

    rep = rep_smem[0]
    step = 4 * SUB
    half_rows = n_row // (n_owner * 2)
    begins = [sum(sizes[:c]) for c in range(n_chunk)]

    for c in range(n_chunk):
        for side in range(2):
            half = rep if side else 1 - rep

            def out_copy(o, first):
                return pltpu.make_async_copy(
                    accs[0].at[pl.ds(first, sizes[c]), :], outs[2 * c + side].at[o],
                    out_sem.at[(2 * c + side) * n_owner + o],
                )

            @pl.loop(0, n_owner)
            def _(o):
                first = pl.multiple_of((o * 2 + half) * half_rows + begins[c], step)

                @pl.loop(0, sizes[c] // step)
                def _(h):
                    rows = pl.ds(pl.multiple_of(first + h * step, step), step)
                    total = accs[0][rows, :]
                    for acc in accs[1:]:
                        total += acc[rows, :]
                    accs[0][rows, :] = total

                out_copy(o, first).start()

    for c in range(n_chunk):
        for side in range(2):

            @pl.loop(0, n_owner)
            def _(o):
                pltpu.make_async_copy(
                    accs[0].at[pl.ds(0, sizes[c]), :], outs[2 * c + side].at[o],
                    out_sem.at[(2 * c + side) * n_owner + o],
                ).wait()


def tiles_in_order(array):
    lead = array.shape[:-2]
    rows, cells = array.shape[-2:]
    array = array.reshape(lead + (rows // SUB, SUB, cells // LANES, LANES))
    return jnp.swapaxes(array, -3, -2)


def accumulate(
    projections, images, transfer, pose_weights, pose_of, pose_blocks, pose_tiles,
    bank_size, n_owner, rep,
):
    n_part, n_pose, n_tile, n_cell = projections.shape
    assert n_cell == SUB * LANES and n_pose == SUB and n_pose == 2 * N_ACC
    n_row = n_owner * NB_DEV * bank_size * SUB
    n_idx = n_part * n_pose
    sizes = [size * bank_size * SUB for size, _ in PARTS]
    n_chunk = len(sizes)
    projections = tiles_in_order(jnp.transpose(projections, (0, 2, 1, 3)))
    projections = projections.reshape(n_part, n_tile * n_pose * SUB, LANES)
    images = tiles_in_order(jnp.transpose(images, (1, 0, 2))).reshape(n_tile * n_part * SUB, LANES)
    transfer = tiles_in_order(jnp.transpose(transfer, (1, 0, 2))).reshape(n_tile * n_part * SUB, LANES)
    anywhere = pl.BlockSpec(memory_space=pl.ANY)
    smem = pl.BlockSpec(memory_space=pltpu.SMEM)
    return pl.pallas_call(
        functools.partial(accumulate_kernel, bank_size, n_owner, sizes),
        out_shape=[
            jax.ShapeDtypeStruct((n_owner, size, LANES), jnp.float32) for size in sizes for _ in range(2)
        ],
        in_specs=[smem] + [anywhere] * 3 + [smem] + [anywhere] * 3,
        out_specs=[anywhere] * (2 * n_chunk),
        scratch_shapes=[
            pltpu.VMEM(projections.shape, jnp.bfloat16),
            pltpu.VMEM(images.shape, jnp.bfloat16),
            pltpu.VMEM(transfer.shape, jnp.bfloat16),
            pltpu.VMEM((n_pose, n_part), jnp.int32),
            pltpu.VMEM(pose_blocks.shape[::-1], jnp.int32),
            pltpu.VMEM(pose_tiles.shape[::-1], jnp.int32),
            pltpu.VMEM((n_idx, LANES), jnp.int32),
            pltpu.SMEM((n_idx, LANES), jnp.int32),
            pltpu.VMEM(transfer.shape, jnp.float32),
            pltpu.VMEM(transfer.shape, jnp.float32),
        ]
        + [pltpu.VMEM((SUB * STRIDE, LANES), jnp.float32)] * UNROLL
        + [pltpu.VMEM((n_row, LANES), jnp.float32)] * N_ACC
        + [
            pltpu.SemaphoreType.DMA((n_part,)),
            pltpu.SemaphoreType.DMA((2,)),
            pltpu.SemaphoreType.DMA((3,)),
            pltpu.SemaphoreType.DMA,
            pltpu.SemaphoreType.DMA((2 * n_chunk * n_owner,)),
        ],
        compiler_params=pltpu.CompilerParams(vmem_limit_bytes=60 * MIB),
        name="accumulate",
    )(rep, projections, images, transfer, pose_weights.T, pose_of.T, pose_blocks.T, pose_tiles.T)


def bank_kernel(sums, bank, out):
    bank_size, n_z, n_cell = bank.shape
    n_blk = out.shape[0]
    group = 2 * SUB

    for c in range(n_cell // LANES):
        cols = slice(c * LANES, (c + 1) * LANES)

        @pl.loop(0, n_z // group)
        def _(g):
            rows = pl.ds(pl.multiple_of(g * group, group), group)
            weights = [bank[t, rows, cols] for t in range(bank_size)]
            for b in range(n_blk):
                total = weights[0] * sums[b * bank_size, c : c + 1, :]
                for t in range(1, bank_size):
                    total += weights[t] * sums[b * bank_size + t, c : c + 1, :]
                out[b, rows, cols] = total


def apply_bank(sums, weight_bank, n_blk):
    bank_size, n_z, n_cell = weight_bank.shape
    vmem = pl.BlockSpec(memory_space=pltpu.VMEM)
    return pl.pallas_call(
        bank_kernel,
        out_shape=jax.ShapeDtypeStruct((n_blk, n_z, n_cell), jnp.float32),
        in_specs=[vmem, vmem],
        out_specs=vmem,
        compiler_params=pltpu.CompilerParams(vmem_limit_bytes=32 * MIB),
        name="apply_bank",
    )(sums, weight_bank)


def body(
    projections, images, transfer, pose_weights, pose_of, pose_blocks, pose_tiles, weight_bank
):
    bank_size = weight_bank.shape[0]
    n_blk = lax.axis_size("blk")
    n_far = n_blk // 2
    here = lax.axis_index("blk")
    far, near = here // 2, here % 2
    rep = lax.axis_index("rep").astype(jnp.int32).reshape(1)
    outs = accumulate(
        projections, images, transfer, pose_weights, pose_of, pose_blocks, pose_tiles,
        bank_size, n_blk, rep,
    )
    swap_rep = [(0, 1), (1, 0)]
    swap_near = [(i, i ^ 1) for i in range(n_blk)]

    def pick(array, index, axis):
        return lax.dynamic_index_in_dim(array, index, axis, keepdims=False)

    def sum_near(array, got, axis):
        away = pick(array, 1 - near, axis)
        stay = pick(array, near, axis)
        if got is not None:
            away, stay = away + pick(got, 1 - near, axis), stay + pick(got, near, axis)
        return stay + lax.ppermute(away, "blk", swap_near)

    def sum_far(array):
        total = pick(array, far, 0)
        for d in range(1, n_far):
            pairs = [(i, i ^ (2 * d)) for i in range(n_blk)]
            total = total + lax.ppermute(pick(array, far ^ d, 0), "blk", pairs)
        return total

    owned = []
    for c, (_, far_first) in enumerate(PARTS):
        sent, kept = outs[2 * c], outs[2 * c + 1]
        got = lax.ppermute(sent, "rep", swap_rep)
        shape = (n_far, 2) + sent.shape[1:]
        got, kept = got.reshape(shape), kept.reshape(shape)
        if far_first:
            owned.append(sum_near(sum_far(kept + got), None, 0))
        else:
            owned.append(sum_far(sum_near(kept, got, 1)))
    owned = jnp.concatenate(owned, axis=0)
    owned = lax.all_gather(owned, "rep", axis=0, tiled=True)
    owned = owned.reshape(NB_DEV * bank_size, SUB, LANES)
    return apply_bank(owned, weight_bank, NB_DEV)


def solution(mesh):
    placed = (
        P(("groups", "blk", "rep"), None, None, None),
        P(("groups", "blk", "rep"), None, None),
        P(("groups", "blk", "rep"), None, None),
        P(("groups", "blk", "rep"), None),
        P(("groups", "blk", "rep"), None),
        P("groups", None),
        P("groups", None),
        P(),
    )
    return jax.shard_map(
        body,
        mesh=mesh,
        in_specs=placed,
        out_specs=P(("groups", "blk"), None, None),
        check_vma=False,
    )
```

```python
import functools

import jax
import jax.numpy as jnp
from jax import lax
from jax.experimental import pallas as pl
from jax.experimental.pallas import tpu as pltpu
from jax.sharding import PartitionSpec as P

NB_DEV = 8
LANES = 128
SUB = 8
MIB = 1 << 20
FAR_FIRST = 21


def accumulate_kernel(
    bank_size, n_owner, n_acc,
    place, proj_hbm, img_hbm, tra_hbm, w_hbm, pose_hbm, blocks_hbm, tiles_hbm,
    sent_away, kept_away, sent_b, kept_b, sent_stay, kept_stay,
    proj, img, tra, w_smem, pose, blocks, tiles, idx_v, idx_s, square, cross,
    *rest,
):
    accs = rest[:n_acc]
    proj_sem, small_sem, table_sem, idx_sem = rest[n_acc:]
    n_pose, n_part = pose.shape
    n_tile, n_table = blocks.shape
    n_row = accs[0].shape[0]
    tile_rows = SUB * SUB
    part_rows = n_tile * tile_rows

    table_copies = [
        pltpu.make_async_copy(src, dst, table_sem.at[i])
        for i, (src, dst) in enumerate(((pose_hbm, pose), (blocks_hbm, blocks), (tiles_hbm, tiles)))
    ]
    small_copies = [
        pltpu.make_async_copy(img_hbm, img, small_sem.at[0]),
        pltpu.make_async_copy(tra_hbm, tra, small_sem.at[1]),
        pltpu.make_async_copy(w_hbm, w_smem, small_sem.at[2]),
    ]
    for copy in table_copies + small_copies:
        copy.start()

    def proj_copy(p):
        rows = pl.ds(pl.multiple_of(p * part_rows, part_rows), part_rows)
        return pltpu.make_async_copy(proj_hbm.at[rows, :], proj.at[rows, :], proj_sem.at[p])

    for p in range(n_part):
        proj_copy(p).start()

    for copy in table_copies:
        copy.wait()
    lane = lax.broadcasted_iota(jnp.int32, (n_pose, n_table), 1)
    chosen = jnp.concatenate(
        [(pose[:, p : p + 1] == lane).astype(jnp.float32) for p in range(n_part)], axis=0
    ).astype(jnp.bfloat16)

    def look_up(table):
        return lax.dot_general(
            chosen, table[...].astype(jnp.float32).astype(jnp.bfloat16),
            (((1,), (1,)), ((), ())), preferred_element_type=jnp.float32,
        )

    idx_v[:, :n_tile] = ((look_up(blocks) * bank_size + look_up(tiles)) * SUB).astype(jnp.int32)
    idx_copy = pltpu.make_async_copy(idx_v, idx_s, idx_sem)
    idx_copy.start()

    zero = jnp.zeros((8 * SUB, LANES), jnp.float32)

    @pl.loop(0, n_row // (8 * SUB))
    def _(i):
        rows = pl.ds(pl.multiple_of(i * (8 * SUB), 8 * SUB), 8 * SUB)
        for acc in accs:
            acc[rows, :] = zero

    def regroup(ref, first):
        block = ref[pl.ds(pl.multiple_of(first, tile_rows), tile_rows), :].astype(jnp.float32)
        return jnp.swapaxes(block.reshape(SUB, SUB, LANES), 0, 1)

    for copy in small_copies:
        copy.wait()

    @pl.loop(0, n_tile)
    def _(j):
        for h in range(n_part // SUB):
            first = (j * (n_part // SUB) + h) * tile_rows
            t, i = regroup(tra, first), regroup(img, first)
            for k in range(SUB):
                rows = pl.ds(pl.multiple_of(((h * SUB + k) * n_tile + j) * SUB, SUB), SUB)
                square[rows, :] = t[k] * t[k]
                cross[rows, :] = t[k] * i[k]

    def terms(unit):
        x = regroup(proj, unit * tile_rows)
        cell = pl.ds(pl.multiple_of(unit * SUB, SUB), SUB)
        tt, ti = square[cell, :], cross[cell, :]
        return [tt * x[k] - ti for k in range(n_pose)]

    def add_rows(p, j, values, weights):
        at = [idx_s[p * n_pose + k, j] for k in range(n_pose)]
        rows = [pl.ds(pl.multiple_of(at[k], SUB), SUB) for k in range(n_pose)]
        values = [values[k] * weights[k] for k in range(n_pose)]
        old = [accs[k % n_acc][rows[k], :] for k in range(n_pose)]
        new = []
        for k in range(n_pose):
            total = old[k] + values[k]
            for m in range(k % n_acc, k, n_acc):
                total += jnp.where(at[m] == at[k], 1.0, 0.0) * values[m]
            new.append(total)
        for k in range(n_pose):
            accs[k % n_acc][rows[k], :] = new[k]

    proj_copy(0).wait()
    idx_copy.wait()
    n_unit = n_part * n_tile

    @pl.loop(0, n_part, init_carry=tuple(terms(0) + terms(1)))
    def _(p, ready):
        @pl.when(p + 1 < n_part)
        def _():
            proj_copy(p + 1).wait()

        weights = [jnp.full((SUB, LANES), w_smem[k, p], jnp.float32) for k in range(n_pose)]

        @pl.loop(0, n_tile, step=2, init_carry=ready)
        def done(j, now):
            unit = jnp.minimum(p * n_tile + j + 2, n_unit - 2)
            later = terms(unit) + terms(unit + 1)
            add_rows(p, j, now[:n_pose], weights)
            add_rows(p, j + 1, now[n_pose:], weights)
            return tuple(later)

        return done

    rep, near = place[0], place[1]
    half_rows = n_row // (n_owner * 2)
    b_rows = sent_b.shape[1]

    def finish(out, o, owner, half, begin):
        size = out.shape[1]
        step = 8 * SUB
        first = (owner * 2 + half) * half_rows + begin

        def sum_rows(offset, count):
            rows = pl.ds(pl.multiple_of(first + offset, SUB), count)
            total = accs[0][rows, :]
            for acc in accs[1:]:
                total += acc[rows, :]
            out[o, pl.ds(pl.multiple_of(offset, SUB), count), :] = total

        @pl.loop(0, size // step)
        def _(i):
            sum_rows(i * step, step)

        if size % step:
            sum_rows(size - size % step, size % step)

    for sent, kept, side in ((sent_away, kept_away, 1 - near), (sent_stay, kept_stay, near)):

        @pl.loop(0, n_owner // 2)
        def _(o):
            finish(sent, o, o * 2 + side, 1 - rep, b_rows)
            finish(kept, o, o * 2 + side, rep, b_rows)

    @pl.loop(0, n_owner)
    def _(o):
        finish(sent_b, o, o, 1 - rep, 0)
        finish(kept_b, o, o, rep, 0)


def tiles_in_order(array):
    lead = array.shape[:-2]
    rows, cells = array.shape[-2:]
    array = array.reshape(lead + (rows // SUB, SUB, cells // LANES, LANES))
    return jnp.swapaxes(array, -3, -2).reshape(-1, LANES)


def accumulate(
    projections, images, transfer, pose_weights, pose_of, pose_blocks, pose_tiles,
    bank_size, n_owner, place,
):
    n_part, n_pose, n_tile, n_cell = projections.shape
    assert n_cell == SUB * LANES and n_pose == SUB and n_part % SUB == 0 and n_tile % 2 == 0
    n_row = n_owner * NB_DEV * bank_size * SUB
    n_acc = 4 if n_row * LANES * 4 <= 4 * MIB else 2
    b_rows = FAR_FIRST * SUB
    a_rows = n_row // (n_owner * 2) - b_rows
    projections = tiles_in_order(jnp.transpose(projections, (0, 2, 1, 3)))
    images = tiles_in_order(jnp.transpose(images, (1, 0, 2)))
    transfer = tiles_in_order(jnp.transpose(transfer, (1, 0, 2)))
    stay = functools.partial(pltpu.with_memory_space_constraint, memory_space=pltpu.HBM)
    hbm = pl.BlockSpec(memory_space=pltpu.HBM)
    smem = pl.BlockSpec(memory_space=pltpu.SMEM)
    vmem = pl.BlockSpec(memory_space=pltpu.VMEM)
    a_out = jax.ShapeDtypeStruct((n_owner // 2, a_rows, LANES), jnp.float32)
    b_out = jax.ShapeDtypeStruct((n_owner, b_rows, LANES), jnp.float32)
    return pl.pallas_call(
        functools.partial(accumulate_kernel, bank_size, n_owner, n_acc),
        out_shape=[a_out, a_out, b_out, b_out, a_out, a_out],
        in_specs=[smem] + [hbm] * 7,
        out_specs=[vmem] * 6,
        scratch_shapes=[
            pltpu.VMEM(projections.shape, jnp.bfloat16),
            pltpu.VMEM(images.shape, jnp.bfloat16),
            pltpu.VMEM(transfer.shape, jnp.bfloat16),
            pltpu.SMEM((n_pose, n_part), jnp.float32),
            pltpu.VMEM((n_pose, n_part), jnp.int32),
            pltpu.VMEM(pose_blocks.shape[::-1], jnp.int32),
            pltpu.VMEM(pose_tiles.shape[::-1], jnp.int32),
            pltpu.VMEM((n_part * n_pose, LANES), jnp.int32),
            pltpu.SMEM((n_part * n_pose, LANES), jnp.int32),
            pltpu.VMEM(transfer.shape, jnp.float32),
            pltpu.VMEM(transfer.shape, jnp.float32),
        ]
        + [pltpu.VMEM((n_row, LANES), jnp.float32)] * n_acc
        + [
            pltpu.SemaphoreType.DMA((n_part,)),
            pltpu.SemaphoreType.DMA((3,)),
            pltpu.SemaphoreType.DMA((3,)),
            pltpu.SemaphoreType.DMA,
        ],
        compiler_params=pltpu.CompilerParams(vmem_limit_bytes=(40 if n_acc == 4 else 56) * MIB),
        name="accumulate",
    )(
        place, stay(projections), stay(images), stay(transfer),
        stay(pose_weights.T), stay(pose_of.T), stay(pose_blocks.T), stay(pose_tiles.T),
    )


def in_vmem(kernel, name, out_shape, place, *operands):
    vmem = pl.BlockSpec(memory_space=pltpu.VMEM)
    return pl.pallas_call(
        kernel,
        out_shape=out_shape,
        in_specs=[pl.BlockSpec(memory_space=pltpu.SMEM)] + [vmem] * len(operands),
        out_specs=jax.tree.map(lambda _: vmem, out_shape),
        compiler_params=pltpu.CompilerParams(vmem_limit_bytes=32 * MIB),
        name=name,
    )(place, *operands)


def first_step_kernel(place, kept_away, got_away, kept_b, got_b, away, own_b, *far_b):
    far = place[2]
    away[...] = kept_away[...] + got_away[...]
    for d, out in enumerate((own_b,) + far_b):
        line = jnp.bitwise_xor(far, d)
        for y in range(2):
            out[y] = kept_b[line * 2 + y] + got_b[line * 2 + y]


def second_step_kernel(n_far, place, kept_stay, got_stay, got_near, own_b, *rest):
    got_b, (own_a, stay_b, away_b, *far_a) = rest[: n_far - 1], rest[n_far - 1 :]
    near, far = place[1], place[2]
    for d, out in enumerate([own_a] + far_a):
        line = jnp.bitwise_xor(far, d)
        out[...] = kept_stay[line] + got_stay[line] + got_near[line]
    for out, y in ((away_b, 1 - near), (stay_b, near)):
        total = own_b[y]
        for got in got_b:
            total += got[y]
        out[...] = total


def last_step_kernel(n_far, place, own_a, stay_b, got_b, *rest):
    got_a, (all_a, all_b) = rest[: n_far - 1], rest[n_far - 1 :]
    total = own_a[...]
    for got in got_a:
        total += got[...]
    all_a[...] = total
    all_b[...] = stay_b[...] + got_b[...]


def bank_kernel(mine, place, rows_b, rows_a, bank, *rest):
    out_hbm, block, sem = rest[-3:]
    bank_size, n_z, n_cell = bank.shape
    n_blk = block.shape[0]
    group = 2 * SUB
    half = place[0] if mine else 1 - place[0]

    def tile_row(row, c):
        if row < FAR_FIRST:
            return rows_b[row * SUB + c : row * SUB + c + 1, :]
        row -= FAR_FIRST
        return rows_a[row * SUB + c : row * SUB + c + 1, :]

    for c in range(n_cell // LANES):
        cols = slice(c * LANES, (c + 1) * LANES)

        @pl.loop(0, n_z // group)
        def _(g):
            rows = pl.ds(pl.multiple_of(g * group, group), group)
            weights = [bank[t, rows, cols] for t in range(bank_size)]
            for b in range(n_blk):
                total = weights[0] * tile_row(b * bank_size, c)
                for t in range(1, bank_size):
                    total += weights[t] * tile_row(b * bank_size + t, c)
                block[b, rows, cols] = total

    copy = pltpu.make_async_copy(block, out_hbm.at[pl.ds(half * n_blk, n_blk)], sem)
    copy.start()
    copy.wait()


def apply_bank(place, rows_b, rows_a, weight_bank, filled):
    bank_size, n_z, n_cell = weight_bank.shape
    vmem = pl.BlockSpec(memory_space=pltpu.VMEM)
    anywhere = pl.BlockSpec(memory_space=pl.ANY)
    mine = filled is None
    operands = (place, rows_b, rows_a, weight_bank) + (() if mine else (filled,))
    return pl.pallas_call(
        functools.partial(bank_kernel, mine),
        out_shape=jax.ShapeDtypeStruct((NB_DEV, n_z, n_cell), jnp.float32),
        in_specs=[pl.BlockSpec(memory_space=pltpu.SMEM), vmem, vmem, vmem] + ([] if mine else [anywhere]),
        out_specs=anywhere,
        scratch_shapes=[
            pltpu.VMEM((NB_DEV // 2, n_z, n_cell), jnp.float32),
            pltpu.SemaphoreType.DMA,
        ],
        input_output_aliases={} if mine else {4: 0},
        compiler_params=pltpu.CompilerParams(vmem_limit_bytes=32 * MIB),
        name="bank_of_own_half" if mine else "bank_of_other_half",
    )(*operands)


def body(
    projections, images, transfer, pose_weights, pose_of, pose_blocks, pose_tiles, weight_bank
):
    bank_size = weight_bank.shape[0]
    n_blk = lax.axis_size("blk")
    n_far = n_blk // 2
    here = lax.axis_index("blk")
    place = jnp.stack([lax.axis_index("rep"), here & 1, here >> 1]).astype(jnp.int32)
    sent_away, kept_away, sent_b, kept_b, sent_stay, kept_stay = accumulate(
        projections, images, transfer, pose_weights, pose_of, pose_blocks, pose_tiles,
        bank_size, n_blk, place,
    )

    def over_rep(array):
        return lax.ppermute(array, "rep", [(0, 1), (1, 0)])

    def over_near(array):
        return lax.ppermute(array, "blk", [(i, i ^ 1) for i in range(n_blk)])

    def over_far(array, d):
        return lax.ppermute(array, "blk", [(i, i ^ (2 * d)) for i in range(n_blk)])

    def like(*shape):
        return jax.ShapeDtypeStruct(shape, jnp.float32)

    a_rows, b_rows = sent_away.shape[1], sent_b.shape[1]
    got_away, got_b, got_stay = over_rep(sent_away), over_rep(sent_b), over_rep(sent_stay)
    away, own_b, *far_b = in_vmem(
        first_step_kernel, "first_step",
        [like(n_far, a_rows, LANES)] + [like(2, b_rows, LANES)] * n_far,
        place, kept_away, got_away, kept_b, got_b,
    )
    got_near = over_near(away)
    got_far_b = [over_far(array, d + 1) for d, array in enumerate(far_b)]
    own_a, stay_b, away_b, *far_a = in_vmem(
        functools.partial(second_step_kernel, n_far), "second_step",
        [like(a_rows, LANES)] + [like(b_rows, LANES)] * 2 + [like(a_rows, LANES)] * (n_far - 1),
        place, kept_stay, got_stay, got_near, own_b, *got_far_b,
    )
    got_far_a = [over_far(array, d + 1) for d, array in enumerate(far_a)]
    rows_a, rows_b = in_vmem(
        functools.partial(last_step_kernel, n_far), "last_step",
        [like(a_rows, LANES), like(b_rows, LANES)],
        place, own_a, stay_b, over_near(away_b), *got_far_a,
    )
    out = apply_bank(place, rows_b, rows_a, weight_bank, None)
    return apply_bank(place, over_rep(rows_b), over_rep(rows_a), weight_bank, out)


def solution(mesh):
    placed = (
        P(("groups", "blk", "rep"), None, None, None),
        P(("groups", "blk", "rep"), None, None),
        P(("groups", "blk", "rep"), None, None),
        P(("groups", "blk", "rep"), None),
        P(("groups", "blk", "rep"), None),
        P("groups", None),
        P("groups", None),
        P(),
    )
    return jax.shard_map(
        body,
        mesh=mesh,
        in_specs=placed,
        out_specs=P(("groups", "blk"), None, None),
        check_vma=False,
    )
```

```python
import functools

import jax
import jax.numpy as jnp
from jax import lax
from jax.experimental import pallas as pl
from jax.experimental.pallas import tpu as pltpu
from jax.sharding import PartitionSpec as P

NB_DEV = 8
LANES = 128
SUB = 8
MIB = 1 << 20
FAR_FIRST = 21


def accumulate_kernel(
    bank_size, n_owner, n_acc,
    place, proj_hbm, img_hbm, tra_hbm, w_hbm, pose_hbm, blocks_hbm, tiles_hbm,
    sent_away, kept_away, sent_b, kept_b, sent_stay, kept_stay,
    proj, img, tra, weight, spread, pose, blocks, tiles, idx_v, idx_s, square, cross,
    *rest,
):
    accs = rest[:n_acc]
    proj_sem, small_sem, table_sem, idx_sem = rest[n_acc:]
    n_pose, n_part = pose.shape
    n_tile, n_table = blocks.shape
    n_row = accs[0].shape[0]
    tile_rows = SUB * SUB
    part_rows = n_tile * tile_rows

    table_copies = [
        pltpu.make_async_copy(src, dst, table_sem.at[i])
        for i, (src, dst) in enumerate(((pose_hbm, pose), (blocks_hbm, blocks), (tiles_hbm, tiles)))
    ]
    small_copies = [
        pltpu.make_async_copy(img_hbm, img, small_sem.at[0]),
        pltpu.make_async_copy(tra_hbm, tra, small_sem.at[1]),
        pltpu.make_async_copy(w_hbm, weight, small_sem.at[2]),
    ]
    for copy in table_copies + small_copies:
        copy.start()

    def proj_copy(p):
        rows = pl.ds(pl.multiple_of(p * part_rows, part_rows), part_rows)
        return pltpu.make_async_copy(proj_hbm.at[rows, :], proj.at[rows, :], proj_sem.at[p])

    for p in range(n_part):
        proj_copy(p).start()

    zero = jnp.zeros((8 * SUB, LANES), jnp.float32)

    @pl.loop(0, n_row // (8 * SUB))
    def _(i):
        rows = pl.ds(pl.multiple_of(i * (8 * SUB), 8 * SUB), 8 * SUB)
        for acc in accs:
            acc[rows, :] = zero

    for copy in table_copies:
        copy.wait()
    lane = lax.broadcasted_iota(jnp.int32, (n_pose, n_table), 1)
    chosen = jnp.concatenate(
        [(pose[:, p : p + 1] == lane).astype(jnp.float32) for p in range(n_part)], axis=0
    ).astype(jnp.bfloat16)

    def look_up(table):
        return lax.dot_general(
            chosen, table[...].astype(jnp.float32).astype(jnp.bfloat16),
            (((1,), (1,)), ((), ())), preferred_element_type=jnp.float32,
        )

    idx_v[:, :n_tile] = ((look_up(blocks) * bank_size + look_up(tiles)) * SUB).astype(jnp.int32)
    idx_copy = pltpu.make_async_copy(idx_v, idx_s, idx_sem)
    idx_copy.start()

    for copy in small_copies:
        copy.wait()
    for p in range(n_part):
        spread[p * n_pose : (p + 1) * n_pose, :] = jnp.broadcast_to(weight[:, p : p + 1], (n_pose, LANES))

    @pl.loop(0, square.shape[0] // tile_rows)
    def _(i):
        rows = pl.ds(pl.multiple_of(i * tile_rows, tile_rows), tile_rows)
        t = tra[rows, :].astype(jnp.float32)
        square[rows, :] = t * t
        cross[rows, :] = t * img[rows, :].astype(jnp.float32)

    sublane = lax.broadcasted_iota(jnp.int32, (SUB, LANES), 0)
    bits = [(sublane & (1 << t)) != 0 for t in range(3)]

    def terms(p, j, unit, weights):
        first = pl.multiple_of(unit * tile_rows, tile_rows)
        cell = (j * (n_part // SUB) + p // SUB) * tile_rows + p % SUB
        turned = []
        for c in range(0, SUB, 2):
            pair = proj[pl.ds(first + c * SUB, 2 * SUB), :].astype(jnp.float32)
            for h in range(2):
                x = pair[h * SUB : (h + 1) * SUB]
                row = pl.ds(cell + (c + h) * SUB, 1)
                value = (square[row, :] * x - cross[row, :]) * weights
                turned.append(pltpu.roll(value, c + h, 0) if c + h else value)
        for t, bit in enumerate(bits):
            turned = [jnp.where(bit, turned[(i + (1 << t)) % SUB], turned[i]) for i in range(SUB)]
        result = []
        for k in range(n_pose):
            back = (k % n_acc - k) % SUB
            value = turned[-k % SUB]
            result.append(pltpu.roll(value, back, 0) if back else value)
        return result

    def add_rows(p, j, values):
        at = [idx_s[p * n_pose + k, j] for k in range(n_pose)]
        rows = [pl.ds(pl.multiple_of(at[k], SUB), SUB) for k in range(n_pose)]
        old = [accs[k % n_acc][rows[k], :] for k in range(n_pose)]
        new = []
        for k in range(n_pose):
            total = old[k] + values[k]
            for m in range(k % n_acc, k, n_acc):
                total += jnp.where(at[m] == at[k], 1.0, 0.0) * values[m]
            new.append(total)
        for k in range(n_pose):
            accs[k % n_acc][rows[k], :] = new[k]

    idx_copy.wait()

    @pl.loop(0, n_part)
    def _(p):
        proj_copy(p).wait()
        weights = spread[pl.ds(pl.multiple_of(p * n_pose, n_pose), n_pose), :]
        base = p * n_tile

        @pl.loop(0, n_tile, step=2, init_carry=tuple(terms(p, 0, base, weights) + terms(p, 1, base + 1, weights)))
        def _(j, now):
            ahead = jnp.minimum(j + 2, n_tile - 2)
            later = terms(p, ahead, base + ahead, weights) + terms(p, ahead + 1, base + ahead + 1, weights)
            add_rows(p, j, now[:n_pose])
            add_rows(p, j + 1, now[n_pose:])
            return tuple(later)

    rep, near = place[0], place[1]
    half_rows = n_row // (n_owner * 2)
    b_rows = sent_b.shape[1]

    def finish(out, o, owner, half, begin):
        size = out.shape[1]
        step = 8 * SUB
        first = (owner * 2 + half) * half_rows + begin

        def sum_rows(offset, count):
            rows = pl.ds(pl.multiple_of(first + offset, SUB), count)
            total = accs[0][rows, :].reshape(count // SUB, SUB, LANES)
            for turn, acc in enumerate(accs[1:]):
                total += pltpu.roll(acc[rows, :].reshape(count // SUB, SUB, LANES), SUB - 1 - turn, 1)
            out[o, pl.ds(pl.multiple_of(offset, SUB), count), :] = total.reshape(count, LANES)

        @pl.loop(0, size // step)
        def _(i):
            sum_rows(i * step, step)

        if size % step:
            sum_rows(size - size % step, size % step)

    for sent, kept, side in ((sent_away, kept_away, 1 - near), (sent_stay, kept_stay, near)):

        @pl.loop(0, n_owner // 2)
        def _(o):
            finish(sent, o, o * 2 + side, 1 - rep, b_rows)
            finish(kept, o, o * 2 + side, rep, b_rows)

    @pl.loop(0, n_owner)
    def _(o):
        finish(sent_b, o, o, 1 - rep, 0)
        finish(kept_b, o, o, rep, 0)


def tiles_in_order(array):
    lead = array.shape[:-2]
    rows, cells = array.shape[-2:]
    array = array.reshape(lead + (rows // SUB, SUB, cells // LANES, LANES))
    return jnp.swapaxes(array, -3, -2).reshape(-1, LANES)


def accumulate(
    projections, images, transfer, pose_weights, pose_of, pose_blocks, pose_tiles,
    bank_size, n_owner, place,
):
    n_part, n_pose, n_tile, n_cell = projections.shape
    assert n_cell == SUB * LANES and n_pose == SUB and n_part % SUB == 0 and n_tile % 2 == 0
    n_row = n_owner * NB_DEV * bank_size * SUB
    n_acc = 4 if n_row * LANES * 4 <= 4 * MIB else 2
    b_rows = FAR_FIRST * SUB
    a_rows = n_row // (n_owner * 2) - b_rows
    projections = tiles_in_order(jnp.transpose(projections, (0, 2, 1, 3)))
    images = tiles_in_order(jnp.transpose(images, (1, 0, 2)))
    transfer = tiles_in_order(jnp.transpose(transfer, (1, 0, 2)))
    stay = functools.partial(pltpu.with_memory_space_constraint, memory_space=pltpu.HBM)
    hbm = pl.BlockSpec(memory_space=pltpu.HBM)
    smem = pl.BlockSpec(memory_space=pltpu.SMEM)
    vmem = pl.BlockSpec(memory_space=pltpu.VMEM)
    a_out = jax.ShapeDtypeStruct((n_owner // 2, a_rows, LANES), jnp.float32)
    b_out = jax.ShapeDtypeStruct((n_owner, b_rows, LANES), jnp.float32)
    return pl.pallas_call(
        functools.partial(accumulate_kernel, bank_size, n_owner, n_acc),
        out_shape=[a_out, a_out, b_out, b_out, a_out, a_out],
        in_specs=[smem] + [hbm] * 7,
        out_specs=[vmem] * 6,
        scratch_shapes=[
            pltpu.VMEM(projections.shape, jnp.bfloat16),
            pltpu.VMEM(images.shape, jnp.bfloat16),
            pltpu.VMEM(transfer.shape, jnp.bfloat16),
            pltpu.VMEM((n_pose, n_part), jnp.float32),
            pltpu.VMEM((n_part * n_pose, LANES), jnp.float32),
            pltpu.VMEM((n_pose, n_part), jnp.int32),
            pltpu.VMEM(pose_blocks.shape[::-1], jnp.int32),
            pltpu.VMEM(pose_tiles.shape[::-1], jnp.int32),
            pltpu.VMEM((n_part * n_pose, LANES), jnp.int32),
            pltpu.SMEM((n_part * n_pose, LANES), jnp.int32),
            pltpu.VMEM(transfer.shape, jnp.float32),
            pltpu.VMEM(transfer.shape, jnp.float32),
        ]
        + [pltpu.VMEM((n_row, LANES), jnp.float32)] * n_acc
        + [
            pltpu.SemaphoreType.DMA((n_part,)),
            pltpu.SemaphoreType.DMA((3,)),
            pltpu.SemaphoreType.DMA((3,)),
            pltpu.SemaphoreType.DMA,
        ],
        compiler_params=pltpu.CompilerParams(vmem_limit_bytes=(40 if n_acc == 4 else 56) * MIB),
        name="accumulate",
    )(
        place, stay(projections), stay(images), stay(transfer),
        stay(pose_weights.T), stay(pose_of.T), stay(pose_blocks.T), stay(pose_tiles.T),
    )


def in_vmem(kernel, name, out_shape, *operands):
    vmem = pl.BlockSpec(memory_space=pltpu.VMEM)
    smem = pl.BlockSpec(memory_space=pltpu.SMEM)
    return pl.pallas_call(
        kernel,
        out_shape=out_shape,
        in_specs=[smem if operand.dtype == jnp.int32 else vmem for operand in operands],
        out_specs=jax.tree.map(lambda _: vmem, out_shape),
        compiler_params=pltpu.CompilerParams(vmem_limit_bytes=32 * MIB),
        name=name,
    )(*operands)


def first_step_kernel(kept_away, got_away, kept_b, got_b, away, both_b):
    away[...] = kept_away[...] + got_away[...]
    both_b[...] = kept_b[...] + got_b[...]


def second_step_kernel(place, kept_stay, got_stay, got_near, got_b, line_a, stay_b, away_b):
    near = place[1]
    line_a[...] = kept_stay[...] + got_stay[...] + got_near[...]
    for out, y in ((away_b, 1 - near), (stay_b, near)):
        total = got_b[y]
        for line in range(1, got_b.shape[0] // 2):
            total += got_b[2 * line + y]
        out[...] = total


def last_step_kernel(got_a, stay_b, got_b, all_a, all_b):
    total = got_a[0]
    for line in range(1, got_a.shape[0]):
        total += got_a[line]
    all_a[...] = total
    all_b[...] = stay_b[...] + got_b[...]


def bank_kernel(mine, place, rows_b, rows_a, bank, *rest):
    out_hbm, block, sem = rest[-3:]
    bank_size, n_z, n_cell = bank.shape
    n_blk = block.shape[0]
    group = 2 * SUB
    half = place[0] if mine else 1 - place[0]

    def tile_row(row, c):
        if row < FAR_FIRST:
            return rows_b[row * SUB + c : row * SUB + c + 1, :]
        row -= FAR_FIRST
        return rows_a[row * SUB + c : row * SUB + c + 1, :]

    for c in range(n_cell // LANES):
        cols = slice(c * LANES, (c + 1) * LANES)

        @pl.loop(0, n_z // group)
        def _(g):
            rows = pl.ds(pl.multiple_of(g * group, group), group)
            weights = [bank[t, rows, cols] for t in range(bank_size)]
            for b in range(n_blk):
                total = weights[0] * tile_row(b * bank_size, c)
                for t in range(1, bank_size):
                    total += weights[t] * tile_row(b * bank_size + t, c)
                block[b, rows, cols] = total

    copy = pltpu.make_async_copy(block, out_hbm.at[pl.ds(half * n_blk, n_blk)], sem)
    copy.start()
    copy.wait()


def apply_bank(place, rows_b, rows_a, weight_bank, filled):
    bank_size, n_z, n_cell = weight_bank.shape
    vmem = pl.BlockSpec(memory_space=pltpu.VMEM)
    anywhere = pl.BlockSpec(memory_space=pl.ANY)
    mine = filled is None
    operands = (place, rows_b, rows_a, weight_bank) + (() if mine else (filled,))
    return pl.pallas_call(
        functools.partial(bank_kernel, mine),
        out_shape=jax.ShapeDtypeStruct((NB_DEV, n_z, n_cell), jnp.float32),
        in_specs=[pl.BlockSpec(memory_space=pltpu.SMEM), vmem, vmem, vmem] + ([] if mine else [anywhere]),
        out_specs=anywhere,
        scratch_shapes=[
            pltpu.VMEM((NB_DEV // 2, n_z, n_cell), jnp.float32),
            pltpu.SemaphoreType.DMA,
        ],
        input_output_aliases={} if mine else {4: 0},
        compiler_params=pltpu.CompilerParams(vmem_limit_bytes=32 * MIB),
        name="bank_of_own_half" if mine else "bank_of_other_half",
    )(*operands)


def body(
    projections, images, transfer, pose_weights, pose_of, pose_blocks, pose_tiles, weight_bank
):
    bank_size = weight_bank.shape[0]
    n_blk = lax.axis_size("blk")
    n_far = n_blk // 2
    here = lax.axis_index("blk")
    place = jnp.stack([lax.axis_index("rep"), here & 1, here >> 1]).astype(jnp.int32)
    sent_away, kept_away, sent_b, kept_b, sent_stay, kept_stay = accumulate(
        projections, images, transfer, pose_weights, pose_of, pose_blocks, pose_tiles,
        bank_size, n_blk, place,
    )

    def over_rep(array):
        return lax.ppermute(array, "rep", [(0, 1), (1, 0)])

    def over_near(array):
        return lax.ppermute(array, "blk", [(i, i ^ 1) for i in range(n_blk)])

    def over_far(array):
        lines = [list(range(i, n_blk, 2)) for i in range(2)]
        return lax.all_to_all(array, "blk", 0, 0, axis_index_groups=lines, tiled=True)

    def like(*shape):
        return jax.ShapeDtypeStruct(shape, jnp.float32)

    a_rows, b_rows = sent_away.shape[1], sent_b.shape[1]
    got_away, got_b, got_stay = over_rep(sent_away), over_rep(sent_b), over_rep(sent_stay)
    away, both_b = in_vmem(
        first_step_kernel, "first_step", [like(n_far, a_rows, LANES), like(n_blk, b_rows, LANES)],
        kept_away, got_away, kept_b, got_b,
    )
    line_a, stay_b, away_b = in_vmem(
        second_step_kernel, "second_step",
        [like(n_far, a_rows, LANES), like(b_rows, LANES), like(b_rows, LANES)],
        place, kept_stay, got_stay, over_near(away), over_far(both_b),
    )
    rows_a, rows_b = in_vmem(
        last_step_kernel, "last_step", [like(a_rows, LANES), like(b_rows, LANES)],
        over_far(line_a), stay_b, over_near(away_b),
    )
    out = apply_bank(place, rows_b, rows_a, weight_bank, None)
    return apply_bank(place, over_rep(rows_b), over_rep(rows_a), weight_bank, out)


def solution(mesh):
    placed = (
        P(("groups", "blk", "rep"), None, None, None),
        P(("groups", "blk", "rep"), None, None),
        P(("groups", "blk", "rep"), None, None),
        P(("groups", "blk", "rep"), None),
        P(("groups", "blk", "rep"), None),
        P("groups", None),
        P("groups", None),
        P(),
    )
    return jax.shard_map(
        body,
        mesh=mesh,
        in_specs=placed,
        out_specs=P(("groups", "blk"), None, None),
        check_vma=False,
    )
```

```python
import functools

import jax
import jax.numpy as jnp
from jax import lax
from jax.experimental import pallas as pl
from jax.experimental.pallas import tpu as pltpu
from jax.sharding import PartitionSpec as P

NB_DEV = 8
LANES = 128
SUB = 8
MIB = 1 << 20
UNROLL = 12


def accumulate_kernel(
    bank_size, n_owner, n_acc,
    place, proj_hbm, img_hbm, tra_hbm, w_hbm, pose_hbm, blocks_hbm, tiles_hbm,
    sent_away, kept_away, sent_stay, kept_stay,
    proj, img, tra, weight, spread, pose, blocks, tiles, idx_v, idx_s, square, cross,
    *rest,
):
    accs = rest[:n_acc]
    proj_sem, small_sem, table_sem, idx_sem = rest[n_acc:]
    n_pose, n_part = pose.shape
    n_tile, n_table = blocks.shape
    n_row = accs[0].shape[0]
    tile_rows = SUB * SUB
    part_rows = n_tile * tile_rows

    table_copies = [
        pltpu.make_async_copy(src, dst, table_sem.at[i])
        for i, (src, dst) in enumerate(((pose_hbm, pose), (blocks_hbm, blocks), (tiles_hbm, tiles)))
    ]
    small_copies = [
        pltpu.make_async_copy(img_hbm, img, small_sem.at[0]),
        pltpu.make_async_copy(tra_hbm, tra, small_sem.at[1]),
        pltpu.make_async_copy(w_hbm, weight, small_sem.at[2]),
    ]
    for copy in table_copies + small_copies:
        copy.start()

    def proj_copy(p):
        rows = pl.ds(pl.multiple_of(p * part_rows, part_rows), part_rows)
        return pltpu.make_async_copy(proj_hbm.at[rows, :], proj.at[rows, :], proj_sem.at[p])

    for p in range(n_part):
        proj_copy(p).start()

    zero = jnp.zeros((8 * SUB, LANES), jnp.float32)

    @pl.loop(0, n_row // (8 * SUB))
    def _(i):
        rows = pl.ds(pl.multiple_of(i * (8 * SUB), 8 * SUB), 8 * SUB)
        for acc in accs:
            acc[rows, :] = zero

    for copy in table_copies:
        copy.wait()
    lane = lax.broadcasted_iota(jnp.int32, (n_pose, n_table), 1)
    chosen = jnp.concatenate(
        [(pose[:, p : p + 1] == lane).astype(jnp.float32) for p in range(n_part)], axis=0
    ).astype(jnp.bfloat16)

    def look_up(table):
        return lax.dot_general(
            chosen, table[...].astype(jnp.float32).astype(jnp.bfloat16),
            (((1,), (1,)), ((), ())), preferred_element_type=jnp.float32,
        )

    idx_v[:, :n_tile] = ((look_up(blocks) * bank_size + look_up(tiles)) * SUB).astype(jnp.int32)
    idx_copy = pltpu.make_async_copy(idx_v, idx_s, idx_sem)
    idx_copy.start()

    for copy in small_copies:
        copy.wait()
    for p in range(n_part):
        spread[p * n_pose : (p + 1) * n_pose, :] = jnp.broadcast_to(weight[:, p : p + 1], (n_pose, LANES))

    @pl.loop(0, square.shape[0] // tile_rows)
    def _(i):
        rows = pl.ds(pl.multiple_of(i * tile_rows, tile_rows), tile_rows)
        t = tra[rows, :].astype(jnp.float32)
        square[rows, :] = t * t
        cross[rows, :] = t * img[rows, :].astype(jnp.float32)

    sublane = lax.broadcasted_iota(jnp.int32, (SUB, LANES), 0)
    bits = [(sublane & (1 << t)) != 0 for t in range(3)]

    def terms(p, j, unit, weights):
        first = pl.multiple_of(unit * tile_rows, tile_rows)
        cell = (j * (n_part // SUB) + p // SUB) * tile_rows + p % SUB
        turned = []
        for c in range(0, SUB, 2):
            pair = proj[pl.ds(first + c * SUB, 2 * SUB), :].astype(jnp.float32)
            for h in range(2):
                x = pair[h * SUB : (h + 1) * SUB]
                row = pl.ds(cell + (c + h) * SUB, 1)
                value = (square[row, :] * x - cross[row, :]) * weights
                turned.append(pltpu.roll(value, c + h, 0) if c + h else value)
        for t, bit in enumerate(bits):
            turned = [jnp.where(bit, turned[(i + (1 << t)) % SUB], turned[i]) for i in range(SUB)]
        result = []
        for k in range(n_pose):
            back = (k % n_acc - k) % SUB
            value = turned[-k % SUB]
            result.append(pltpu.roll(value, back, 0) if back else value)
        return result

    def add_rows(p, j, values):
        at = [idx_s[p * n_pose + k, j] for k in range(n_pose)]
        rows = [pl.ds(pl.multiple_of(at[k], SUB), SUB) for k in range(n_pose)]
        old = [accs[k % n_acc][rows[k], :] for k in range(n_pose)]
        new = []
        for k in range(n_pose):
            total = old[k] + values[k]
            for m in range(k % n_acc, k, n_acc):
                total += jnp.where(at[m] == at[k], 1.0, 0.0) * values[m]
            new.append(total)
        for k in range(n_pose):
            accs[k % n_acc][rows[k], :] = new[k]

    idx_copy.wait()

    @pl.loop(0, n_part)
    def _(p):
        proj_copy(p).wait()
        weights = spread[pl.ds(pl.multiple_of(p * n_pose, n_pose), n_pose), :]
        base = p * n_tile

        def ready(j):
            return terms(p, j, base + j, weights)

        @pl.loop(0, n_tile, step=UNROLL, init_carry=tuple(ready(0) + ready(1)))
        def _(j, carry):
            queue = [list(carry[:n_pose]), list(carry[n_pose:])]
            for u in range(UNROLL):
                ahead = j + u + 2
                queue.append(ready(ahead if u + 2 < UNROLL else jnp.minimum(ahead, n_tile - 1)))
                add_rows(p, j + u, queue.pop(0))
            return tuple(queue[0] + queue[1])

    rep, near, low, high = place[0], place[1], place[2], place[3]
    half_rows = n_row // (n_owner * 2)
    part_size = half_rows // 2
    step = 16 * SUB

    def finish(out, part, h, other, owner, half):
        first = (owner * 2 + half) * half_rows + part * part_size

        @pl.loop(0, part_size // step)
        def _(i):
            rows = pl.ds(pl.multiple_of(first + i * step, step), step)
            total = accs[0][rows, :].reshape(step // SUB, SUB, LANES)
            for turn, acc in enumerate(accs[1:]):
                total += pltpu.roll(acc[rows, :].reshape(step // SUB, SUB, LANES), SUB - 1 - turn, 1)
            out[part, other, h, pl.ds(pl.multiple_of(i * step, step), step), :] = total.reshape(step, LANES)

    for sent, kept, away in ((sent_away, kept_away, 1), (sent_stay, kept_stay, 0)):

        @pl.loop(0, n_owner // 4)
        def _(h):
            for part in range(2):
                for other in range(2):
                    y = near ^ (other if part else away)
                    l = low ^ (away if part else other)
                    owner = ((high ^ h) * 2 + l) * 2 + y
                    finish(sent, part, h, other, owner, 1 - rep)
                    finish(kept, part, h, other, owner, rep)


def tiles_in_order(array):
    lead = array.shape[:-2]
    rows, cells = array.shape[-2:]
    array = array.reshape(lead + (rows // SUB, SUB, cells // LANES, LANES))
    return jnp.swapaxes(array, -3, -2).reshape(-1, LANES)


def accumulate(
    projections, images, transfer, pose_weights, pose_of, pose_blocks, pose_tiles,
    bank_size, n_owner, place,
):
    n_part, n_pose, n_tile, n_cell = projections.shape
    assert n_cell == SUB * LANES and n_pose == SUB and n_part % SUB == 0 and n_tile % UNROLL == 0
    n_row = n_owner * NB_DEV * bank_size * SUB
    n_acc = 4 if n_row * LANES * 4 <= 4 * MIB else 2
    projections = tiles_in_order(jnp.transpose(projections, (0, 2, 1, 3)))
    images = tiles_in_order(jnp.transpose(images, (1, 0, 2)))
    transfer = tiles_in_order(jnp.transpose(transfer, (1, 0, 2)))
    stay = functools.partial(pltpu.with_memory_space_constraint, memory_space=pltpu.HBM)
    hbm = pl.BlockSpec(memory_space=pltpu.HBM)
    smem = pl.BlockSpec(memory_space=pltpu.SMEM)
    vmem = pl.BlockSpec(memory_space=pltpu.VMEM)
    out = jax.ShapeDtypeStruct((2, 2, n_owner // 4, n_row // (n_owner * 4), LANES), jnp.float32)
    return pl.pallas_call(
        functools.partial(accumulate_kernel, bank_size, n_owner, n_acc),
        out_shape=[out] * 4,
        in_specs=[smem] + [hbm] * 7,
        out_specs=[vmem] * 4,
        scratch_shapes=[
            pltpu.VMEM(projections.shape, jnp.bfloat16),
            pltpu.VMEM(images.shape, jnp.bfloat16),
            pltpu.VMEM(transfer.shape, jnp.bfloat16),
            pltpu.VMEM((n_pose, n_part), jnp.float32),
            pltpu.VMEM((n_part * n_pose, LANES), jnp.float32),
            pltpu.VMEM((n_pose, n_part), jnp.int32),
            pltpu.VMEM(pose_blocks.shape[::-1], jnp.int32),
            pltpu.VMEM(pose_tiles.shape[::-1], jnp.int32),
            pltpu.VMEM((n_part * n_pose, LANES), jnp.int32),
            pltpu.SMEM((n_part * n_pose, LANES), jnp.int32),
            pltpu.VMEM(transfer.shape, jnp.float32),
            pltpu.VMEM(transfer.shape, jnp.float32),
        ]
        + [pltpu.VMEM((n_row, LANES), jnp.float32)] * n_acc
        + [
            pltpu.SemaphoreType.DMA((n_part,)),
            pltpu.SemaphoreType.DMA((3,)),
            pltpu.SemaphoreType.DMA((3,)),
            pltpu.SemaphoreType.DMA,
        ],
        compiler_params=pltpu.CompilerParams(vmem_limit_bytes=(40 if n_acc == 4 else 56) * MIB),
        name="accumulate",
    )(
        place, stay(projections), stay(images), stay(transfer),
        stay(pose_weights.T), stay(pose_of.T), stay(pose_blocks.T), stay(pose_tiles.T),
    )


def bank_kernel(place, own, other, bank, out_hbm, block, sem):
    bank_size, n_z, n_cell = bank.shape
    n_half = block.shape[0] // 2
    group = 2 * SUB
    rep = place[0]

    def block_copy(b):
        half = rep if b < n_half else 1 - rep
        return pltpu.make_async_copy(block.at[b], out_hbm.at[half * n_half + b % n_half], sem.at[b])

    for first in range(0, 2 * n_half, 2):
        source = own if first < n_half else other
        rows_of = [(first + b) % n_half * bank_size for b in range(2)]
        for c in range(n_cell // LANES):
            cols = slice(c * LANES, (c + 1) * LANES)

            @pl.loop(0, n_z // group)
            def _(g):
                rows = pl.ds(pl.multiple_of(g * group, group), group)
                weights = [bank[t, rows, cols] for t in range(bank_size)]
                for b in range(2):
                    total = None
                    for t in range(bank_size):
                        at = (rows_of[b] + t) * SUB + c
                        value = weights[t] * source[at : at + 1, :]
                        total = value if total is None else total + value
                    block[first + b, rows, cols] = total

        for b in range(2):
            block_copy(first + b).start()

    for b in range(2 * n_half):
        block_copy(b).wait()


def apply_bank(place, own, other, weight_bank):
    bank_size, n_z, n_cell = weight_bank.shape
    vmem = pl.BlockSpec(memory_space=pltpu.VMEM)
    return pl.pallas_call(
        bank_kernel,
        out_shape=jax.ShapeDtypeStruct((NB_DEV, n_z, n_cell), jnp.float32),
        in_specs=[pl.BlockSpec(memory_space=pltpu.SMEM), vmem, vmem, vmem],
        out_specs=pl.BlockSpec(memory_space=pl.ANY),
        scratch_shapes=[
            pltpu.VMEM((NB_DEV, n_z, n_cell), jnp.float32),
            pltpu.SemaphoreType.DMA((NB_DEV,)),
        ],
        compiler_params=pltpu.CompilerParams(vmem_limit_bytes=32 * MIB),
        name="apply_bank",
    )(place, own, other, weight_bank)


def body(
    projections, images, transfer, pose_weights, pose_of, pose_blocks, pose_tiles, weight_bank
):
    bank_size = weight_bank.shape[0]
    n_blk = lax.axis_size("blk")
    here = lax.axis_index("blk")
    place = jnp.stack([lax.axis_index("rep"), here & 1, (here >> 1) & 1, here >> 2]).astype(jnp.int32)
    sent_away, kept_away, sent_stay, kept_stay = accumulate(
        projections, images, transfer, pose_weights, pose_of, pose_blocks, pose_tiles,
        bank_size, n_blk, place,
    )

    def over_rep(array):
        return lax.ppermute(array, "rep", [(0, 1), (1, 0)])

    def over_blk(array, bits):
        return lax.ppermute(array, "blk", [(i, i ^ bits) for i in range(n_blk)])

    got_away, got_stay = over_rep(sent_away), over_rep(sent_stay)
    first = [kept_away[part] + got_away[part] for part in range(2)]
    first = [over_blk(first[0], 1), over_blk(first[1], 2)]
    second = [kept_stay[part] + got_stay[part] + first[part] for part in range(2)]
    got_second = [over_blk(second[0][1], 2), over_blk(second[1][1], 1)]
    third = jnp.stack([second[part][0] + got_second[part] for part in range(2)], axis=1)
    own = third[0]
    for high in range(1, n_blk // 4):
        own = own + over_blk(third[high], 4 * high)
    own = own.reshape(-1, LANES)
    return apply_bank(place, own, over_rep(own), weight_bank)


def solution(mesh):
    placed = (
        P(("groups", "blk", "rep"), None, None, None),
        P(("groups", "blk", "rep"), None, None),
        P(("groups", "blk", "rep"), None, None),
        P(("groups", "blk", "rep"), None),
        P(("groups", "blk", "rep"), None),
        P("groups", None),
        P("groups", None),
        P(),
    )
    return jax.shard_map(
        body,
        mesh=mesh,
        in_specs=placed,
        out_specs=P(("groups", "blk"), None, None),
        check_vma=False,
    )
```

```python
import functools

import jax
import jax.numpy as jnp
from jax import lax
from jax.experimental import pallas as pl
from jax.experimental.pallas import tpu as pltpu
from jax.sharding import PartitionSpec as P

NB_DEV = 8
LANES = 128
SUB = 8
MIB = 1 << 20
UNROLL = 12
N_BUF = 4


def accumulate_kernel(
    bank_size, n_owner, n_acc,
    place, proj_hbm, img_hbm, tra_hbm, w_hbm, pose_hbm, blocks_hbm, tiles_hbm,
    sent_away, kept_away, sent_stay, kept_stay,
    proj, img, tra, weight, pose, blocks, tiles, idx_v, idx_s, square, cross,
    *rest,
):
    parts, accs = rest[:N_BUF], rest[N_BUF : N_BUF + n_acc]
    proj_sem, small_sem, table_sem, idx_sem = rest[N_BUF + n_acc :]
    n_pose, n_part = pose.shape
    n_tile, n_table = blocks.shape
    n_row = accs[0].shape[0]
    tile_rows = SUB * SUB
    part_rows = n_tile * tile_rows

    table_copies = [
        pltpu.make_async_copy(src, dst, table_sem.at[i])
        for i, (src, dst) in enumerate(((pose_hbm, pose), (blocks_hbm, blocks), (tiles_hbm, tiles)))
    ]
    small_copies = [
        pltpu.make_async_copy(img_hbm, img, small_sem.at[0]),
        pltpu.make_async_copy(tra_hbm, tra, small_sem.at[1]),
        pltpu.make_async_copy(w_hbm, weight, small_sem.at[2]),
    ]
    for copy in table_copies + small_copies:
        copy.start()

    def proj_copy(p):
        rows = pl.ds(pl.multiple_of(p * part_rows, part_rows), part_rows)
        return pltpu.make_async_copy(proj_hbm.at[rows, :], proj.at[rows, :], proj_sem.at[p])

    for p in range(n_part):
        proj_copy(p).start()

    zero = jnp.zeros((8 * SUB, LANES), jnp.float32)

    @pl.loop(0, n_row // (8 * SUB))
    def _(i):
        rows = pl.ds(pl.multiple_of(i * (8 * SUB), 8 * SUB), 8 * SUB)
        for acc in accs:
            acc[rows, :] = zero

    for copy in table_copies:
        copy.wait()
    lane = lax.broadcasted_iota(jnp.int32, (n_pose, n_table), 1)
    chosen = jnp.concatenate(
        [(pose[:, p : p + 1] == lane).astype(jnp.float32) for p in range(n_part)], axis=0
    ).astype(jnp.bfloat16)

    def look_up(table):
        return lax.dot_general(
            table[...].astype(jnp.float32).astype(jnp.bfloat16), chosen,
            (((1,), (1,)), ((), ())), preferred_element_type=jnp.float32,
        )

    idx_v[...] = ((look_up(blocks) * bank_size + look_up(tiles)) * SUB).astype(jnp.int32)
    idx_copy = pltpu.make_async_copy(idx_v, idx_s, idx_sem)
    idx_copy.start()

    for copy in small_copies:
        copy.wait()
    @pl.loop(0, square.shape[0] // tile_rows)
    def _(i):
        rows = pl.ds(pl.multiple_of(i * tile_rows, tile_rows), tile_rows)
        t = tra[rows, :].astype(jnp.float32)
        square[rows, :] = t * t
        cross[rows, :] = t * img[rows, :].astype(jnp.float32)

    def stage(unit, part):
        first = pl.multiple_of(unit * tile_rows, tile_rows)
        part[...] = proj[pl.ds(first, tile_rows), :].astype(jnp.float32)

    def terms(p, j, part, weights):
        cell = pl.ds((j * (n_part // SUB) + p // SUB) * tile_rows + p % SUB, SUB, stride=SUB)
        tt, ti = square[cell, :], cross[cell, :]
        return [(tt * part[pl.ds(k, SUB, stride=SUB), :] - ti) * weights[k] for k in range(n_pose)]

    def add_rows(p, j, values):
        for first in range(0, n_pose, n_acc):
            group = range(first, first + n_acc)
            rows = [pl.ds(pl.multiple_of(idx_s[j, p * n_pose + k], SUB), SUB) for k in group]
            old = [accs[i][rows[i], :] for i in range(n_acc)]
            for i, k in enumerate(group):
                accs[i][rows[i], :] = old[i] + values[k]

    idx_copy.wait()
    n_buf = len(parts)

    @pl.loop(0, n_part)
    def _(p):
        proj_copy(p).wait()
        weights = [jnp.full((SUB, LANES), weight[k, p], jnp.float32) for k in range(n_pose)]
        base = p * n_tile
        stage(base, parts[0])
        stage(base + 1, parts[1])

        @pl.loop(0, n_tile, step=UNROLL, init_carry=tuple(terms(p, 0, parts[0], weights)))
        def _(j, values):
            for u in range(UNROLL):
                ahead = j + u + 2
                stage(base + (ahead if u + 2 < UNROLL else jnp.minimum(ahead, n_tile - 1)), parts[(u + 2) % n_buf])
                following = j + u + 1
                later = terms(
                    p, following if u + 1 < UNROLL else jnp.minimum(following, n_tile - 1),
                    parts[(u + 1) % n_buf], weights,
                )
                add_rows(p, j + u, values)
                values = later
            return tuple(values)

    rep, near, low, high = place[0], place[1], place[2], place[3]
    half_rows = n_row // (n_owner * 2)
    part_size = half_rows // 2
    step = 16 * SUB

    def finish(out, part, h, other, owner, half):
        first = (owner * 2 + half) * half_rows + part * part_size

        @pl.loop(0, part_size // step)
        def _(i):
            rows = pl.ds(pl.multiple_of(first + i * step, step), step)
            total = accs[0][rows, :]
            for acc in accs[1:]:
                total += acc[rows, :]
            out[part, other, h, pl.ds(pl.multiple_of(i * step, step), step), :] = total

    for sent, kept, away in ((sent_away, kept_away, 1), (sent_stay, kept_stay, 0)):

        @pl.loop(0, n_owner // 4)
        def _(h):
            for part in range(2):
                for other in range(2):
                    y = near ^ (other if part else away)
                    l = low ^ (away if part else other)
                    owner = ((high ^ h) * 2 + l) * 2 + y
                    finish(sent, part, h, other, owner, 1 - rep)
                    finish(kept, part, h, other, owner, rep)


def tiles_in_order(array):
    lead = array.shape[:-2]
    rows, cells = array.shape[-2:]
    array = array.reshape(lead + (rows // SUB, SUB, cells // LANES, LANES))
    return jnp.swapaxes(array, -3, -2).reshape(-1, LANES)


def accumulate(
    projections, images, transfer, pose_weights, pose_of, pose_blocks, pose_tiles,
    bank_size, n_owner, place,
):
    n_part, n_pose, n_tile, n_cell = projections.shape
    assert n_cell == SUB * LANES and n_pose == SUB and n_part % SUB == 0 and n_tile % UNROLL == 0 and UNROLL % N_BUF == 0
    n_row = n_owner * NB_DEV * bank_size * SUB
    n_acc = 4 if n_row * LANES * 4 <= 4 * MIB else 2
    projections = tiles_in_order(jnp.transpose(projections, (0, 2, 1, 3)))
    images = tiles_in_order(jnp.transpose(images, (1, 0, 2)))
    transfer = tiles_in_order(jnp.transpose(transfer, (1, 0, 2)))
    stay = functools.partial(pltpu.with_memory_space_constraint, memory_space=pltpu.HBM)
    hbm = pl.BlockSpec(memory_space=pltpu.HBM)
    smem = pl.BlockSpec(memory_space=pltpu.SMEM)
    vmem = pl.BlockSpec(memory_space=pltpu.VMEM)
    out = jax.ShapeDtypeStruct((2, 2, n_owner // 4, n_row // (n_owner * 4), LANES), jnp.float32)
    return pl.pallas_call(
        functools.partial(accumulate_kernel, bank_size, n_owner, n_acc),
        out_shape=[out] * 4,
        in_specs=[smem] + [hbm] * 7,
        out_specs=[vmem] * 4,
        scratch_shapes=[
            pltpu.VMEM(projections.shape, jnp.bfloat16),
            pltpu.VMEM(images.shape, jnp.bfloat16),
            pltpu.VMEM(transfer.shape, jnp.bfloat16),
            pltpu.SMEM((n_pose, n_part), jnp.float32),
            pltpu.VMEM((n_pose, n_part), jnp.int32),
            pltpu.VMEM(pose_blocks.shape[::-1], jnp.int32),
            pltpu.VMEM(pose_tiles.shape[::-1], jnp.int32),
            pltpu.VMEM((n_tile, n_part * n_pose), jnp.int32),
            pltpu.SMEM((n_tile, n_part * n_pose), jnp.int32),
            pltpu.VMEM(transfer.shape, jnp.float32),
            pltpu.VMEM(transfer.shape, jnp.float32),
        ]
        + [pltpu.VMEM((n_pose * SUB, LANES), jnp.float32)] * N_BUF
        + [pltpu.VMEM((n_row, LANES), jnp.float32)] * n_acc
        + [
            pltpu.SemaphoreType.DMA((n_part,)),
            pltpu.SemaphoreType.DMA((3,)),
            pltpu.SemaphoreType.DMA((3,)),
            pltpu.SemaphoreType.DMA,
        ],
        compiler_params=pltpu.CompilerParams(vmem_limit_bytes=(40 if n_acc == 4 else 56) * MIB),
        name="accumulate",
    )(
        place, stay(projections), stay(images), stay(transfer),
        stay(pose_weights.T), stay(pose_of.T), stay(pose_blocks.T), stay(pose_tiles.T),
    )


def bank_kernel(place, own, other, bank, out):
    bank_size, n_z, n_cell = bank.shape
    n_half = out.shape[0] // 2
    group = 2 * SUB
    rep = place[0]

    for c in range(n_cell // LANES):
        cols = slice(c * LANES, (c + 1) * LANES)

        @pl.loop(0, n_z // group)
        def _(g):
            rows = pl.ds(pl.multiple_of(g * group, group), group)
            weights = [bank[t, rows, cols] for t in range(bank_size)]
            for source, half in ((own, rep), (other, 1 - rep)):
                for b in range(n_half):
                    total = None
                    for t in range(bank_size):
                        at = (b * bank_size + t) * SUB + c
                        value = weights[t] * source[at : at + 1, :]
                        total = value if total is None else total + value
                    out[half * n_half + b, rows, cols] = total


def apply_bank(place, own, other, weight_bank):
    bank_size, n_z, n_cell = weight_bank.shape
    vmem = pl.BlockSpec(memory_space=pltpu.VMEM)
    return pl.pallas_call(
        bank_kernel,
        out_shape=jax.ShapeDtypeStruct((NB_DEV, n_z, n_cell), jnp.float32),
        in_specs=[pl.BlockSpec(memory_space=pltpu.SMEM), vmem, vmem, vmem],
        out_specs=vmem,
        compiler_params=pltpu.CompilerParams(vmem_limit_bytes=32 * MIB),
        name="apply_bank",
    )(place, own, other, weight_bank)


def body(
    projections, images, transfer, pose_weights, pose_of, pose_blocks, pose_tiles, weight_bank
):
    bank_size = weight_bank.shape[0]
    n_blk = lax.axis_size("blk")
    here = lax.axis_index("blk")
    place = jnp.stack([lax.axis_index("rep"), here & 1, (here >> 1) & 1, here >> 2]).astype(jnp.int32)
    sent_away, kept_away, sent_stay, kept_stay = accumulate(
        projections, images, transfer, pose_weights, pose_of, pose_blocks, pose_tiles,
        bank_size, n_blk, place,
    )

    def over_rep(array):
        return lax.ppermute(array, "rep", [(0, 1), (1, 0)])

    def over_blk(array, bits):
        return lax.ppermute(array, "blk", [(i, i ^ bits) for i in range(n_blk)])

    got_away, got_stay = over_rep(sent_away), over_rep(sent_stay)
    first = [kept_away[part] + got_away[part] for part in range(2)]
    first = [over_blk(first[0], 1), over_blk(first[1], 2)]
    second = [kept_stay[part] + got_stay[part] + first[part] for part in range(2)]
    got_second = [over_blk(second[0][1], 2), over_blk(second[1][1], 1)]
    third = jnp.stack([second[part][0] + got_second[part] for part in range(2)], axis=1)
    own = third[0]
    for high in range(1, n_blk // 4):
        own = own + over_blk(third[high], 4 * high)
    own = own.reshape(-1, LANES)
    return apply_bank(place, own, over_rep(own), weight_bank)


def solution(mesh):
    placed = (
        P(("groups", "blk", "rep"), None, None, None),
        P(("groups", "blk", "rep"), None, None),
        P(("groups", "blk", "rep"), None, None),
        P(("groups", "blk", "rep"), None),
        P(("groups", "blk", "rep"), None),
        P("groups", None),
        P("groups", None),
        P(),
    )
    return jax.shard_map(
        body,
        mesh=mesh,
        in_specs=placed,
        out_specs=P(("groups", "blk"), None, None),
        check_vma=False,
    )
```

```python
import functools

import jax
import jax.numpy as jnp
from jax import lax
from jax.experimental import pallas as pl
from jax.experimental.pallas import tpu as pltpu
from jax.sharding import PartitionSpec as P

NB_DEV = 8
LANES = 128
SUB = 8
MIB = 1 << 20
UNROLL = 12
N_BUF = 4


def accumulate_kernel(
    bank_size, n_owner, n_acc,
    place, proj_hbm, img_hbm, tra_hbm, w_hbm, pose_hbm, blocks_hbm, tiles_hbm,
    sent_away_1, kept_away_1, sent_stay_1, kept_stay_1, sent_away_2, kept_away_2, sent_stay_2, kept_stay_2,
    proj, img, tra, weight, pose, blocks, tiles, idx_v, idx_s, square, cross,
    *rest,
):
    parts, accs = rest[:N_BUF], rest[N_BUF : N_BUF + n_acc]
    proj_sem, small_sem, table_sem, idx_sem = rest[N_BUF + n_acc :]
    n_pose, n_part = pose.shape
    n_tile, n_table = blocks.shape
    n_row = accs[0].shape[0]
    tile_rows = SUB * SUB
    part_rows = n_tile * tile_rows

    table_copies = [
        pltpu.make_async_copy(src, dst, table_sem.at[i])
        for i, (src, dst) in enumerate(((pose_hbm, pose), (blocks_hbm, blocks), (tiles_hbm, tiles)))
    ]
    small_copies = [
        pltpu.make_async_copy(img_hbm, img, small_sem.at[0]),
        pltpu.make_async_copy(tra_hbm, tra, small_sem.at[1]),
        pltpu.make_async_copy(w_hbm, weight, small_sem.at[2]),
    ]
    for copy in table_copies + small_copies:
        copy.start()

    def proj_copy(p):
        rows = pl.ds(pl.multiple_of(p * part_rows, part_rows), part_rows)
        return pltpu.make_async_copy(proj_hbm.at[rows, :], proj.at[rows, :], proj_sem.at[p])

    for p in range(n_part):
        proj_copy(p).start()

    zero = jnp.zeros((16 * SUB, LANES), jnp.float32)

    def clear(half):
        @pl.loop(0, n_row // (32 * SUB))
        def _(i):
            rows = pl.ds(pl.multiple_of(half * (n_row // 2) + i * (16 * SUB), 16 * SUB), 16 * SUB)
            for acc in accs:
                acc[rows, :] = zero

    clear(0)
    for copy in table_copies:
        copy.wait()
    lane = lax.broadcasted_iota(jnp.int32, (n_pose, n_table), 1)
    chosen = jnp.concatenate(
        [(pose[:, p : p + 1] == lane).astype(jnp.float32) for p in range(n_part)], axis=0
    ).astype(jnp.bfloat16)

    def look_up(table):
        return lax.dot_general(
            table[...].astype(jnp.float32).astype(jnp.bfloat16), chosen,
            (((1,), (1,)), ((), ())), preferred_element_type=jnp.float32,
        )

    idx_v[...] = ((look_up(blocks) * bank_size + look_up(tiles)) * SUB).astype(jnp.int32)
    idx_copy = pltpu.make_async_copy(idx_v, idx_s, idx_sem)
    idx_copy.start()
    clear(1)

    for copy in small_copies:
        copy.wait()
    @pl.loop(0, square.shape[0] // tile_rows)
    def _(i):
        rows = pl.ds(pl.multiple_of(i * tile_rows, tile_rows), tile_rows)
        t = tra[rows, :].astype(jnp.float32)
        square[rows, :] = t * t
        cross[rows, :] = t * img[rows, :].astype(jnp.float32)

    def stage(unit, part):
        first = pl.multiple_of(unit * tile_rows, tile_rows)
        part[...] = proj[pl.ds(first, tile_rows), :].astype(jnp.float32)

    def terms(p, j, part, weights):
        cell = pl.ds((j * (n_part // SUB) + p // SUB) * tile_rows + p % SUB, SUB, stride=SUB)
        tt, ti = square[cell, :], cross[cell, :]
        return [(tt * part[pl.ds(k, SUB, stride=SUB), :] - ti) * weights[k] for k in range(n_pose)]

    def add_rows(p, j, values):
        at = [idx_s[j, p * n_pose + k] for k in range(n_pose)]
        rows = [pl.ds(pl.multiple_of(at[k], SUB), SUB) for k in range(n_pose)]
        old = [accs[k % n_acc][rows[k], :] for k in range(n_pose)]
        new = []
        for k in range(n_pose):
            total = old[k]
            for m in range(k % n_acc, k, n_acc):
                total = jnp.where(at[m] == at[k], new[m], total)
            new.append(total + values[k])
        for k in range(n_pose):
            accs[k % n_acc][rows[k], :] = new[k]

    idx_copy.wait()
    n_buf = len(parts)

    @pl.loop(0, n_part)
    def _(p):
        proj_copy(p).wait()
        weights = [jnp.full((SUB, LANES), weight[k, p], jnp.float32) for k in range(n_pose)]
        base = p * n_tile
        stage(base, parts[0])
        stage(base + 1, parts[1])

        @pl.loop(0, n_tile, step=UNROLL, init_carry=tuple(terms(p, 0, parts[0], weights)))
        def _(j, values):
            for u in range(UNROLL):
                ahead = j + u + 2
                stage(base + (ahead if u + 2 < UNROLL else jnp.minimum(ahead, n_tile - 1)), parts[(u + 2) % n_buf])
                following = j + u + 1
                later = terms(
                    p, following if u + 1 < UNROLL else jnp.minimum(following, n_tile - 1),
                    parts[(u + 1) % n_buf], weights,
                )
                add_rows(p, j + u, values)
                values = later
            return tuple(values)

    rep, near, low, high = place[0], place[1], place[2], place[3]
    half_rows = n_row // (n_owner * 2)
    size = half_rows // 4
    step = min(size, 16 * SUB)

    def finish(out, block, part, other, h, owner, half):
        first = (owner * 2 + half) * half_rows + block * size

        @pl.loop(0, size // step)
        def _(i):
            rows = pl.ds(pl.multiple_of(first + i * step, step), step)
            total = accs[0][rows, :]
            for acc in accs[1:]:
                total += acc[rows, :]
            out[part, other, h, pl.ds(pl.multiple_of(i * step, step), step), :] = total

    for group, sent, kept, away in (
        (0, sent_away_1, kept_away_1, 1), (0, sent_stay_1, kept_stay_1, 0),
        (1, sent_away_2, kept_away_2, 1), (1, sent_stay_2, kept_stay_2, 0),
    ):

        @pl.loop(0, n_owner // 4)
        def _(h):
            for part in range(2):
                for other in range(2):
                    y = near ^ (other if part else away)
                    l = low ^ (away if part else other)
                    owner = ((high ^ h) * 2 + l) * 2 + y
                    finish(sent, part * 2 + group, part, other, h, owner, 1 - rep)
                    finish(kept, part * 2 + group, part, other, h, owner, rep)


def tiles_in_order(array):
    lead = array.shape[:-2]
    rows, cells = array.shape[-2:]
    array = array.reshape(lead + (rows // SUB, SUB, cells // LANES, LANES))
    return jnp.swapaxes(array, -3, -2).reshape(-1, LANES)


def accumulate(
    projections, images, transfer, pose_weights, pose_of, pose_blocks, pose_tiles,
    bank_size, n_owner, place,
):
    n_part, n_pose, n_tile, n_cell = projections.shape
    assert n_cell == SUB * LANES and n_pose == SUB and n_part % SUB == 0 and n_tile % UNROLL == 0 and UNROLL % N_BUF == 0
    n_row = n_owner * NB_DEV * bank_size * SUB
    n_acc = 4 if n_row * LANES * 4 <= 4 * MIB else 2
    projections = tiles_in_order(jnp.transpose(projections, (0, 2, 1, 3)))
    images = tiles_in_order(jnp.transpose(images, (1, 0, 2)))
    transfer = tiles_in_order(jnp.transpose(transfer, (1, 0, 2)))
    stay = functools.partial(pltpu.with_memory_space_constraint, memory_space=pltpu.HBM)
    hbm = pl.BlockSpec(memory_space=pltpu.HBM)
    smem = pl.BlockSpec(memory_space=pltpu.SMEM)
    vmem = pl.BlockSpec(memory_space=pltpu.VMEM)
    out = jax.ShapeDtypeStruct((2, 2, n_owner // 4, n_row // (n_owner * 8), LANES), jnp.float32)
    return pl.pallas_call(
        functools.partial(accumulate_kernel, bank_size, n_owner, n_acc),
        out_shape=[out] * 8,
        in_specs=[smem] + [hbm] * 7,
        out_specs=[vmem] * 8,
        scratch_shapes=[
            pltpu.VMEM(projections.shape, jnp.bfloat16),
            pltpu.VMEM(images.shape, jnp.bfloat16),
            pltpu.VMEM(transfer.shape, jnp.bfloat16),
            pltpu.SMEM((n_pose, n_part), jnp.float32),
            pltpu.VMEM((n_pose, n_part), jnp.int32),
            pltpu.VMEM(pose_blocks.shape[::-1], jnp.int32),
            pltpu.VMEM(pose_tiles.shape[::-1], jnp.int32),
            pltpu.VMEM((n_tile, n_part * n_pose), jnp.int32),
            pltpu.SMEM((n_tile, n_part * n_pose), jnp.int32),
            pltpu.VMEM(transfer.shape, jnp.float32),
            pltpu.VMEM(transfer.shape, jnp.float32),
        ]
        + [pltpu.VMEM((n_pose * SUB, LANES), jnp.float32)] * N_BUF
        + [pltpu.VMEM((n_row, LANES), jnp.float32)] * n_acc
        + [
            pltpu.SemaphoreType.DMA((n_part,)),
            pltpu.SemaphoreType.DMA((3,)),
            pltpu.SemaphoreType.DMA((3,)),
            pltpu.SemaphoreType.DMA,
        ],
        compiler_params=pltpu.CompilerParams(vmem_limit_bytes=(40 if n_acc == 4 else 56) * MIB),
        name="accumulate",
    )(
        place, stay(projections), stay(images), stay(transfer),
        stay(pose_weights.T), stay(pose_of.T), stay(pose_blocks.T), stay(pose_tiles.T),
    )


def middle_kernel(kept_stay, got_stay, near_a, near_b, kept_away, got_away, away_a, away_b, own, next_a, next_b):
    for part, got, away, following in ((0, near_a, away_a, next_a), (1, near_b, away_b, next_b)):
        own[part] = kept_stay[part, 0] + got_stay[part, 0] + got[0]
        away[...] = kept_stay[part, 1] + got_stay[part, 1] + got[1]
        following[...] = kept_away[part] + got_away[part]


def middle(*operands):
    shape = operands[0].shape
    vmem = pl.BlockSpec(memory_space=pltpu.VMEM)

    def like(*lead):
        return jax.ShapeDtypeStruct(lead + shape[2:], jnp.float32)

    return pl.pallas_call(
        middle_kernel,
        out_shape=[like(), like(), like(2), like(2), like(2)],
        in_specs=[vmem] * len(operands),
        out_specs=[vmem] * 5,
        compiler_params=pltpu.CompilerParams(vmem_limit_bytes=32 * MIB),
        name="middle",
    )(*operands)


def bank_kernel(place, own_1, own_2, other_1, other_2, bank, out):
    bank_size, n_z, n_cell = bank.shape
    n_half = out.shape[0] // 2
    group = 2 * SUB
    rep = place[0]

    for c in range(n_cell // LANES):
        cols = slice(c * LANES, (c + 1) * LANES)

        @pl.loop(0, n_z // group)
        def _(g):
            rows = pl.ds(pl.multiple_of(g * group, group), group)
            weights = [bank[t, rows, cols] for t in range(bank_size)]
            for sources, half in (((own_1, own_2), rep), ((other_1, other_2), 1 - rep)):
                for b in range(n_half):
                    total = None
                    for t in range(bank_size):
                        value = weights[t] * sources[b % 2][b // 2, t, c : c + 1, :]
                        total = value if total is None else total + value
                    out[half * n_half + b, rows, cols] = total


def apply_bank(place, sums, weight_bank):
    bank_size, n_z, n_cell = weight_bank.shape
    vmem = pl.BlockSpec(memory_space=pltpu.VMEM)
    sums = [array.reshape(2, bank_size, SUB, LANES) for array in sums]
    return pl.pallas_call(
        bank_kernel,
        out_shape=jax.ShapeDtypeStruct((NB_DEV, n_z, n_cell), jnp.float32),
        in_specs=[pl.BlockSpec(memory_space=pltpu.SMEM)] + [vmem] * 5,
        out_specs=vmem,
        compiler_params=pltpu.CompilerParams(vmem_limit_bytes=32 * MIB),
        name="apply_bank",
    )(place, *sums, weight_bank)


def body(
    projections, images, transfer, pose_weights, pose_of, pose_blocks, pose_tiles, weight_bank
):
    bank_size = weight_bank.shape[0]
    n_blk = lax.axis_size("blk")
    here = lax.axis_index("blk")
    place = jnp.stack([lax.axis_index("rep"), here & 1, (here >> 1) & 1, here >> 2]).astype(jnp.int32)
    outs = accumulate(
        projections, images, transfer, pose_weights, pose_of, pose_blocks, pose_tiles,
        bank_size, n_blk, place,
    )

    def over_rep(array):
        return lax.ppermute(array, "rep", [(0, 1), (1, 0)])

    def over_blk(array, bits):
        return lax.ppermute(array, "blk", [(i, i ^ bits) for i in range(n_blk)])

    def last_step(own, got):
        third = jnp.stack([own[part] + got[part] for part in range(2)], axis=1)
        total = third[0]
        for high in range(1, n_blk // 4):
            total = total + over_blk(third[high], 4 * high)
        return total

    (sent_away_1, kept_away_1, sent_stay_1, kept_stay_1), (sent_away_2, kept_away_2, sent_stay_2, kept_stay_2) = (
        outs[:4], outs[4:]
    )
    got_away_1, got_stay_1 = over_rep(sent_away_1), over_rep(sent_stay_1)
    got_away_2, got_stay_2 = over_rep(sent_away_2), over_rep(sent_stay_2)
    first_1 = [kept_away_1[part] + got_away_1[part] for part in range(2)]
    near_1 = [over_blk(first_1[0], 1), over_blk(first_1[1], 2)]
    away_a, away_b, own_1, first_2a, first_2b = middle(
        kept_stay_1, got_stay_1, *near_1, kept_away_2, got_away_2
    )
    far_1 = [over_blk(away_a, 2), over_blk(away_b, 1)]
    near_2 = [over_blk(first_2a, 1), over_blk(first_2b, 2)]
    own_1 = last_step(own_1, far_1)
    second_2 = [kept_stay_2[part] + got_stay_2[part] + near_2[part] for part in range(2)]
    far_2 = [over_blk(second_2[0][1], 2), over_blk(second_2[1][1], 1)]
    own_2 = last_step([second_2[0][0], second_2[1][0]], far_2)
    return apply_bank(place, (own_1, own_2, over_rep(own_1), over_rep(own_2)), weight_bank)


def solution(mesh):
    placed = (
        P(("groups", "blk", "rep"), None, None, None),
        P(("groups", "blk", "rep"), None, None),
        P(("groups", "blk", "rep"), None, None),
        P(("groups", "blk", "rep"), None),
        P(("groups", "blk", "rep"), None),
        P("groups", None),
        P("groups", None),
        P(),
    )
    return jax.shard_map(
        body,
        mesh=mesh,
        in_specs=placed,
        out_specs=P(("groups", "blk"), None, None),
        check_vma=False,
    )
```

```python
import functools

import jax
import jax.numpy as jnp
from jax import lax
from jax.experimental import pallas as pl
from jax.experimental.pallas import tpu as pltpu
from jax.sharding import PartitionSpec as P

NB_DEV = 8
LANES = 128
SUB = 8
MIB = 1 << 20
UNROLL = 12
ORDERS = ("ylh", "yhl", "lyh", "hyl")
N_BUF = 4


def accumulate_kernel(
    bank_size, n_owner, n_acc,
    place, proj_hbm, img_hbm, tra_hbm, w_hbm, pose_hbm, blocks_hbm, tiles_hbm,
    sent_away, kept_away, sent_stay, kept_stay,
    proj, img, tra, weight, pose, blocks, tiles, idx_v, idx_s, same_v, same_s, square, cross,
    *rest,
):
    parts, accs = rest[:N_BUF], rest[N_BUF : N_BUF + n_acc]
    proj_sem, small_sem, table_sem, idx_sem = rest[N_BUF + n_acc :]
    n_pose, n_part = pose.shape
    n_tile, n_table = blocks.shape
    n_row = accs[0].shape[0]
    tile_rows = SUB * SUB
    part_rows = n_tile * tile_rows

    table_copies = [
        pltpu.make_async_copy(src, dst, table_sem.at[i])
        for i, (src, dst) in enumerate(((pose_hbm, pose), (blocks_hbm, blocks), (tiles_hbm, tiles)))
    ]
    small_copies = [
        pltpu.make_async_copy(img_hbm, img, small_sem.at[0]),
        pltpu.make_async_copy(tra_hbm, tra, small_sem.at[1]),
        pltpu.make_async_copy(w_hbm, weight, small_sem.at[2]),
    ]
    for copy in table_copies + small_copies:
        copy.start()

    def proj_copy(p):
        rows = pl.ds(pl.multiple_of(p * part_rows, part_rows), part_rows)
        return pltpu.make_async_copy(proj_hbm.at[rows, :], proj.at[rows, :], proj_sem.at[p])

    for p in range(n_part):
        proj_copy(p).start()

    zero = jnp.zeros((16 * SUB, LANES), jnp.float32)

    def clear(half):
        @pl.loop(0, n_row // (32 * SUB))
        def _(i):
            rows = pl.ds(pl.multiple_of(half * (n_row // 2) + i * (16 * SUB), 16 * SUB), 16 * SUB)
            for acc in accs:
                acc[rows, :] = zero

    clear(0)
    for copy in table_copies:
        copy.wait()
    lane = lax.broadcasted_iota(jnp.int32, (n_pose, n_table), 1)
    chosen = jnp.concatenate(
        [(pose[:, p : p + 1] == lane).astype(jnp.float32) for p in range(n_part)], axis=0
    ).astype(jnp.bfloat16)

    def look_up(table):
        return lax.dot_general(
            table[...].astype(jnp.float32).astype(jnp.bfloat16), chosen,
            (((1,), (1,)), ((), ())), preferred_element_type=jnp.float32,
        )

    idx_v[...] = ((look_up(blocks) * bank_size + look_up(tiles)) * SUB).astype(jnp.int32)
    for d in range(n_acc, n_pose, n_acc):
        shifted = pltpu.roll(idx_v[...], idx_v.shape[1] - d, 1)
        at = (d // n_acc - 1) * n_tile
        same_v[at : at + n_tile, :] = jnp.where(idx_v[...] == shifted, 1.0, 0.0)
    idx_copies = [
        pltpu.make_async_copy(idx_v, idx_s, idx_sem.at[0]),
        pltpu.make_async_copy(same_v, same_s, idx_sem.at[1]),
    ]
    for copy in idx_copies:
        copy.start()
    clear(1)

    for copy in small_copies:
        copy.wait()
    @pl.loop(0, square.shape[0] // tile_rows)
    def _(i):
        rows = pl.ds(pl.multiple_of(i * tile_rows, tile_rows), tile_rows)
        t = tra[rows, :].astype(jnp.float32)
        square[rows, :] = t * t
        cross[rows, :] = t * img[rows, :].astype(jnp.float32)

    def stage(unit, part):
        first = pl.multiple_of(unit * tile_rows, tile_rows)
        part[...] = proj[pl.ds(first, tile_rows), :].astype(jnp.float32)

    def terms(p, j, part, weights):
        cell = pl.ds((j * (n_part // SUB) + p // SUB) * tile_rows + p % SUB, SUB, stride=SUB)
        tt, ti = square[cell, :], cross[cell, :]
        return [(tt * part[pl.ds(k, SUB, stride=SUB), :] - ti) * weights[k] for k in range(n_pose)]

    def add_rows(p, j, values):
        at = [idx_s[j, p * n_pose + k] for k in range(n_pose)]
        rows = [pl.ds(pl.multiple_of(at[k], SUB), SUB) for k in range(n_pose)]
        old = [accs[k % n_acc][rows[k], :] for k in range(n_pose)]
        new = []
        for k in range(n_pose):
            total = old[k] + values[k]
            for m in range(k % n_acc, k, n_acc):
                total += same_s[((k - m) // n_acc - 1) * n_tile + j, p * n_pose + m] * values[m]
            new.append(total)
        for k in range(n_pose):
            accs[k % n_acc][rows[k], :] = new[k]

    for copy in idx_copies:
        copy.wait()
    n_buf = len(parts)

    @pl.loop(0, n_part)
    def _(p):
        proj_copy(p).wait()
        weights = [jnp.full((SUB, LANES), weight[k, p], jnp.float32) for k in range(n_pose)]
        base = p * n_tile
        stage(base, parts[0])
        stage(base + 1, parts[1])

        @pl.loop(0, n_tile, step=UNROLL, init_carry=tuple(terms(p, 0, parts[0], weights)))
        def _(j, values):
            for u in range(UNROLL):
                ahead = j + u + 2
                stage(base + (ahead if u + 2 < UNROLL else jnp.minimum(ahead, n_tile - 1)), parts[(u + 2) % n_buf])
                following = j + u + 1
                later = terms(
                    p, following if u + 1 < UNROLL else jnp.minimum(following, n_tile - 1),
                    parts[(u + 1) % n_buf], weights,
                )
                add_rows(p, j + u, values)
                values = later
            return tuple(values)

    rep, near, low, high = place[0], place[1], place[2], place[3]
    half_rows = n_row // (n_owner * 2)
    size = half_rows // len(ORDERS)
    sizes = {"y": 2, "l": 2, "h": n_owner // 4}

    def finish(out, place_of, part, owner, half):
        first = pl.multiple_of((owner * 2 + half) * half_rows + part * size, size)
        rows = pl.ds(first, size)
        total = accs[0][rows, :]
        for acc in accs[1:]:
            total += acc[rows, :]
        out[place_of] = total

    def pieces(sent, kept, begin, part, firsts):
        order = ORDERS[part]
        inner = sizes[order[1]] * sizes[order[2]]

        @pl.loop(0, len(firsts) * inner)
        def _(i):
            off = {order[0]: firsts[0] + i // inner}
            off[order[1]] = i % inner // sizes[order[2]]
            off[order[2]] = i % sizes[order[2]]
            owner = ((high ^ off["h"]) * 2 + (low ^ off["l"])) * 2 + (near ^ off["y"])
            finish(sent, begin + i, part, owner, 1 - rep)
            finish(kept, begin + i, part, owner, rep)

        return begin + len(firsts) * inner

    for sent, kept, away in ((sent_away, kept_away, True), (sent_stay, kept_stay, False)):
        begin = 0
        for part, order in enumerate(ORDERS):
            begin = pieces(sent, kept, begin, part, range(1, sizes[order[0]]) if away else range(1))


def tiles_in_order(array):
    lead = array.shape[:-2]
    rows, cells = array.shape[-2:]
    array = array.reshape(lead + (rows // SUB, SUB, cells // LANES, LANES))
    return jnp.swapaxes(array, -3, -2).reshape(-1, LANES)


def accumulate(
    projections, images, transfer, pose_weights, pose_of, pose_blocks, pose_tiles,
    bank_size, n_owner, place,
):
    n_part, n_pose, n_tile, n_cell = projections.shape
    assert n_cell == SUB * LANES and n_pose == SUB and n_part % SUB == 0 and n_tile % UNROLL == 0 and UNROLL % N_BUF == 0
    n_row = n_owner * NB_DEV * bank_size * SUB
    n_acc = 4 if n_row * LANES * 4 <= 4 * MIB else 2
    projections = tiles_in_order(jnp.transpose(projections, (0, 2, 1, 3)))
    images = tiles_in_order(jnp.transpose(images, (1, 0, 2)))
    transfer = tiles_in_order(jnp.transpose(transfer, (1, 0, 2)))
    stay = functools.partial(pltpu.with_memory_space_constraint, memory_space=pltpu.HBM)
    hbm = pl.BlockSpec(memory_space=pltpu.HBM)
    smem = pl.BlockSpec(memory_space=pltpu.SMEM)
    vmem = pl.BlockSpec(memory_space=pltpu.VMEM)
    n_high = n_owner // 4
    size = n_row // (n_owner * 2 * len(ORDERS))

    def out(pieces):
        return jax.ShapeDtypeStruct((pieces, size, LANES), jnp.float32)

    return pl.pallas_call(
        functools.partial(accumulate_kernel, bank_size, n_owner, n_acc),
        out_shape=[out(6 * n_high + 4 * (n_high - 1))] * 2 + [out(6 * n_high + 4)] * 2,
        in_specs=[smem] + [hbm] * 7,
        out_specs=[vmem] * 4,
        scratch_shapes=[
            pltpu.VMEM(projections.shape, jnp.bfloat16),
            pltpu.VMEM(images.shape, jnp.bfloat16),
            pltpu.VMEM(transfer.shape, jnp.bfloat16),
            pltpu.SMEM((n_pose, n_part), jnp.float32),
            pltpu.VMEM((n_pose, n_part), jnp.int32),
            pltpu.VMEM(pose_blocks.shape[::-1], jnp.int32),
            pltpu.VMEM(pose_tiles.shape[::-1], jnp.int32),
            pltpu.VMEM((n_tile, n_part * n_pose), jnp.int32),
            pltpu.SMEM((n_tile, n_part * n_pose), jnp.int32),
            pltpu.VMEM((n_tile * (n_pose // n_acc - 1), n_part * n_pose), jnp.float32),
            pltpu.SMEM((n_tile * (n_pose // n_acc - 1), n_part * n_pose), jnp.float32),
            pltpu.VMEM(transfer.shape, jnp.float32),
            pltpu.VMEM(transfer.shape, jnp.float32),
        ]
        + [pltpu.VMEM((n_pose * SUB, LANES), jnp.float32)] * N_BUF
        + [pltpu.VMEM((n_row, LANES), jnp.float32)] * n_acc
        + [
            pltpu.SemaphoreType.DMA((n_part,)),
            pltpu.SemaphoreType.DMA((3,)),
            pltpu.SemaphoreType.DMA((3,)),
            pltpu.SemaphoreType.DMA((2,)),
        ],
        compiler_params=pltpu.CompilerParams(vmem_limit_bytes=(40 if n_acc == 4 else 56) * MIB),
        name="accumulate",
    )(
        place, stay(projections), stay(images), stay(transfer),
        stay(pose_weights.T), stay(pose_of.T), stay(pose_blocks.T), stay(pose_tiles.T),
    )


def in_vmem(kernel, name, pieces, *operands):
    vmem = pl.BlockSpec(memory_space=pltpu.VMEM)
    size = operands[0].shape[1:]
    return pl.pallas_call(
        kernel,
        out_shape=[jax.ShapeDtypeStruct((n,) + size, jnp.float32) for n in pieces],
        in_specs=[vmem] * len(operands),
        out_specs=[vmem] * len(pieces),
        compiler_params=pltpu.CompilerParams(vmem_limit_bytes=32 * MIB),
        name=name,
    )(*operands)


def first_kernel(n_high, kept, got, to_y, to_l, *to_h):
    begin = 0
    for out in (to_y, to_l) + to_h:
        rows = slice(begin, begin + out.shape[0])
        out[...] = kept[rows] + got[rows]
        begin += out.shape[0]


def second_kernel(n_high, kept, got, got_y, got_l, *rest):
    got_h, (own, to_y, to_l, *to_h) = rest[: n_high - 1], rest[n_high - 1 :]
    n = 2 * n_high

    def part_sum(begin, count, *arrivals):
        total = kept[begin : begin + count] + got[begin : begin + count]
        for array, at in arrivals:
            total += array[at : at + count]
        return total

    ylh = part_sum(0, n, (got_y, 0))
    yhl = part_sum(n, n, (got_y, n))
    lyh = part_sum(2 * n, n, (got_l, 0))
    hyl = part_sum(3 * n, 4, *[(array, 0) for array in got_h])
    to_l[...] = ylh[n_high:]
    for i, out in enumerate(to_h):
        out[...] = yhl[2 * (i + 1) : 2 * (i + 2)]
    to_y[:n_high] = lyh[n_high:]
    to_y[n_high:] = hyl[2:]
    own[:n_high] = ylh[:n_high]
    own[n_high : n_high + 2] = yhl[:2]
    own[n_high + 2 : 2 * n_high + 2] = lyh[:n_high]
    own[2 * n_high + 2 :] = hyl[:2]


def third_kernel(n_high, before, got_y, got_l, *rest):
    got_h, (own, to_l, *to_h) = rest[: n_high - 1], rest[n_high - 1 :]
    ylh = before[:n_high] + got_l[...]
    yhl = before[n_high : n_high + 2]
    for array in got_h:
        yhl += array[...]
    lyh = before[n_high + 2 : 2 * n_high + 2] + got_y[:n_high]
    hyl = before[2 * n_high + 2 :] + got_y[n_high:]
    for part, value in enumerate((ylh, yhl, lyh, hyl)):
        own[part] = value[0]
    to_l[0] = yhl[1]
    to_l[1] = hyl[1]
    for i, out in enumerate(to_h):
        out[0] = ylh[i + 1]
        out[1] = lyh[i + 1]


def last_kernel(n_high, before, got_l, *rest):
    got_h, (own,) = rest[: n_high - 1], rest[n_high - 1 :]
    for part, (arrivals, at) in enumerate(((got_h, 0), ((got_l,), 0), (got_h, 1), ((got_l,), 1))):
        total = before[part]
        for array in arrivals:
            total += array[at]
        own[part] = total


def bank_kernel(place, own, other, bank, out):
    bank_size, n_z, n_cell = bank.shape
    n_half = out.shape[0] // 2
    group = 2 * SUB

    def apply(halves):
        for c in range(n_cell // LANES):
            cols = slice(c * LANES, (c + 1) * LANES)

            @pl.loop(0, n_z // group)
            def _(g):
                rows = pl.ds(pl.multiple_of(g * group, group), group)
                weights = [bank[t, rows, cols] for t in range(bank_size)]
                for b in range(2 * n_half):
                    total = None
                    for t in range(bank_size):
                        value = weights[t] * halves[b // n_half][b % n_half, t, c : c + 1, :]
                        total = value if total is None else total + value
                    out[b, rows, cols] = total

    @pl.when(place[0] == 0)
    def _():
        apply((own, other))

    @pl.when(place[0] == 1)
    def _():
        apply((other, own))


def apply_bank(place, own, other, weight_bank):
    bank_size, n_z, n_cell = weight_bank.shape
    vmem = pl.BlockSpec(memory_space=pltpu.VMEM)
    own, other = [array.reshape(NB_DEV // 2, bank_size, SUB, LANES) for array in (own, other)]
    return pl.pallas_call(
        bank_kernel,
        out_shape=jax.ShapeDtypeStruct((NB_DEV, n_z, n_cell), jnp.float32),
        in_specs=[pl.BlockSpec(memory_space=pltpu.SMEM)] + [vmem] * 3,
        out_specs=vmem,
        compiler_params=pltpu.CompilerParams(vmem_limit_bytes=32 * MIB),
        name="apply_bank",
    )(place, own, other, weight_bank)


def body(
    projections, images, transfer, pose_weights, pose_of, pose_blocks, pose_tiles, weight_bank
):
    bank_size = weight_bank.shape[0]
    n_blk = lax.axis_size("blk")
    n_high = n_blk // 4
    here = lax.axis_index("blk")
    place = jnp.stack([lax.axis_index("rep"), here & 1, (here >> 1) & 1, here >> 2]).astype(jnp.int32)
    sent_away, kept_away, sent_stay, kept_stay = accumulate(
        projections, images, transfer, pose_weights, pose_of, pose_blocks, pose_tiles,
        bank_size, n_blk, place,
    )

    def over_rep(array):
        return lax.ppermute(array, "rep", [(0, 1), (1, 0)])

    def over_blk(array, bits):
        return lax.ppermute(array, "blk", [(i, i ^ bits) for i in range(n_blk)])

    def over_h(arrays):
        return [over_blk(array, 4 * (i + 1)) for i, array in enumerate(arrays)]

    def step(kernel, name, pieces, *operands):
        return in_vmem(functools.partial(kernel, n_high), name, pieces, *operands)

    n_h = n_high - 1
    got_away, got_stay = over_rep(sent_away), over_rep(sent_stay)
    to_y, to_l, *to_h = step(first_kernel, "first", [4 * n_high, 2 * n_high] + [4] * n_h, kept_away, got_away)
    got_h, got_y, got_l = over_h(to_h), over_blk(to_y, 1), over_blk(to_l, 2)
    own, to_y, to_l, *to_h = step(
        second_kernel, "second", [2 * n_high + 4, n_high + 2, n_high] + [2] * n_h,
        kept_stay, got_stay, got_y, got_l, *got_h,
    )
    got_h, got_y, got_l = over_h(to_h), over_blk(to_y, 1), over_blk(to_l, 2)
    own, to_l, *to_h = step(third_kernel, "third", [4, 2] + [2] * n_h, own, got_y, got_l, *got_h)
    got_h, got_l = over_h(to_h), over_blk(to_l, 2)
    (own,) = step(last_kernel, "last", [4], own, got_l, *got_h)
    return apply_bank(place, own, over_rep(own), weight_bank)


def solution(mesh):
    placed = (
        P(("groups", "blk", "rep"), None, None, None),
        P(("groups", "blk", "rep"), None, None),
        P(("groups", "blk", "rep"), None, None),
        P(("groups", "blk", "rep"), None),
        P(("groups", "blk", "rep"), None),
        P("groups", None),
        P("groups", None),
        P(),
    )
    return jax.shard_map(
        body,
        mesh=mesh,
        in_specs=placed,
        out_specs=P(("groups", "blk"), None, None),
        check_vma=False,
    )
```

```python
import functools

import jax
import jax.numpy as jnp
from jax import lax
from jax.experimental import pallas as pl
from jax.experimental.pallas import tpu as pltpu
from jax.sharding import PartitionSpec as P

NB_DEV = 8
LANES = 128
SUB = 8
MIB = 1 << 20
UNROLL = 12
ORDERS = ("ylh", "yhl", "lyh", "hyl")
N_BUF = 4


def position():
    here = lax.axis_index("blk")
    return lax.axis_index("rep"), here & 1, (here >> 1) & 1, here >> 2


def accumulate_kernel(
    bank_size, n_owner, n_acc,
    proj_hbm, img_hbm, tra_hbm, w_hbm, pose_hbm, blocks_hbm, tiles_hbm,
    sent_away, kept_away, sent_stay, kept_stay,
    proj, weight, pose, blocks, tiles, idx_v, idx_s, square, cross,
    *rest,
):
    parts, accs = rest[:N_BUF], rest[N_BUF : N_BUF + n_acc]
    proj_sem, small_sem, table_sem, idx_sem = rest[N_BUF + n_acc :]
    n_pose, n_part = pose.shape
    n_tile, n_table = blocks.shape
    n_row = accs[0].shape[0]
    tile_rows = SUB * SUB
    part_rows = n_tile * tile_rows

    table_copies = [
        pltpu.make_async_copy(src, dst, table_sem.at[i])
        for i, (src, dst) in enumerate(((pose_hbm, pose), (blocks_hbm, blocks), (tiles_hbm, tiles)))
    ]
    n_late = n_part // 4
    n_small = img_hbm.shape[0]
    img_first, tra_first = proj.shape[0] - n_small, proj.shape[0] - 2 * n_small
    img, tra = proj.at[pl.ds(img_first, n_small), :], proj.at[pl.ds(tra_first, n_small), :]
    small_copies = [
        pltpu.make_async_copy(img_hbm, img, small_sem.at[0]),
        pltpu.make_async_copy(tra_hbm, tra, small_sem.at[1]),
        pltpu.make_async_copy(w_hbm, weight, small_sem.at[2]),
    ]
    for copy in table_copies + small_copies:
        copy.start()

    def proj_copy(p):
        rows = pl.ds(pl.multiple_of(p * part_rows, part_rows), part_rows)
        return pltpu.make_async_copy(proj_hbm.at[rows, :], proj.at[rows, :], proj_sem.at[p])

    for p in range(n_part - n_late):
        proj_copy(p).start()

    zero = jnp.zeros((16 * SUB, LANES), jnp.float32)

    def clear(half):
        @pl.loop(0, n_row // (32 * SUB))
        def _(i):
            rows = pl.ds(pl.multiple_of(half * (n_row // 2) + i * (16 * SUB), 16 * SUB), 16 * SUB)
            for acc in accs:
                acc[rows, :] = zero

    clear(0)
    for copy in table_copies:
        copy.wait()
    lane = lax.broadcasted_iota(jnp.int32, (n_pose, n_table), 1)
    chosen = jnp.concatenate(
        [(pose[:, p : p + 1] == lane).astype(jnp.float32) for p in range(n_part)], axis=0
    ).astype(jnp.bfloat16)

    def look_up(table):
        return lax.dot_general(
            table[...].astype(jnp.float32).astype(jnp.bfloat16), chosen,
            (((1,), (1,)), ((), ())), preferred_element_type=jnp.float32,
        )

    idx_v[...] = ((look_up(blocks) * bank_size + look_up(tiles)) * SUB).astype(jnp.int32)
    idx_copy = pltpu.make_async_copy(idx_v, idx_s, idx_sem)
    idx_copy.start()
    clear(1)

    for copy in small_copies:
        copy.wait()
    @pl.loop(0, square.shape[0] // tile_rows)
    def _(i):
        rows = pl.ds(pl.multiple_of(i * tile_rows, tile_rows), tile_rows)
        t = proj[pl.ds(pl.multiple_of(tra_first + i * tile_rows, tile_rows), tile_rows), :].astype(jnp.float32)
        x = proj[pl.ds(pl.multiple_of(img_first + i * tile_rows, tile_rows), tile_rows), :].astype(jnp.float32)
        square[rows, :] = t * t
        cross[rows, :] = t * x

    for p in range(n_part - n_late, n_part):
        proj_copy(p).start()

    def stage(unit, part):
        first = pl.multiple_of(unit * tile_rows, tile_rows)
        part[...] = proj[pl.ds(first, tile_rows), :].astype(jnp.float32)

    def terms(p, j, part, weights):
        cell = pl.ds((j * (n_part // SUB) + p // SUB) * tile_rows + p % SUB, SUB, stride=SUB)
        tt, ti = square[cell, :], cross[cell, :]
        return [(tt * part[pl.ds(k, SUB, stride=SUB), :] - ti) * weights[k] for k in range(n_pose)]

    def add_rows(p, j, values):
        for first in range(0, n_pose, n_acc):
            group = range(first, first + n_acc)
            rows = [pl.ds(pl.multiple_of(idx_s[j, p * n_pose + k], SUB), SUB) for k in group]
            old = [accs[i][rows[i], :] for i in range(n_acc)]
            for i, k in enumerate(group):
                accs[i][rows[i], :] = old[i] + values[k]

    idx_copy.wait()
    n_buf = len(parts)

    @pl.loop(0, n_part)
    def _(p):
        proj_copy(p).wait()
        weights = [jnp.full((SUB, LANES), weight[k, p], jnp.float32) for k in range(n_pose)]
        base = p * n_tile
        stage(base, parts[0])
        stage(base + 1, parts[1])

        @pl.loop(0, n_tile, step=UNROLL, init_carry=tuple(terms(p, 0, parts[0], weights)))
        def _(j, values):
            for u in range(UNROLL):
                ahead = j + u + 2
                stage(base + (ahead if u + 2 < UNROLL else jnp.minimum(ahead, n_tile - 1)), parts[(u + 2) % n_buf])
                following = j + u + 1
                later = terms(
                    p, following if u + 1 < UNROLL else jnp.minimum(following, n_tile - 1),
                    parts[(u + 1) % n_buf], weights,
                )
                add_rows(p, j + u, values)
                values = later
            return tuple(values)

    rep, near, low, high = position()
    half_rows = n_row // (n_owner * 2)
    size = half_rows // len(ORDERS)
    sizes = {"y": 2, "l": 2, "h": n_owner // 4}

    def finish(out, place_of, part, owner, half):
        first = pl.multiple_of((owner * 2 + half) * half_rows + part * size, size)
        rows = pl.ds(first, size)
        total = accs[0][rows, :]
        for acc in accs[1:]:
            total += acc[rows, :]
        out[place_of] = total

    def pieces(sent, kept, begin, part, firsts):
        order = ORDERS[part]
        inner = sizes[order[1]] * sizes[order[2]]

        @pl.loop(0, len(firsts) * inner)
        def _(i):
            off = {order[0]: firsts[0] + i // inner}
            off[order[1]] = i % inner // sizes[order[2]]
            off[order[2]] = i % sizes[order[2]]
            owner = ((high ^ off["h"]) * 2 + (low ^ off["l"])) * 2 + (near ^ off["y"])
            finish(sent, begin + i, part, owner, 1 - rep)
            finish(kept, begin + i, part, owner, rep)

        return begin + len(firsts) * inner

    for sent, kept, away in ((sent_away, kept_away, True), (sent_stay, kept_stay, False)):
        begin = 0
        for part, order in enumerate(ORDERS):
            begin = pieces(sent, kept, begin, part, range(1, sizes[order[0]]) if away else range(1))


def tiles_in_order(array):
    lead = array.shape[:-2]
    rows, cells = array.shape[-2:]
    array = array.reshape(lead + (rows // SUB, SUB, cells // LANES, LANES))
    return jnp.swapaxes(array, -3, -2).reshape(-1, LANES)


def accumulate(
    projections, images, transfer, pose_weights, pose_of, pose_blocks, pose_tiles,
    bank_size, n_owner,
):
    n_part, n_pose, n_tile, n_cell = projections.shape
    assert n_cell == SUB * LANES and n_pose == SUB and n_part % SUB == 0 and n_tile % UNROLL == 0 and UNROLL % N_BUF == 0
    n_row = n_owner * NB_DEV * bank_size * SUB
    n_acc = 8 if n_row * LANES * 4 <= 4 * MIB else 2
    projections = tiles_in_order(jnp.transpose(projections, (0, 2, 1, 3)))
    images = tiles_in_order(jnp.transpose(images, (1, 0, 2)))
    transfer = tiles_in_order(jnp.transpose(transfer, (1, 0, 2)))
    stay = functools.partial(pltpu.with_memory_space_constraint, memory_space=pltpu.HBM)
    hbm = pl.BlockSpec(memory_space=pltpu.HBM)
    vmem = pl.BlockSpec(memory_space=pltpu.VMEM)
    n_high = n_owner // 4
    size = n_row // (n_owner * 2 * len(ORDERS))

    def out(pieces):
        return jax.ShapeDtypeStruct((pieces, size, LANES), jnp.float32)

    return pl.pallas_call(
        functools.partial(accumulate_kernel, bank_size, n_owner, n_acc),
        out_shape=[out(6 * n_high + 4 * (n_high - 1))] * 2 + [out(6 * n_high + 4)] * 2,
        in_specs=[hbm] * 7,
        out_specs=[vmem] * 4,
        scratch_shapes=[
            pltpu.VMEM(projections.shape, jnp.bfloat16),
            pltpu.SMEM((n_pose, n_part), jnp.float32),
            pltpu.VMEM((n_pose, n_part), jnp.int32),
            pltpu.VMEM(pose_blocks.shape[::-1], jnp.int32),
            pltpu.VMEM(pose_tiles.shape[::-1], jnp.int32),
            pltpu.VMEM((n_tile, n_part * n_pose), jnp.int32),
            pltpu.SMEM((n_tile, n_part * n_pose), jnp.int32),
            pltpu.VMEM(transfer.shape, jnp.float32),
            pltpu.VMEM(transfer.shape, jnp.float32),
        ]
        + [pltpu.VMEM((n_pose * SUB, LANES), jnp.float32)] * N_BUF
        + [pltpu.VMEM((n_row, LANES), jnp.float32)] * n_acc
        + [
            pltpu.SemaphoreType.DMA((n_part,)),
            pltpu.SemaphoreType.DMA((3,)),
            pltpu.SemaphoreType.DMA((3,)),
            pltpu.SemaphoreType.DMA,
        ],
        compiler_params=pltpu.CompilerParams(vmem_limit_bytes=(47 if n_acc == 8 else 56) * MIB),
        name="accumulate",
    )(
        stay(projections), stay(images), stay(transfer),
        stay(pose_weights.T), stay(pose_of.T), stay(pose_blocks.T), stay(pose_tiles.T),
    )


def in_vmem(kernel, name, pieces, *operands):
    vmem = pl.BlockSpec(memory_space=pltpu.VMEM)
    size = operands[0].shape[1:]
    return pl.pallas_call(
        kernel,
        out_shape=[jax.ShapeDtypeStruct((n,) + size, jnp.float32) for n in pieces],
        in_specs=[vmem] * len(operands),
        out_specs=[vmem] * len(pieces),
        compiler_params=pltpu.CompilerParams(vmem_limit_bytes=32 * MIB),
        name=name,
    )(*operands)


def first_kernel(n_high, kept, got, to_y, to_l, *to_h):
    begin = 0
    for out in (to_y, to_l) + to_h:
        rows = slice(begin, begin + out.shape[0])
        out[...] = kept[rows] + got[rows]
        begin += out.shape[0]


def second_kernel(n_high, kept, got, got_y, got_l, *rest):
    got_h, (own, to_y, to_l, *to_h) = rest[: n_high - 1], rest[n_high - 1 :]
    n = 2 * n_high

    def part_sum(begin, count, *arrivals):
        total = kept[begin : begin + count] + got[begin : begin + count]
        for array, at in arrivals:
            total += array[at : at + count]
        return total

    ylh = part_sum(0, n, (got_y, 0))
    yhl = part_sum(n, n, (got_y, n))
    lyh = part_sum(2 * n, n, (got_l, 0))
    hyl = part_sum(3 * n, 4, *[(array, 0) for array in got_h])
    to_l[...] = ylh[n_high:]
    for i, out in enumerate(to_h):
        out[...] = yhl[2 * (i + 1) : 2 * (i + 2)]
    to_y[:n_high] = lyh[n_high:]
    to_y[n_high:] = hyl[2:]
    own[:n_high] = ylh[:n_high]
    own[n_high : n_high + 2] = yhl[:2]
    own[n_high + 2 : 2 * n_high + 2] = lyh[:n_high]
    own[2 * n_high + 2 :] = hyl[:2]


def third_kernel(n_high, before, got_y, got_l, *rest):
    got_h, (own, to_l, *to_h) = rest[: n_high - 1], rest[n_high - 1 :]
    ylh = before[:n_high] + got_l[...]
    yhl = before[n_high : n_high + 2]
    for array in got_h:
        yhl += array[...]
    lyh = before[n_high + 2 : 2 * n_high + 2] + got_y[:n_high]
    hyl = before[2 * n_high + 2 :] + got_y[n_high:]
    for part, value in enumerate((ylh, yhl, lyh, hyl)):
        own[part] = value[0]
    to_l[0] = yhl[1]
    to_l[1] = hyl[1]
    for i, out in enumerate(to_h):
        out[0] = ylh[i + 1]
        out[1] = lyh[i + 1]


def last_kernel(n_high, before, got_l, *rest):
    got_h, (own,) = rest[: n_high - 1], rest[n_high - 1 :]
    for part, (arrivals, at) in enumerate(((got_h, 0), ((got_l,), 0), (got_h, 1), ((got_l,), 1))):
        total = before[part]
        for array in arrivals:
            total += array[at]
        own[part] = total


def bank_kernel(own, other, bank, out):
    bank_size, n_z, n_cell = bank.shape
    n_half = out.shape[0] // 2
    group = 2 * SUB

    def apply(halves):
        for c in range(n_cell // LANES):
            cols = slice(c * LANES, (c + 1) * LANES)

            @pl.loop(0, n_z // group)
            def _(g):
                rows = pl.ds(pl.multiple_of(g * group, group), group)
                weights = [bank[t, rows, cols] for t in range(bank_size)]
                for b in range(2 * n_half):
                    total = None
                    for t in range(bank_size):
                        value = weights[t] * halves[b // n_half][b % n_half, t, c : c + 1, :]
                        total = value if total is None else total + value
                    out[b, rows, cols] = total

    rep = position()[0]

    @pl.when(rep == 0)
    def _():
        apply((own, other))

    @pl.when(rep == 1)
    def _():
        apply((other, own))


def apply_bank(own, other, weight_bank):
    bank_size, n_z, n_cell = weight_bank.shape
    vmem = pl.BlockSpec(memory_space=pltpu.VMEM)
    own, other = [array.reshape(NB_DEV // 2, bank_size, SUB, LANES) for array in (own, other)]
    return pl.pallas_call(
        bank_kernel,
        out_shape=jax.ShapeDtypeStruct((NB_DEV, n_z, n_cell), jnp.float32),
        in_specs=[vmem] * 3,
        out_specs=vmem,
        compiler_params=pltpu.CompilerParams(vmem_limit_bytes=32 * MIB),
        name="apply_bank",
    )(own, other, weight_bank)


def body(
    projections, images, transfer, pose_weights, pose_of, pose_blocks, pose_tiles, weight_bank
):
    bank_size = weight_bank.shape[0]
    n_blk = lax.axis_size("blk")
    n_high = n_blk // 4
    sent_away, kept_away, sent_stay, kept_stay = accumulate(
        projections, images, transfer, pose_weights, pose_of, pose_blocks, pose_tiles,
        bank_size, n_blk,
    )

    def over_rep(array):
        return lax.ppermute(array, "rep", [(0, 1), (1, 0)])

    def over_blk(array, bits):
        return lax.ppermute(array, "blk", [(i, i ^ bits) for i in range(n_blk)])

    def over_h(arrays):
        return [over_blk(array, 4 * (i + 1)) for i, array in enumerate(arrays)]

    def step(kernel, name, pieces, *operands):
        return in_vmem(functools.partial(kernel, n_high), name, pieces, *operands)

    n_h = n_high - 1
    got_away, got_stay = over_rep(sent_away), over_rep(sent_stay)
    to_y, to_l, *to_h = step(first_kernel, "first", [4 * n_high, 2 * n_high] + [4] * n_h, kept_away, got_away)
    got_h, got_y, got_l = over_h(to_h), over_blk(to_y, 1), over_blk(to_l, 2)
    own, to_y, to_l, *to_h = step(
        second_kernel, "second", [2 * n_high + 4, n_high + 2, n_high] + [2] * n_h,
        kept_stay, got_stay, got_y, got_l, *got_h,
    )
    got_h, got_y, got_l = over_h(to_h), over_blk(to_y, 1), over_blk(to_l, 2)
    own, to_l, *to_h = step(third_kernel, "third", [4, 2] + [2] * n_h, own, got_y, got_l, *got_h)
    got_h, got_l = over_h(to_h), over_blk(to_l, 2)
    (own,) = step(last_kernel, "last", [4], own, got_l, *got_h)
    return apply_bank(own, over_rep(own), weight_bank)


def solution(mesh):
    placed = (
        P(("groups", "blk", "rep"), None, None, None),
        P(("groups", "blk", "rep"), None, None),
        P(("groups", "blk", "rep"), None, None),
        P(("groups", "blk", "rep"), None),
        P(("groups", "blk", "rep"), None),
        P("groups", None),
        P("groups", None),
        P(),
    )
    return jax.shard_map(
        body,
        mesh=mesh,
        in_specs=placed,
        out_specs=P(("groups", "blk"), None, None),
        check_vma=False,
    )
```

```python
import functools

import jax
import jax.numpy as jnp
from jax import lax
from jax.experimental import pallas as pl
from jax.experimental.pallas import tpu as pltpu
from jax.sharding import PartitionSpec as P

NB_DEV = 8
LANES = 128
SUB = 8
MIB = 1 << 20
UNROLL = 12
ORDERS = ("ylh", "yhl", "lyh", "hyl")
PART_ROWS = (24, 10, 18, 12)


def position():
    here = lax.axis_index("blk")
    return lax.axis_index("rep"), here & 1, (here >> 1) & 1, here >> 2


def accumulate_kernel(
    bank_size, n_owner, n_acc,
    proj_hbm, img_hbm, tra_hbm, w_hbm, pose_hbm, blocks_hbm, tiles_hbm,
    sent_y, kept_y, sent_z, kept_z, sent_stay, kept_stay,
    proj, weight, pose, blocks, tiles, idx_v, idx_s, square, cross,
    *rest,
):
    accs = rest[:n_acc]
    proj_sem, small_sem, table_sem, idx_sem = rest[n_acc:]
    n_pose, n_part = pose.shape
    n_tile, n_table = blocks.shape
    n_row = accs[0].shape[0]
    tile_rows = SUB * SUB
    part_rows = n_tile * tile_rows

    table_copies = [
        pltpu.make_async_copy(src, dst, table_sem.at[i])
        for i, (src, dst) in enumerate(((pose_hbm, pose), (blocks_hbm, blocks), (tiles_hbm, tiles)))
    ]
    n_late = n_part // 4
    n_small = img_hbm.shape[0]
    img_first, tra_first = proj.shape[0] - n_small, proj.shape[0] - 2 * n_small
    img, tra = proj.at[pl.ds(img_first, n_small), :], proj.at[pl.ds(tra_first, n_small), :]
    small_copies = [
        pltpu.make_async_copy(img_hbm, img, small_sem.at[0]),
        pltpu.make_async_copy(tra_hbm, tra, small_sem.at[1]),
        pltpu.make_async_copy(w_hbm, weight, small_sem.at[2]),
    ]
    for copy in table_copies + small_copies:
        copy.start()

    def proj_copy(p):
        rows = pl.ds(pl.multiple_of(p * part_rows, part_rows), part_rows)
        return pltpu.make_async_copy(proj_hbm.at[rows, :], proj.at[rows, :], proj_sem.at[p])

    for p in range(n_part - n_late):
        proj_copy(p).start()

    zero = jnp.zeros((16 * SUB, LANES), jnp.float32)

    def clear(half):
        @pl.loop(0, n_row // (32 * SUB))
        def _(i):
            rows = pl.ds(pl.multiple_of(half * (n_row // 2) + i * (16 * SUB), 16 * SUB), 16 * SUB)
            for acc in accs:
                acc[rows, :] = zero

    clear(0)
    for copy in table_copies:
        copy.wait()
    lane = lax.broadcasted_iota(jnp.int32, (n_pose, n_table), 1)
    chosen = jnp.concatenate(
        [(pose[:, p : p + 1] == lane).astype(jnp.float32) for p in range(n_part)], axis=0
    ).astype(jnp.bfloat16)

    def look_up(table):
        return lax.dot_general(
            table[...].astype(jnp.float32).astype(jnp.bfloat16), chosen,
            (((1,), (1,)), ((), ())), preferred_element_type=jnp.float32,
        )

    idx_v[...] = ((look_up(blocks) * bank_size + look_up(tiles)) * SUB).astype(jnp.int32)
    idx_copy = pltpu.make_async_copy(idx_v, idx_s, idx_sem)
    idx_copy.start()
    clear(1)

    for copy in small_copies:
        copy.wait()
    @pl.loop(0, square.shape[0] // tile_rows)
    def _(i):
        rows = pl.ds(pl.multiple_of(i * tile_rows, tile_rows), tile_rows)
        t = proj[pl.ds(pl.multiple_of(tra_first + i * tile_rows, tile_rows), tile_rows), :].astype(jnp.float32)
        x = proj[pl.ds(pl.multiple_of(img_first + i * tile_rows, tile_rows), tile_rows), :].astype(jnp.float32)
        square[rows, :] = t * t
        cross[rows, :] = t * x

    for p in range(n_part - n_late, n_part):
        proj_copy(p).start()

    sublane = lax.broadcasted_iota(jnp.int32, (SUB, LANES), 0)
    bits = [(sublane & (1 << t)) != 0 for t in range(3)]

    def terms(p, j, weights):
        first = (p * n_tile + j) * tile_rows
        cells = []
        for c in range(0, SUB, 2):
            pair = proj[pl.ds(pl.multiple_of(first + c * SUB, 2 * SUB), 2 * SUB), :].astype(jnp.float32)
            cells += [pair[:SUB], pair[SUB:]]
        cells = [pltpu.roll(x, c, 0) if c else x for c, x in enumerate(cells)]
        for t, bit in enumerate(bits):
            cells = [jnp.where(bit, cells[(i + (1 << t)) % SUB], cells[i]) for i in range(SUB)]
        cells = [pltpu.roll(cells[-k % SUB], SUB - k, 0) if k else cells[0] for k in range(n_pose)]
        cell = pl.ds((j * (n_part // SUB) + p // SUB) * tile_rows + p % SUB, SUB, stride=SUB)
        tt, ti = square[cell, :], cross[cell, :]
        return [(tt * cells[k] - ti) * weights[k] for k in range(n_pose)]

    def add_rows(p, j, values):
        for first in range(0, n_pose, n_acc):
            group = range(first, first + n_acc)
            rows = [pl.ds(pl.multiple_of(idx_s[j, p * n_pose + k], SUB), SUB) for k in group]
            old = [accs[i][rows[i], :] for i in range(n_acc)]
            for i, k in enumerate(group):
                accs[i][rows[i], :] = old[i] + values[k]

    idx_copy.wait()

    @pl.loop(0, n_part)
    def _(p):
        proj_copy(p).wait()
        weights = [jnp.full((SUB, LANES), weight[k, p], jnp.float32) for k in range(n_pose)]

        @pl.loop(0, n_tile, step=UNROLL, init_carry=tuple(terms(p, 0, weights)))
        def _(j, values):
            for u in range(UNROLL):
                following = j + u + 1
                later = terms(p, following if u + 1 < UNROLL else jnp.minimum(following, n_tile - 1), weights)
                add_rows(p, j + u, values)
                values = later
            return tuple(values)

    rep, near, low, high = position()
    half_rows = n_row // (n_owner * 2)
    sizes = {"y": 2, "l": 2, "h": n_owner // 4}

    def finish(out, at, first, size):
        first = pl.multiple_of(first, SUB)
        total = accs[0][pl.ds(first, size), :]
        for acc in accs[1:]:
            total += acc[pl.ds(first, size), :]
        out[pl.ds(pl.multiple_of(at, SUB), size), :] = total

    def pieces(sent, kept, begin, part, firsts):
        order = ORDERS[part]
        inner = sizes[order[1]] * sizes[order[2]]
        size = PART_ROWS[part] * SUB
        within = sum(PART_ROWS[:part]) * SUB

        @pl.loop(0, len(firsts) * inner)
        def _(i):
            off = {order[0]: firsts[0] + i // inner}
            off[order[1]] = i % inner // sizes[order[2]]
            off[order[2]] = i % sizes[order[2]]
            owner = ((high ^ off["h"]) * 2 + (low ^ off["l"])) * 2 + (near ^ off["y"])
            finish(sent, begin + i * size, (owner * 2 + 1 - rep) * half_rows + within, size)
            finish(kept, begin + i * size, (owner * 2 + rep) * half_rows + within, size)

        return begin + len(firsts) * inner * size

    away_y = pieces(sent_y, kept_y, 0, 0, range(1, 2))
    pieces(sent_y, kept_y, away_y, 1, range(1, 2))
    away_z = pieces(sent_z, kept_z, 0, 2, range(1, 2))
    pieces(sent_z, kept_z, away_z, 3, range(1, sizes["h"]))
    begin = 0
    for part in range(len(ORDERS)):
        begin = pieces(sent_stay, kept_stay, begin, part, range(1))


def tiles_in_order(array):
    lead = array.shape[:-2]
    rows, cells = array.shape[-2:]
    array = array.reshape(lead + (rows // SUB, SUB, cells // LANES, LANES))
    return jnp.swapaxes(array, -3, -2).reshape(-1, LANES)


def accumulate(
    projections, images, transfer, pose_weights, pose_of, pose_blocks, pose_tiles,
    bank_size, n_owner,
):
    n_part, n_pose, n_tile, n_cell = projections.shape
    assert n_cell == SUB * LANES and n_pose == SUB and n_part % SUB == 0 and n_tile % UNROLL == 0
    n_row = n_owner * NB_DEV * bank_size * SUB
    n_acc = 4 if n_row * LANES * 4 <= 4 * MIB else 2
    projections = tiles_in_order(jnp.transpose(projections, (0, 2, 1, 3)))
    images = tiles_in_order(jnp.transpose(images, (1, 0, 2)))
    transfer = tiles_in_order(jnp.transpose(transfer, (1, 0, 2)))
    stay = functools.partial(pltpu.with_memory_space_constraint, memory_space=pltpu.HBM)
    hbm = pl.BlockSpec(memory_space=pltpu.HBM)
    vmem = pl.BlockSpec(memory_space=pltpu.VMEM)
    n_high = n_owner // 4
    a, d, b, e = (rows * SUB for rows in PART_ROWS)
    assert sum(PART_ROWS) == NB_DEV // 2 * bank_size

    def out(rows):
        return [jax.ShapeDtypeStruct((rows, LANES), jnp.float32)] * 2

    return pl.pallas_call(
        functools.partial(accumulate_kernel, bank_size, n_owner, n_acc),
        out_shape=out(2 * n_high * (a + d))
        + out(2 * n_high * b + 4 * (n_high - 1) * e)
        + out(2 * n_high * (a + d + b) + 4 * e),
        in_specs=[hbm] * 7,
        out_specs=[vmem] * 6,
        scratch_shapes=[
            pltpu.VMEM(projections.shape, jnp.bfloat16),
            pltpu.SMEM((n_pose, n_part), jnp.float32),
            pltpu.VMEM((n_pose, n_part), jnp.int32),
            pltpu.VMEM(pose_blocks.shape[::-1], jnp.int32),
            pltpu.VMEM(pose_tiles.shape[::-1], jnp.int32),
            pltpu.VMEM((n_tile, n_part * n_pose), jnp.int32),
            pltpu.SMEM((n_tile, n_part * n_pose), jnp.int32),
            pltpu.VMEM(transfer.shape, jnp.float32),
            pltpu.VMEM(transfer.shape, jnp.float32),
        ]
        + [pltpu.VMEM((n_row, LANES), jnp.float32)] * n_acc
        + [
            pltpu.SemaphoreType.DMA((n_part,)),
            pltpu.SemaphoreType.DMA((3,)),
            pltpu.SemaphoreType.DMA((3,)),
            pltpu.SemaphoreType.DMA,
        ],
        compiler_params=pltpu.CompilerParams(vmem_limit_bytes=(40 if n_acc == 4 else 56) * MIB),
        name="accumulate",
    )(
        stay(projections), stay(images), stay(transfer),
        stay(pose_weights.T), stay(pose_of.T), stay(pose_blocks.T), stay(pose_tiles.T),
    )


def in_vmem(kernel, name, rows, *operands):
    vmem = pl.BlockSpec(memory_space=pltpu.VMEM)
    return pl.pallas_call(
        kernel,
        out_shape=[jax.ShapeDtypeStruct((n, LANES), jnp.float32) for n in rows],
        in_specs=[vmem] * len(operands),
        out_specs=[vmem] * len(rows),
        compiler_params=pltpu.CompilerParams(vmem_limit_bytes=32 * MIB),
        name=name,
    )(*operands)


def first_kernel(kept, got, *to):
    begin = 0
    for out in to:
        rows = slice(begin, begin + out.shape[0])
        out[...] = kept[rows, :] + got[rows, :]
        begin += out.shape[0]


def second_kernel(n_high, kept, got, got_y, got_l, *rest):
    got_h, (own_a, own_d, own_b, own_e, to_y, to_l, *to_h) = rest[: n_high - 1], rest[n_high - 1 :]
    a, d, b, e = (rows * SUB for rows in PART_ROWS)

    def put(out, at, begin, size, *arrivals):
        total = kept[begin : begin + size, :] + got[begin : begin + size, :]
        for array, first in arrivals:
            total += array[first : first + size, :]
        out[at : at + size, :] = total

    n = n_high * a
    put(own_a, 0, 0, n, (got_y, 0))
    put(to_l, 0, n, n, (got_y, n))
    begin, y_begin = 2 * n, 2 * n
    put(own_d, 0, begin, 2 * d, (got_y, y_begin))
    for i, out in enumerate(to_h):
        put(out, 0, begin + 2 * d * (i + 1), 2 * d, (got_y, y_begin + 2 * d * (i + 1)))
    begin, n = begin + 2 * n_high * d, n_high * b
    put(own_b, 0, begin, n, (got_l, 0))
    put(to_y, 0, begin + n, n, (got_l, n))
    begin += 2 * n
    put(own_e, 0, begin, 2 * e, *[(array, 0) for array in got_h])
    put(to_y, n, begin + 2 * e, 2 * e, *[(array, 2 * e) for array in got_h])


def third_kernel(n_high, own_a, own_d, own_b, own_e, got_y, got_l, *rest):
    got_h, (own, to_l, *to_h) = rest[: n_high - 1], rest[n_high - 1 :]
    a, d, b, e = (rows * SUB for rows in PART_ROWS)

    def put(out, at, source, begin, size, *arrivals):
        total = source[begin : begin + size, :]
        for array, first in arrivals:
            total += array[first : first + size, :]
        out[at : at + size, :] = total

    put(own, 0, own_a, 0, a, (got_l, 0))
    put(own, a, own_d, 0, d, *[(array, 0) for array in got_h])
    put(own, a + d, own_b, 0, b, (got_y, 0))
    put(own, a + d + b, own_e, 0, e, (got_y, n_high * b))
    put(to_l, 0, own_d, d, d, *[(array, d) for array in got_h])
    put(to_l, d, own_e, e, e, (got_y, n_high * b + e))
    for i, out in enumerate(to_h):
        put(out, 0, own_a, (i + 1) * a, a, (got_l, (i + 1) * a))
        put(out, a, own_b, (i + 1) * b, b, (got_y, (i + 1) * b))


def last_kernel(before, got_l, *rest):
    got_h, (own,) = rest[:-1], rest[-1:]
    a, d, b, e = (rows * SUB for rows in PART_ROWS)
    for at, size, arrivals in (
        (0, a, [(array, 0) for array in got_h]),
        (a, d, [(got_l, 0)]),
        (a + d, b, [(array, a) for array in got_h]),
        (a + d + b, e, [(got_l, d)]),
    ):
        total = before[at : at + size, :]
        for array, first in arrivals:
            total += array[first : first + size, :]
        own[at : at + size, :] = total


def bank_kernel(own, other, bank, out):
    bank_size, n_z, n_cell = bank.shape
    n_half = out.shape[0] // 2
    group = 2 * SUB

    def apply(halves):
        for c in range(n_cell // LANES):
            cols = slice(c * LANES, (c + 1) * LANES)

            @pl.loop(0, n_z // group)
            def _(g):
                rows = pl.ds(pl.multiple_of(g * group, group), group)
                weights = [bank[t, rows, cols] for t in range(bank_size)]
                for b in range(2 * n_half):
                    total = None
                    for t in range(bank_size):
                        value = weights[t] * halves[b // n_half][b % n_half, t, c : c + 1, :]
                        total = value if total is None else total + value
                    out[b, rows, cols] = total

    rep = position()[0]

    @pl.when(rep == 0)
    def _():
        apply((own, other))

    @pl.when(rep == 1)
    def _():
        apply((other, own))


def apply_bank(own, other, weight_bank):
    bank_size, n_z, n_cell = weight_bank.shape
    vmem = pl.BlockSpec(memory_space=pltpu.VMEM)
    own, other = [array.reshape(NB_DEV // 2, bank_size, SUB, LANES) for array in (own, other)]
    return pl.pallas_call(
        bank_kernel,
        out_shape=jax.ShapeDtypeStruct((NB_DEV, n_z, n_cell), jnp.float32),
        in_specs=[vmem] * 3,
        out_specs=vmem,
        compiler_params=pltpu.CompilerParams(vmem_limit_bytes=32 * MIB),
        name="apply_bank",
    )(own, other, weight_bank)


def body(
    projections, images, transfer, pose_weights, pose_of, pose_blocks, pose_tiles, weight_bank
):
    bank_size = weight_bank.shape[0]
    n_blk = lax.axis_size("blk")
    n_high = n_blk // 4
    sent_y, kept_y, sent_z, kept_z, sent_stay, kept_stay = accumulate(
        projections, images, transfer, pose_weights, pose_of, pose_blocks, pose_tiles,
        bank_size, n_blk,
    )
    a, d, b, e = (rows * SUB for rows in PART_ROWS)

    def over_rep(array):
        return lax.ppermute(array, "rep", [(0, 1), (1, 0)])

    def over_blk(array, bits):
        return lax.ppermute(array, "blk", [(i, i ^ bits) for i in range(n_blk)])

    def over_h(arrays):
        return [over_blk(array, 4 * (i + 1)) for i, array in enumerate(arrays)]

    n_h = n_high - 1
    got_y, got_z, got_stay = over_rep(sent_y), over_rep(sent_z), over_rep(sent_stay)
    (to_y,) = in_vmem(first_kernel, "first_y", [kept_y.shape[0]], kept_y, got_y)
    got_y = over_blk(to_y, 1)
    to_l, *to_h = in_vmem(first_kernel, "first_z", [2 * n_high * b] + [4 * e] * n_h, kept_z, got_z)
    got_l, got_h = over_blk(to_l, 2), over_h(to_h)
    own_a, own_d, own_b, own_e, to_y, to_l, *to_h = in_vmem(
        functools.partial(second_kernel, n_high), "second",
        [n_high * a, 2 * d, n_high * b, 2 * e, n_high * b + 2 * e, n_high * a] + [2 * d] * n_h,
        kept_stay, got_stay, got_y, got_l, *got_h,
    )
    got_y, got_l, got_h = over_blk(to_y, 1), over_blk(to_l, 2), over_h(to_h)
    own, to_l, *to_h = in_vmem(
        functools.partial(third_kernel, n_high), "third", [a + d + b + e, d + e] + [a + b] * n_h,
        own_a, own_d, own_b, own_e, got_y, got_l, *got_h,
    )
    got_l, got_h = over_blk(to_l, 2), over_h(to_h)
    (own,) = in_vmem(last_kernel, "last", [a + d + b + e], own, got_l, *got_h)
    return apply_bank(own, over_rep(own), weight_bank)


def solution(mesh):
    placed = (
        P(("groups", "blk", "rep"), None, None, None),
        P(("groups", "blk", "rep"), None, None),
        P(("groups", "blk", "rep"), None, None),
        P(("groups", "blk", "rep"), None),
        P(("groups", "blk", "rep"), None),
        P("groups", None),
        P("groups", None),
        P(),
    )
    return jax.shard_map(
        body,
        mesh=mesh,
        in_specs=placed,
        out_specs=P(("groups", "blk"), None, None),
        check_vma=False,
    )
```

```python
import functools

import jax
import jax.numpy as jnp
from jax import lax
from jax.experimental import pallas as pl
from jax.experimental.pallas import tpu as pltpu
from jax.sharding import PartitionSpec as P

NB_DEV = 8
LANES = 128
SUB = 8
MIB = 1 << 20
UNROLL = 12
N_BUF = 2
ORDERS = ("ylh", "yhl", "lyh", "hyl")
PART_ROWS = (16, 16, 18, 14)


def position():
    here = lax.axis_index("blk")
    return lax.axis_index("rep"), here & 1, (here >> 1) & 1, here >> 2


def accumulate_kernel(
    bank_size, n_owner, n_acc,
    proj_hbm, img_hbm, tra_hbm, w_hbm, pose_hbm, blocks_hbm, tiles_hbm,
    sent_y, sent_z, *rest,
):
    accs, rest = rest[:n_acc], rest[n_acc:]
    proj, weight, pose, blocks, tiles, idx_v, idx_s, square, cross = rest[:9]
    parts = rest[9 : 9 + N_BUF]
    proj_sem, small_sem, table_sem, idx_sem = rest[9 + N_BUF :]
    n_pose, n_part = pose.shape
    n_tile, n_table = blocks.shape
    n_row = accs[0].shape[0]
    tile_rows = SUB * SUB
    part_rows = n_tile * tile_rows

    table_copies = [
        pltpu.make_async_copy(src, dst, table_sem.at[i])
        for i, (src, dst) in enumerate(((pose_hbm, pose), (blocks_hbm, blocks), (tiles_hbm, tiles)))
    ]
    n_late = n_part // 4
    n_small = img_hbm.shape[0]
    img_first, tra_first = proj.shape[0] - n_small, proj.shape[0] - 2 * n_small
    img, tra = proj.at[pl.ds(img_first, n_small), :], proj.at[pl.ds(tra_first, n_small), :]
    small_copies = [
        pltpu.make_async_copy(img_hbm, img, small_sem.at[0]),
        pltpu.make_async_copy(tra_hbm, tra, small_sem.at[1]),
        pltpu.make_async_copy(w_hbm, weight, small_sem.at[2]),
    ]
    for copy in table_copies + small_copies:
        copy.start()

    def proj_copy(p):
        rows = pl.ds(pl.multiple_of(p * part_rows, part_rows), part_rows)
        return pltpu.make_async_copy(proj_hbm.at[rows, :], proj.at[rows, :], proj_sem.at[p])

    for p in range(n_part - n_late):
        proj_copy(p).start()

    zero = jnp.zeros((16 * SUB, LANES), jnp.float32)

    def clear(half):
        @pl.loop(0, n_row // (32 * SUB))
        def _(i):
            rows = pl.ds(pl.multiple_of(half * (n_row // 2) + i * (16 * SUB), 16 * SUB), 16 * SUB)
            for acc in accs:
                acc[rows, :] = zero

    clear(0)
    for copy in table_copies:
        copy.wait()
    lane = lax.broadcasted_iota(jnp.int32, (n_pose, n_table), 1)
    chosen = jnp.concatenate(
        [(pose[:, p : p + 1] == lane).astype(jnp.float32) for p in range(n_part)], axis=0
    ).astype(jnp.bfloat16)

    def look_up(table):
        return lax.dot_general(
            table[...].astype(jnp.float32).astype(jnp.bfloat16), chosen,
            (((1,), (1,)), ((), ())), preferred_element_type=jnp.float32,
        )

    idx_v[...] = ((look_up(blocks) * bank_size + look_up(tiles)) * SUB).astype(jnp.int32)
    idx_copy = pltpu.make_async_copy(idx_v, idx_s, idx_sem)
    idx_copy.start()
    clear(1)

    for copy in small_copies:
        copy.wait()
    @pl.loop(0, square.shape[0] // tile_rows)
    def _(i):
        rows = pl.ds(pl.multiple_of(i * tile_rows, tile_rows), tile_rows)
        t = proj[pl.ds(pl.multiple_of(tra_first + i * tile_rows, tile_rows), tile_rows), :].astype(jnp.float32)
        x = proj[pl.ds(pl.multiple_of(img_first + i * tile_rows, tile_rows), tile_rows), :].astype(jnp.float32)
        square[rows, :] = t * t
        cross[rows, :] = t * x

    for p in range(n_part - n_late, n_part):
        proj_copy(p).start()

    sublane = lax.broadcasted_iota(jnp.int32, (SUB, LANES), 0)
    bits = [(sublane & (1 << t)) != 0 for t in range(3)]

    def stage(p, j, part):
        first = pl.multiple_of((p * n_tile + j) * tile_rows, tile_rows)
        part[...] = proj[pl.ds(first, tile_rows), :].astype(jnp.float32)

    def staged(part):
        return [part[pl.ds(k, SUB, stride=SUB), :] for k in range(n_pose)]

    def rolled(p, j):
        first = (p * n_tile + j) * tile_rows
        cells = []
        for c in range(0, SUB, 2):
            pair = proj[pl.ds(pl.multiple_of(first + c * SUB, 2 * SUB), 2 * SUB), :].astype(jnp.float32)
            cells += [pair[:SUB], pair[SUB:]]
        cells = [pltpu.roll(x, c, 0) if c else x for c, x in enumerate(cells)]
        for t, bit in enumerate(bits):
            cells = [jnp.where(bit, cells[(i + (1 << t)) % SUB], cells[i]) for i in range(SUB)]
        return [pltpu.roll(cells[-k % SUB], SUB - k, 0) if k else cells[0] for k in range(n_pose)]

    def terms(p, j, cells, weights):
        cell = pl.ds((j * (n_part // SUB) + p // SUB) * tile_rows + p % SUB, SUB, stride=SUB)
        tt, ti = square[cell, :], cross[cell, :]
        return [(tt * cells[k] - ti) * weights[k] for k in range(n_pose)]

    def add_rows(p, j, values):
        for first in range(0, n_pose, n_acc):
            group = range(first, first + n_acc)
            rows = [pl.ds(pl.multiple_of(idx_s[j, p * n_pose + k], SUB), SUB) for k in group]
            old = [accs[i][rows[i], :] for i in range(n_acc)]
            for i, k in enumerate(group):
                accs[i][rows[i], :] = old[i] + values[k]

    idx_copy.wait()

    @pl.loop(0, n_part)
    def _(p):
        proj_copy(p).wait()
        weights = [jnp.full((SUB, LANES), weight[k, p], jnp.float32) for k in range(n_pose)]

        stage(p, 0, parts[0])

        @pl.loop(0, n_tile, step=UNROLL, init_carry=tuple(terms(p, 0, staged(parts[0]), weights)))
        def _(j, values):
            for u in range(UNROLL):
                part = parts[(u // 2 + 1) % len(parts)]
                if u % 2 == 0:
                    stage(p, jnp.minimum(j + u + 2, n_tile - 1) if u + 2 == UNROLL else j + u + 2, part)
                    following = j + u + 1
                    later = terms(p, following, rolled(p, following), weights)
                else:
                    following = jnp.minimum(j + u + 1, n_tile - 1) if u + 1 == UNROLL else j + u + 1
                    later = terms(p, following, staged(part), weights)
                add_rows(p, j + u, values)
                values = later
            return tuple(values)

    Sums(n_owner, accs).pieces_away(sent_y, sent_z, sent=True)


class Sums:
    def __init__(self, n_owner, accs):
        self.accs = accs
        self.half_rows = accs[0].shape[0] // (n_owner * 2)
        self.sizes = {"y": 2, "l": 2, "h": n_owner // 4}

    def pieces(self, out, begin, part, firsts, sent):
        rep, near, low, high = position()
        order = ORDERS[part]
        inner = self.sizes[order[1]] * self.sizes[order[2]]
        size = PART_ROWS[part] * SUB
        within = sum(PART_ROWS[:part]) * SUB
        half = 1 - rep if sent else rep

        @pl.loop(0, len(firsts) * inner)
        def _(i):
            off = {order[0]: firsts[0] + i // inner}
            off[order[1]] = i % inner // self.sizes[order[2]]
            off[order[2]] = i % self.sizes[order[2]]
            owner = ((high ^ off["h"]) * 2 + (low ^ off["l"])) * 2 + (near ^ off["y"])
            first = pl.multiple_of((owner * 2 + half) * self.half_rows + within, SUB)
            total = self.accs[0][pl.ds(first, size), :]
            for acc in self.accs[1:]:
                total += acc[pl.ds(first, size), :]
            out[pl.ds(pl.multiple_of(begin + i * size, SUB), size), :] = total

        return begin + len(firsts) * inner * size

    def pieces_away(self, out_y, out_z, sent):
        begin = self.pieces(out_y, 0, 0, range(1, 2), sent)
        self.pieces(out_y, begin, 1, range(1, 2), sent)
        begin = self.pieces(out_z, 0, 2, range(1, 2), sent)
        self.pieces(out_z, begin, 3, range(1, self.sizes["h"]), sent)

    def pieces_stay(self, out, sent):
        begin = 0
        for part in range(len(ORDERS)):
            begin = self.pieces(out, begin, part, range(1), sent)


def rest_kernel(n_owner, *refs):
    accs, (kept_y, kept_z, sent_stay, kept_stay) = refs[:-4], refs[-4:]
    sums = Sums(n_owner, accs)
    sums.pieces_away(kept_y, kept_z, sent=False)
    sums.pieces_stay(sent_stay, sent=True)
    sums.pieces_stay(kept_stay, sent=False)


def tiles_in_order(array):
    lead = array.shape[:-2]
    rows, cells = array.shape[-2:]
    array = array.reshape(lead + (rows // SUB, SUB, cells // LANES, LANES))
    return jnp.swapaxes(array, -3, -2).reshape(-1, LANES)


def accumulate(
    projections, images, transfer, pose_weights, pose_of, pose_blocks, pose_tiles,
    bank_size, n_owner,
):
    n_part, n_pose, n_tile, n_cell = projections.shape
    assert n_cell == SUB * LANES and n_pose == SUB and n_part % SUB == 0 and n_tile % UNROLL == 0
    n_row = n_owner * NB_DEV * bank_size * SUB
    n_acc = 4 if n_row * LANES * 4 <= 4 * MIB else 2
    projections = tiles_in_order(jnp.transpose(projections, (0, 2, 1, 3)))
    images = tiles_in_order(jnp.transpose(images, (1, 0, 2)))
    transfer = tiles_in_order(jnp.transpose(transfer, (1, 0, 2)))
    stay = functools.partial(pltpu.with_memory_space_constraint, memory_space=pltpu.HBM)
    hbm = pl.BlockSpec(memory_space=pltpu.HBM)
    vmem = pl.BlockSpec(memory_space=pltpu.VMEM)
    n_high = n_owner // 4
    a, d, b, e = (rows * SUB for rows in PART_ROWS)
    assert sum(PART_ROWS) == NB_DEV // 2 * bank_size

    away_y, away_z = 2 * n_high * (a + d), 2 * n_high * b + 4 * (n_high - 1) * e

    def out(rows):
        return jax.ShapeDtypeStruct((rows, LANES), jnp.float32)

    sent_y, sent_z, *accs = pl.pallas_call(
        functools.partial(accumulate_kernel, bank_size, n_owner, n_acc),
        out_shape=[out(away_y), out(away_z)] + [out(n_row)] * n_acc,
        in_specs=[hbm] * 7,
        out_specs=[vmem] * (2 + n_acc),
        scratch_shapes=[
            pltpu.VMEM(projections.shape, jnp.bfloat16),
            pltpu.SMEM((n_pose, n_part), jnp.float32),
            pltpu.VMEM((n_pose, n_part), jnp.int32),
            pltpu.VMEM(pose_blocks.shape[::-1], jnp.int32),
            pltpu.VMEM(pose_tiles.shape[::-1], jnp.int32),
            pltpu.VMEM((n_tile, n_part * n_pose), jnp.int32),
            pltpu.SMEM((n_tile, n_part * n_pose), jnp.int32),
            pltpu.VMEM(transfer.shape, jnp.float32),
            pltpu.VMEM(transfer.shape, jnp.float32),
        ]
        + [pltpu.VMEM((n_pose * SUB, LANES), jnp.float32)] * N_BUF
        + [
            pltpu.SemaphoreType.DMA((n_part,)),
            pltpu.SemaphoreType.DMA((3,)),
            pltpu.SemaphoreType.DMA((3,)),
            pltpu.SemaphoreType.DMA,
        ],
        compiler_params=pltpu.CompilerParams(vmem_limit_bytes=24 * MIB),
        name="accumulate",
    )(
        stay(projections), stay(images), stay(transfer),
        stay(pose_weights.T), stay(pose_of.T), stay(pose_blocks.T), stay(pose_tiles.T),
    )
    rows = 2 * n_high * (a + d + b) + 4 * e
    kept_y, kept_z, sent_stay, kept_stay = in_vmem(
        functools.partial(rest_kernel, n_owner), "rest", [away_y, away_z, rows, rows], *accs
    )
    return sent_y, kept_y, sent_z, kept_z, sent_stay, kept_stay


def in_vmem(kernel, name, rows, *operands):
    vmem = pl.BlockSpec(memory_space=pltpu.VMEM)
    return pl.pallas_call(
        kernel,
        out_shape=[jax.ShapeDtypeStruct((n, LANES), jnp.float32) for n in rows],
        in_specs=[vmem] * len(operands),
        out_specs=[vmem] * len(rows),
        compiler_params=pltpu.CompilerParams(vmem_limit_bytes=32 * MIB),
        name=name,
    )(*operands)


def first_kernel(kept, got, *to):
    begin = 0
    for out in to:
        rows = slice(begin, begin + out.shape[0])
        out[...] = kept[rows, :] + got[rows, :]
        begin += out.shape[0]


def second_kernel(n_high, kept, got, got_y, got_l, *rest):
    got_h, (own_a, own_d, own_b, own_e, to_y, to_l, *to_h) = rest[: n_high - 1], rest[n_high - 1 :]
    a, d, b, e = (rows * SUB for rows in PART_ROWS)

    def put(out, at, begin, size, *arrivals):
        total = kept[begin : begin + size, :] + got[begin : begin + size, :]
        for array, first in arrivals:
            total += array[first : first + size, :]
        out[at : at + size, :] = total

    n = n_high * a
    put(own_a, 0, 0, n, (got_y, 0))
    put(to_l, 0, n, n, (got_y, n))
    begin, y_begin = 2 * n, 2 * n
    put(own_d, 0, begin, 2 * d, (got_y, y_begin))
    for i, out in enumerate(to_h):
        put(out, 0, begin + 2 * d * (i + 1), 2 * d, (got_y, y_begin + 2 * d * (i + 1)))
    begin, n = begin + 2 * n_high * d, n_high * b
    put(own_b, 0, begin, n, (got_l, 0))
    put(to_y, 0, begin + n, n, (got_l, n))
    begin += 2 * n
    put(own_e, 0, begin, 2 * e, *[(array, 0) for array in got_h])
    put(to_y, n, begin + 2 * e, 2 * e, *[(array, 2 * e) for array in got_h])


def third_kernel(n_high, own_a, own_d, own_b, own_e, got_y, got_l, *rest):
    got_h, (own, to_l, *to_h) = rest[: n_high - 1], rest[n_high - 1 :]
    a, d, b, e = (rows * SUB for rows in PART_ROWS)

    def put(out, at, source, begin, size, *arrivals):
        total = source[begin : begin + size, :]
        for array, first in arrivals:
            total += array[first : first + size, :]
        out[at : at + size, :] = total

    put(own, 0, own_a, 0, a, (got_l, 0))
    put(own, a, own_d, 0, d, *[(array, 0) for array in got_h])
    put(own, a + d, own_b, 0, b, (got_y, 0))
    put(own, a + d + b, own_e, 0, e, (got_y, n_high * b))
    put(to_l, 0, own_d, d, d, *[(array, d) for array in got_h])
    put(to_l, d, own_e, e, e, (got_y, n_high * b + e))
    for i, out in enumerate(to_h):
        put(out, 0, own_a, (i + 1) * a, a, (got_l, (i + 1) * a))
        put(out, a, own_b, (i + 1) * b, b, (got_y, (i + 1) * b))


def last_kernel(before, got_l, *rest):
    got_h, (own,) = rest[:-1], rest[-1:]
    a, d, b, e = (rows * SUB for rows in PART_ROWS)
    for at, size, arrivals in (
        (0, a, [(array, 0) for array in got_h]),
        (a, d, [(got_l, 0)]),
        (a + d, b, [(array, a) for array in got_h]),
        (a + d + b, e, [(got_l, d)]),
    ):
        total = before[at : at + size, :]
        for array, first in arrivals:
            total += array[first : first + size, :]
        own[at : at + size, :] = total


def bank_kernel(own, other, bank, out):
    bank_size, n_z, n_cell = bank.shape
    n_half = out.shape[0] // 2
    group = 2 * SUB

    def apply(halves):
        for c in range(n_cell // LANES):
            cols = slice(c * LANES, (c + 1) * LANES)

            @pl.loop(0, n_z // group)
            def _(g):
                rows = pl.ds(pl.multiple_of(g * group, group), group)
                weights = [bank[t, rows, cols] for t in range(bank_size)]
                for b in range(2 * n_half):
                    total = None
                    for t in range(bank_size):
                        value = weights[t] * halves[b // n_half][b % n_half, t, c : c + 1, :]
                        total = value if total is None else total + value
                    out[b, rows, cols] = total

    rep = position()[0]

    @pl.when(rep == 0)
    def _():
        apply((own, other))

    @pl.when(rep == 1)
    def _():
        apply((other, own))


def apply_bank(own, other, weight_bank):
    bank_size, n_z, n_cell = weight_bank.shape
    vmem = pl.BlockSpec(memory_space=pltpu.VMEM)
    own, other = [array.reshape(NB_DEV // 2, bank_size, SUB, LANES) for array in (own, other)]
    return pl.pallas_call(
        bank_kernel,
        out_shape=jax.ShapeDtypeStruct((NB_DEV, n_z, n_cell), jnp.float32),
        in_specs=[vmem] * 3,
        out_specs=vmem,
        compiler_params=pltpu.CompilerParams(vmem_limit_bytes=32 * MIB),
        name="apply_bank",
    )(own, other, weight_bank)


def body(
    projections, images, transfer, pose_weights, pose_of, pose_blocks, pose_tiles, weight_bank
):
    bank_size = weight_bank.shape[0]
    n_blk = lax.axis_size("blk")
    n_high = n_blk // 4
    sent_y, kept_y, sent_z, kept_z, sent_stay, kept_stay = accumulate(
        projections, images, transfer, pose_weights, pose_of, pose_blocks, pose_tiles,
        bank_size, n_blk,
    )
    a, d, b, e = (rows * SUB for rows in PART_ROWS)

    def over_rep(array):
        return lax.ppermute(array, "rep", [(0, 1), (1, 0)])

    def over_blk(array, bits):
        return lax.ppermute(array, "blk", [(i, i ^ bits) for i in range(n_blk)])

    def over_h(arrays):
        return [over_blk(array, 4 * (i + 1)) for i, array in enumerate(arrays)]

    n_h = n_high - 1
    got_y, got_z, got_stay = over_rep(sent_y), over_rep(sent_z), over_rep(sent_stay)
    (to_y,) = in_vmem(first_kernel, "first_y", [kept_y.shape[0]], kept_y, got_y)
    got_y = over_blk(to_y, 1)
    to_l, *to_h = in_vmem(first_kernel, "first_z", [2 * n_high * b] + [4 * e] * n_h, kept_z, got_z)
    got_l, got_h = over_blk(to_l, 2), over_h(to_h)
    own_a, own_d, own_b, own_e, to_y, to_l, *to_h = in_vmem(
        functools.partial(second_kernel, n_high), "second",
        [n_high * a, 2 * d, n_high * b, 2 * e, n_high * b + 2 * e, n_high * a] + [2 * d] * n_h,
        kept_stay, got_stay, got_y, got_l, *got_h,
    )
    got_y, got_l, got_h = over_blk(to_y, 1), over_blk(to_l, 2), over_h(to_h)
    own, to_l, *to_h = in_vmem(
        functools.partial(third_kernel, n_high), "third", [a + d + b + e, d + e] + [a + b] * n_h,
        own_a, own_d, own_b, own_e, got_y, got_l, *got_h,
    )
    got_l, got_h = over_blk(to_l, 2), over_h(to_h)
    (own,) = in_vmem(last_kernel, "last", [a + d + b + e], own, got_l, *got_h)
    return apply_bank(own, over_rep(own), weight_bank)


def solution(mesh):
    placed = (
        P(("groups", "blk", "rep"), None, None, None),
        P(("groups", "blk", "rep"), None, None),
        P(("groups", "blk", "rep"), None, None),
        P(("groups", "blk", "rep"), None),
        P(("groups", "blk", "rep"), None),
        P("groups", None),
        P("groups", None),
        P(),
    )
    return jax.shard_map(
        body,
        mesh=mesh,
        in_specs=placed,
        out_specs=P(("groups", "blk"), None, None),
        check_vma=False,
    )
```

```python
import functools

import jax
import jax.numpy as jnp
from jax import lax
from jax.experimental import pallas as pl
from jax.experimental.pallas import tpu as pltpu
from jax.sharding import PartitionSpec as P

NB_DEV = 8
LANES = 128
SUB = 8
MIB = 1 << 20
UNROLL = 12
N_BUF = 4
ORDERS = ("ylh", "yhl", "lyh", "hyl")
PART_ROWS = (16, 16, 16, 16)


def position():
    here = lax.axis_index("blk")
    return lax.axis_index("rep"), here & 1, (here >> 1) & 1, here >> 2


def accumulate_kernel(
    bank_size, n_owner, n_acc,
    proj_hbm, img_hbm, tra_hbm, w_hbm, pose_hbm, blocks_hbm, tiles_hbm,
    sent_away, *rest,
):
    accs, rest = rest[:n_acc], rest[n_acc:]
    proj, weight, pose, blocks, tiles, idx_v, idx_s, square, cross = rest[:9]
    parts = rest[9 : 9 + N_BUF]
    proj_sem, small_sem, table_sem, idx_sem = rest[9 + N_BUF :]
    n_pose, n_part = pose.shape
    n_tile, n_table = blocks.shape
    n_row = accs[0].shape[0]
    tile_rows = SUB * SUB
    part_rows = n_tile * tile_rows

    table_copies = [
        pltpu.make_async_copy(src, dst, table_sem.at[i])
        for i, (src, dst) in enumerate(((pose_hbm, pose), (blocks_hbm, blocks), (tiles_hbm, tiles)))
    ]
    n_late = n_part // 4
    n_small = img_hbm.shape[0]
    img_first, tra_first = proj.shape[0] - n_small, proj.shape[0] - 2 * n_small
    img, tra = proj.at[pl.ds(img_first, n_small), :], proj.at[pl.ds(tra_first, n_small), :]
    small_copies = [
        pltpu.make_async_copy(img_hbm, img, small_sem.at[0]),
        pltpu.make_async_copy(tra_hbm, tra, small_sem.at[1]),
        pltpu.make_async_copy(w_hbm, weight, small_sem.at[2]),
    ]
    for copy in table_copies + small_copies:
        copy.start()

    def proj_copy(p):
        rows = pl.ds(pl.multiple_of(p * part_rows, part_rows), part_rows)
        return pltpu.make_async_copy(proj_hbm.at[rows, :], proj.at[rows, :], proj_sem.at[p])

    for p in range(n_part - n_late):
        proj_copy(p).start()

    zero = jnp.zeros((16 * SUB, LANES), jnp.float32)

    def clear(half):
        @pl.loop(0, n_row // (32 * SUB))
        def _(i):
            rows = pl.ds(pl.multiple_of(half * (n_row // 2) + i * (16 * SUB), 16 * SUB), 16 * SUB)
            for acc in accs:
                acc[rows, :] = zero

    clear(0)
    for copy in table_copies:
        copy.wait()
    lane = lax.broadcasted_iota(jnp.int32, (n_pose, n_table), 1)
    chosen = jnp.concatenate(
        [(pose[:, p : p + 1] == lane).astype(jnp.float32) for p in range(n_part)], axis=0
    ).astype(jnp.bfloat16)

    def look_up(table):
        return lax.dot_general(
            table[...].astype(jnp.float32).astype(jnp.bfloat16), chosen,
            (((1,), (1,)), ((), ())), preferred_element_type=jnp.float32,
        )

    idx_v[...] = ((look_up(blocks) * bank_size + look_up(tiles)) * SUB).astype(jnp.int32)
    idx_copy = pltpu.make_async_copy(idx_v, idx_s, idx_sem)
    idx_copy.start()
    clear(1)

    for copy in small_copies:
        copy.wait()
    @pl.loop(0, square.shape[0] // tile_rows)
    def _(i):
        rows = pl.ds(pl.multiple_of(i * tile_rows, tile_rows), tile_rows)
        t = proj[pl.ds(pl.multiple_of(tra_first + i * tile_rows, tile_rows), tile_rows), :].astype(jnp.float32)
        x = proj[pl.ds(pl.multiple_of(img_first + i * tile_rows, tile_rows), tile_rows), :].astype(jnp.float32)
        square[rows, :] = t * t
        cross[rows, :] = t * x

    for p in range(n_part - n_late, n_part):
        proj_copy(p).start()

    sublane = lax.broadcasted_iota(jnp.int32, (SUB, LANES), 0)
    bits = [(sublane & (1 << t)) != 0 for t in range(3)]

    def stage(p, j, part):
        first = pl.multiple_of((p * n_tile + j) * tile_rows, tile_rows)
        part[...] = proj[pl.ds(first, tile_rows), :].astype(jnp.float32)

    def staged(part):
        return [part[pl.ds(k, SUB, stride=SUB), :] for k in range(n_pose)]

    def rolled(p, j):
        first = (p * n_tile + j) * tile_rows
        cells = []
        for c in range(0, SUB, 2):
            pair = proj[pl.ds(pl.multiple_of(first + c * SUB, 2 * SUB), 2 * SUB), :].astype(jnp.float32)
            cells += [pair[:SUB], pair[SUB:]]
        cells = [pltpu.roll(x, c, 0) if c else x for c, x in enumerate(cells)]
        for t, bit in enumerate(bits):
            cells = [jnp.where(bit, cells[(i + (1 << t)) % SUB], cells[i]) for i in range(SUB)]
        return [pltpu.roll(cells[-k % SUB], SUB - k, 0) if k else cells[0] for k in range(n_pose)]

    def terms(p, j, cells, weights):
        cell = pl.ds((j * (n_part // SUB) + p // SUB) * tile_rows + p % SUB, SUB, stride=SUB)
        tt, ti = square[cell, :], cross[cell, :]
        return [(tt * cells[k] - ti) * weights[k] for k in range(n_pose)]

    def add_rows(p, j, values):
        for first in range(0, n_pose, n_acc):
            group = range(first, first + n_acc)
            rows = [pl.ds(pl.multiple_of(idx_s[j, p * n_pose + k], SUB), SUB) for k in group]
            old = [accs[i][rows[i], :] for i in range(n_acc)]
            for i, k in enumerate(group):
                accs[i][rows[i], :] = old[i] + values[k]

    idx_copy.wait()

    @pl.loop(0, n_part)
    def _(p):
        proj_copy(p).wait()
        weights = [jnp.full((SUB, LANES), weight[k, p], jnp.float32) for k in range(n_pose)]

        stage(p, 0, parts[0])
        stage(p, 1, parts[1])

        @pl.loop(0, n_tile, step=UNROLL, init_carry=tuple(terms(p, 0, staged(parts[0]), weights)))
        def _(j, values):
            def tile(u):
                return jnp.minimum(j + u, n_tile - 1) if u >= UNROLL else j + u

            for u in range(UNROLL):
                if (u + 2) % 3 != 2:
                    stage(p, tile(u + 2), parts[(u + 2) % N_BUF])
                cells = staged(parts[(u + 1) % N_BUF]) if (u + 1) % 3 != 2 else rolled(p, tile(u + 1))
                later = terms(p, tile(u + 1), cells, weights)
                add_rows(p, j + u, values)
                values = later
            return tuple(values)

    Sums(n_owner, accs).pieces_away(sent_away, sent=True)


class Sums:
    def __init__(self, n_owner, accs):
        self.accs = accs
        self.half_rows = accs[0].shape[0] // (n_owner * 2)
        self.sizes = {"y": 2, "l": 2, "h": n_owner // 4}

    def pieces(self, out, begin, part, firsts, sent):
        rep, near, low, high = position()
        order = ORDERS[part]
        inner = self.sizes[order[1]] * self.sizes[order[2]]
        size = PART_ROWS[part] * SUB
        within = sum(PART_ROWS[:part]) * SUB
        half = 1 - rep if sent else rep

        @pl.loop(0, len(firsts) * inner)
        def _(i):
            off = {order[0]: firsts[0] + i // inner}
            off[order[1]] = i % inner // self.sizes[order[2]]
            off[order[2]] = i % self.sizes[order[2]]
            owner = ((high ^ off["h"]) * 2 + (low ^ off["l"])) * 2 + (near ^ off["y"])
            first = pl.multiple_of((owner * 2 + half) * self.half_rows + within, SUB)
            total = self.accs[0][pl.ds(first, size), :]
            for acc in self.accs[1:]:
                total += acc[pl.ds(first, size), :]
            out[pl.ds(pl.multiple_of(begin + i * size, SUB), size), :] = total

        return begin + len(firsts) * inner * size

    def pieces_away(self, out, sent):
        begin = 0
        for part, order in enumerate(ORDERS):
            begin = self.pieces(out, begin, part, range(1, self.sizes[order[0]]), sent)

    def pieces_stay(self, out, sent):
        begin = 0
        for part in range(len(ORDERS)):
            begin = self.pieces(out, begin, part, range(1), sent)


def rest_kernel(n_owner, *refs):
    accs, (kept_away, sent_stay, kept_stay) = refs[:-3], refs[-3:]
    sums = Sums(n_owner, accs)
    sums.pieces_away(kept_away, sent=False)
    sums.pieces_stay(sent_stay, sent=True)
    sums.pieces_stay(kept_stay, sent=False)


def tiles_in_order(array):
    lead = array.shape[:-2]
    rows, cells = array.shape[-2:]
    array = array.reshape(lead + (rows // SUB, SUB, cells // LANES, LANES))
    return jnp.swapaxes(array, -3, -2).reshape(-1, LANES)


def accumulate(
    projections, images, transfer, pose_weights, pose_of, pose_blocks, pose_tiles,
    bank_size, n_owner,
):
    n_part, n_pose, n_tile, n_cell = projections.shape
    assert n_cell == SUB * LANES and n_pose == SUB and n_part % SUB == 0 and n_tile % UNROLL == 0 and UNROLL % (3 * N_BUF) == 0
    n_row = n_owner * NB_DEV * bank_size * SUB
    n_acc = 4 if n_row * LANES * 4 <= 4 * MIB else 2
    projections = tiles_in_order(jnp.transpose(projections, (0, 2, 1, 3)))
    images = tiles_in_order(jnp.transpose(images, (1, 0, 2)))
    transfer = tiles_in_order(jnp.transpose(transfer, (1, 0, 2)))
    stay = functools.partial(pltpu.with_memory_space_constraint, memory_space=pltpu.HBM)
    hbm = pl.BlockSpec(memory_space=pltpu.HBM)
    vmem = pl.BlockSpec(memory_space=pltpu.VMEM)
    n_high = n_owner // 4
    a, d, b, e = (rows * SUB for rows in PART_ROWS)
    assert sum(PART_ROWS) == NB_DEV // 2 * bank_size

    away = 2 * n_high * (a + d + b) + 4 * (n_high - 1) * e

    def out(rows):
        return jax.ShapeDtypeStruct((rows, LANES), jnp.float32)

    sent_away, *accs = pl.pallas_call(
        functools.partial(accumulate_kernel, bank_size, n_owner, n_acc),
        out_shape=[out(away)] + [out(n_row)] * n_acc,
        in_specs=[hbm] * 7,
        out_specs=[vmem] * (1 + n_acc),
        scratch_shapes=[
            pltpu.VMEM(projections.shape, jnp.bfloat16),
            pltpu.SMEM((n_pose, n_part), jnp.float32),
            pltpu.VMEM((n_pose, n_part), jnp.int32),
            pltpu.VMEM(pose_blocks.shape[::-1], jnp.int32),
            pltpu.VMEM(pose_tiles.shape[::-1], jnp.int32),
            pltpu.VMEM((n_tile, n_part * n_pose), jnp.int32),
            pltpu.SMEM((n_tile, n_part * n_pose), jnp.int32),
            pltpu.VMEM(transfer.shape, jnp.float32),
            pltpu.VMEM(transfer.shape, jnp.float32),
        ]
        + [pltpu.VMEM((n_pose * SUB, LANES), jnp.float32)] * N_BUF
        + [
            pltpu.SemaphoreType.DMA((n_part,)),
            pltpu.SemaphoreType.DMA((3,)),
            pltpu.SemaphoreType.DMA((3,)),
            pltpu.SemaphoreType.DMA,
        ],
        compiler_params=pltpu.CompilerParams(vmem_limit_bytes=24 * MIB),
        name="accumulate",
    )(
        stay(projections), stay(images), stay(transfer),
        stay(pose_weights.T), stay(pose_of.T), stay(pose_blocks.T), stay(pose_tiles.T),
    )
    rows = 2 * n_high * (a + d + b) + 4 * e
    return sent_away, *in_vmem(functools.partial(rest_kernel, n_owner), "rest", [away, rows, rows], *accs)


def in_vmem(kernel, name, rows, *operands):
    vmem = pl.BlockSpec(memory_space=pltpu.VMEM)
    return pl.pallas_call(
        kernel,
        out_shape=[jax.ShapeDtypeStruct((n, LANES), jnp.float32) for n in rows],
        in_specs=[vmem] * len(operands),
        out_specs=[vmem] * len(rows),
        compiler_params=pltpu.CompilerParams(vmem_limit_bytes=32 * MIB),
        name=name,
    )(*operands)


def first_kernel(kept, got, *to):
    begin = 0
    for out in to:
        rows = slice(begin, begin + out.shape[0])
        out[...] = kept[rows, :] + got[rows, :]
        begin += out.shape[0]


def second_kernel(n_high, kept, got, got_y, got_l, *rest):
    got_h, (own_a, own_d, own_b, own_e, to_y, to_l, *to_h) = rest[: n_high - 1], rest[n_high - 1 :]
    a, d, b, e = (rows * SUB for rows in PART_ROWS)

    def put(out, at, begin, size, *arrivals):
        total = kept[begin : begin + size, :] + got[begin : begin + size, :]
        for array, first in arrivals:
            total += array[first : first + size, :]
        out[at : at + size, :] = total

    n = n_high * a
    put(own_a, 0, 0, n, (got_y, 0))
    put(to_l, 0, n, n, (got_y, n))
    begin, y_begin = 2 * n, 2 * n
    put(own_d, 0, begin, 2 * d, (got_y, y_begin))
    for i, out in enumerate(to_h):
        put(out, 0, begin + 2 * d * (i + 1), 2 * d, (got_y, y_begin + 2 * d * (i + 1)))
    begin, n = begin + 2 * n_high * d, n_high * b
    put(own_b, 0, begin, n, (got_l, 0))
    put(to_y, 0, begin + n, n, (got_l, n))
    begin += 2 * n
    put(own_e, 0, begin, 2 * e, *[(array, 0) for array in got_h])
    put(to_y, n, begin + 2 * e, 2 * e, *[(array, 2 * e) for array in got_h])


def third_kernel(n_high, own_a, own_d, own_b, own_e, got_y, got_l, *rest):
    got_h, (own, to_l, *to_h) = rest[: n_high - 1], rest[n_high - 1 :]
    a, d, b, e = (rows * SUB for rows in PART_ROWS)

    def put(out, at, source, begin, size, *arrivals):
        total = source[begin : begin + size, :]
        for array, first in arrivals:
            total += array[first : first + size, :]
        out[at : at + size, :] = total

    put(own, 0, own_a, 0, a, (got_l, 0))
    put(own, a, own_d, 0, d, *[(array, 0) for array in got_h])
    put(own, a + d, own_b, 0, b, (got_y, 0))
    put(own, a + d + b, own_e, 0, e, (got_y, n_high * b))
    put(to_l, 0, own_d, d, d, *[(array, d) for array in got_h])
    put(to_l, d, own_e, e, e, (got_y, n_high * b + e))
    for i, out in enumerate(to_h):
        put(out, 0, own_a, (i + 1) * a, a, (got_l, (i + 1) * a))
        put(out, a, own_b, (i + 1) * b, b, (got_y, (i + 1) * b))


def last_kernel(before, got_l, *rest):
    got_h, (own,) = rest[:-1], rest[-1:]
    a, d, b, e = (rows * SUB for rows in PART_ROWS)
    for at, size, arrivals in (
        (0, a, [(array, 0) for array in got_h]),
        (a, d, [(got_l, 0)]),
        (a + d, b, [(array, a) for array in got_h]),
        (a + d + b, e, [(got_l, d)]),
    ):
        total = before[at : at + size, :]
        for array, first in arrivals:
            total += array[first : first + size, :]
        own[at : at + size, :] = total


def bank_kernel(own, other, bank, out):
    bank_size, n_z, n_cell = bank.shape
    n_half = out.shape[0] // 2
    group = 2 * SUB

    def apply(halves):
        for c in range(n_cell // LANES):
            cols = slice(c * LANES, (c + 1) * LANES)

            @pl.loop(0, n_z // group)
            def _(g):
                rows = pl.ds(pl.multiple_of(g * group, group), group)
                weights = [bank[t, rows, cols] for t in range(bank_size)]
                for b in range(2 * n_half):
                    total = None
                    for t in range(bank_size):
                        value = weights[t] * halves[b // n_half][b % n_half, t, c : c + 1, :]
                        total = value if total is None else total + value
                    out[b, rows, cols] = total

    rep = position()[0]

    @pl.when(rep == 0)
    def _():
        apply((own, other))

    @pl.when(rep == 1)
    def _():
        apply((other, own))


def apply_bank(own, other, weight_bank):
    bank_size, n_z, n_cell = weight_bank.shape
    vmem = pl.BlockSpec(memory_space=pltpu.VMEM)
    own, other = [array.reshape(NB_DEV // 2, bank_size, SUB, LANES) for array in (own, other)]
    return pl.pallas_call(
        bank_kernel,
        out_shape=jax.ShapeDtypeStruct((NB_DEV, n_z, n_cell), jnp.float32),
        in_specs=[vmem] * 3,
        out_specs=vmem,
        compiler_params=pltpu.CompilerParams(vmem_limit_bytes=32 * MIB),
        name="apply_bank",
    )(own, other, weight_bank)


def body(
    projections, images, transfer, pose_weights, pose_of, pose_blocks, pose_tiles, weight_bank
):
    bank_size = weight_bank.shape[0]
    n_blk = lax.axis_size("blk")
    n_high = n_blk // 4
    sent_away, kept_away, sent_stay, kept_stay = accumulate(
        projections, images, transfer, pose_weights, pose_of, pose_blocks, pose_tiles,
        bank_size, n_blk,
    )
    a, d, b, e = (rows * SUB for rows in PART_ROWS)

    def over_rep(array):
        return lax.ppermute(array, "rep", [(0, 1), (1, 0)])

    def over_blk(array, bits):
        return lax.ppermute(array, "blk", [(i, i ^ bits) for i in range(n_blk)])

    def over_h(arrays):
        return [over_blk(array, 4 * (i + 1)) for i, array in enumerate(arrays)]

    n_h = n_high - 1
    got_away, got_stay = over_rep(sent_away), over_rep(sent_stay)
    to_y, to_l, *to_h = in_vmem(
        first_kernel, "first", [2 * n_high * (a + d), 2 * n_high * b] + [4 * e] * n_h, kept_away, got_away
    )
    got_y, got_l, got_h = over_blk(to_y, 1), over_blk(to_l, 2), over_h(to_h)
    own_a, own_d, own_b, own_e, to_y, to_l, *to_h = in_vmem(
        functools.partial(second_kernel, n_high), "second",
        [n_high * a, 2 * d, n_high * b, 2 * e, n_high * b + 2 * e, n_high * a] + [2 * d] * n_h,
        kept_stay, got_stay, got_y, got_l, *got_h,
    )
    got_y, got_l, got_h = over_blk(to_y, 1), over_blk(to_l, 2), over_h(to_h)
    own, to_l, *to_h = in_vmem(
        functools.partial(third_kernel, n_high), "third", [a + d + b + e, d + e] + [a + b] * n_h,
        own_a, own_d, own_b, own_e, got_y, got_l, *got_h,
    )
    got_l, got_h = over_blk(to_l, 2), over_h(to_h)
    (own,) = in_vmem(last_kernel, "last", [a + d + b + e], own, got_l, *got_h)
    return apply_bank(own, over_rep(own), weight_bank)


def solution(mesh):
    placed = (
        P(("groups", "blk", "rep"), None, None, None),
        P(("groups", "blk", "rep"), None, None),
        P(("groups", "blk", "rep"), None, None),
        P(("groups", "blk", "rep"), None),
        P(("groups", "blk", "rep"), None),
        P("groups", None),
        P("groups", None),
        P(),
    )
    return jax.shard_map(
        body,
        mesh=mesh,
        in_specs=placed,
        out_specs=P(("groups", "blk"), None, None),
        check_vma=False,
    )
```

```python
import functools

import jax
import jax.numpy as jnp
from jax import lax
from jax.experimental import pallas as pl
from jax.experimental.pallas import tpu as pltpu
from jax.sharding import PartitionSpec as P

NB_DEV = 8
LANES = 128
SUB = 8
MIB = 1 << 20
UNROLL = 12
N_BUF = 4
ORDERS = ("ylh", "yhl", "lyh", "hyl")
PART_ROWS = (16, 16, 16, 16)


def position():
    here = lax.axis_index("blk")
    return lax.axis_index("rep"), here & 1, (here >> 1) & 1, here >> 2


def accumulate_kernel(
    bank_size, n_owner, n_acc,
    proj_hbm, img_hbm, tra_hbm, w_hbm, pose_hbm, blocks_hbm, tiles_hbm,
    sent_away, *rest,
):
    accs, rest = rest[:n_acc], rest[n_acc:]
    proj, img, tra, weight, pose, blocks, tiles, idx_v, idx_s, square, cross = rest[:11]
    parts = rest[11 : 11 + N_BUF]
    proj_sem, small_sem, table_sem, idx_sem = rest[11 + N_BUF :]
    n_pose, n_part = pose.shape
    n_tile, n_table = blocks.shape
    n_row = accs[0].shape[0]
    tile_rows = SUB * SUB
    part_rows = n_tile * tile_rows

    table_copies = [
        pltpu.make_async_copy(src, dst, table_sem.at[i])
        for i, (src, dst) in enumerate(((pose_hbm, pose), (blocks_hbm, blocks), (tiles_hbm, tiles)))
    ]
    small_copies = [
        pltpu.make_async_copy(img_hbm, img, small_sem.at[0]),
        pltpu.make_async_copy(tra_hbm, tra, small_sem.at[1]),
        pltpu.make_async_copy(w_hbm, weight, small_sem.at[2]),
    ]
    for copy in table_copies + small_copies:
        copy.start()

    def proj_copy(p):
        rows = pl.ds(pl.multiple_of(p * part_rows, part_rows), part_rows)
        return pltpu.make_async_copy(proj_hbm.at[rows, :], proj.at[rows, :], proj_sem.at[p])

    for p in range(n_part):
        proj_copy(p).start()

    zero = jnp.zeros((8 * SUB, LANES), jnp.float32)

    @pl.loop(0, n_row // (8 * SUB))
    def _(i):
        rows = pl.ds(pl.multiple_of(i * (8 * SUB), 8 * SUB), 8 * SUB)
        for acc in accs:
            acc[rows, :] = zero

    for copy in table_copies:
        copy.wait()
    lane = lax.broadcasted_iota(jnp.int32, (n_pose, n_table), 1)
    chosen = jnp.concatenate(
        [(pose[:, p : p + 1] == lane).astype(jnp.float32) for p in range(n_part)], axis=0
    ).astype(jnp.bfloat16)

    def look_up(table):
        return lax.dot_general(
            table[...].astype(jnp.float32).astype(jnp.bfloat16), chosen,
            (((1,), (1,)), ((), ())), preferred_element_type=jnp.float32,
        )

    idx_v[...] = ((look_up(blocks) * bank_size + look_up(tiles)) * SUB).astype(jnp.int32)
    idx_copy = pltpu.make_async_copy(idx_v, idx_s, idx_sem)
    idx_copy.start()

    for copy in small_copies:
        copy.wait()

    @pl.loop(0, square.shape[0] // tile_rows)
    def _(i):
        rows = pl.ds(pl.multiple_of(i * tile_rows, tile_rows), tile_rows)
        t = tra[rows, :].astype(jnp.float32)
        square[rows, :] = t * t
        cross[rows, :] = t * img[rows, :].astype(jnp.float32)

    def stage(p, j, part):
        first = pl.multiple_of((p * n_tile + j) * tile_rows, tile_rows)
        part[...] = proj[pl.ds(first, tile_rows), :].astype(jnp.float32)

    def staged(part):
        return [part[pl.ds(k, SUB, stride=SUB), :] for k in range(n_pose)]

    def terms(p, j, cells, weights):
        cell = pl.ds((j * (n_part // SUB) + p // SUB) * tile_rows + p % SUB, SUB, stride=SUB)
        tt, ti = square[cell, :], cross[cell, :]
        return [(tt * cells[k] - ti) * weights[k] for k in range(n_pose)]

    def add_rows(p, j, values):
        for first in range(0, n_pose, n_acc):
            group = range(first, first + n_acc)
            rows = [pl.ds(pl.multiple_of(idx_s[j, p * n_pose + k], SUB), SUB) for k in group]
            old = [accs[i][rows[i], :] for i in range(n_acc)]
            for i, k in enumerate(group):
                accs[i][rows[i], :] = old[i] + values[k]

    idx_copy.wait()

    @pl.loop(0, n_part)
    def _(p):
        proj_copy(p).wait()
        weights = [jnp.full((SUB, LANES), weight[k, p], jnp.float32) for k in range(n_pose)]

        stage(p, 0, parts[0])
        stage(p, 1, parts[1])

        @pl.loop(0, n_tile, step=UNROLL, init_carry=tuple(terms(p, 0, staged(parts[0]), weights)))
        def _(j, values):
            def tile(u):
                return jnp.minimum(j + u, n_tile - 1) if u >= UNROLL else j + u

            for u in range(UNROLL):
                stage(p, tile(u + 2), parts[(u + 2) % N_BUF])
                later = terms(p, tile(u + 1), staged(parts[(u + 1) % N_BUF]), weights)
                add_rows(p, j + u, values)
                values = later
            return tuple(values)

    Sums(n_owner, accs).pieces_away(sent_away, sent=True)


class Sums:
    def __init__(self, n_owner, accs):
        self.accs = accs
        self.half_rows = accs[0].shape[0] // (n_owner * 2)
        self.sizes = {"y": 2, "l": 2, "h": n_owner // 4}

    def pieces(self, out, begin, part, firsts, sent):
        rep, near, low, high = position()
        order = ORDERS[part]
        inner = self.sizes[order[1]] * self.sizes[order[2]]
        size = PART_ROWS[part] * SUB
        within = sum(PART_ROWS[:part]) * SUB
        half = 1 - rep if sent else rep

        @pl.loop(0, len(firsts) * inner)
        def _(i):
            off = {order[0]: firsts[0] + i // inner}
            off[order[1]] = i % inner // self.sizes[order[2]]
            off[order[2]] = i % self.sizes[order[2]]
            owner = ((high ^ off["h"]) * 2 + (low ^ off["l"])) * 2 + (near ^ off["y"])
            first = pl.multiple_of((owner * 2 + half) * self.half_rows + within, SUB)
            total = self.accs[0][pl.ds(first, size), :]
            for acc in self.accs[1:]:
                total += acc[pl.ds(first, size), :]
            out[pl.ds(pl.multiple_of(begin + i * size, SUB), size), :] = total

        return begin + len(firsts) * inner * size

    def pieces_away(self, out, sent):
        begin = 0
        for part, order in enumerate(ORDERS):
            begin = self.pieces(out, begin, part, range(1, self.sizes[order[0]]), sent)

    def pieces_stay(self, out, sent):
        begin = 0
        for part in range(len(ORDERS)):
            begin = self.pieces(out, begin, part, range(1), sent)


def rest_kernel(n_owner, *refs):
    accs, (kept_away, sent_stay, kept_stay) = refs[:-3], refs[-3:]
    sums = Sums(n_owner, accs)
    sums.pieces_away(kept_away, sent=False)
    sums.pieces_stay(sent_stay, sent=True)
    sums.pieces_stay(kept_stay, sent=False)


def tiles_in_order(array):
    lead = array.shape[:-2]
    rows, cells = array.shape[-2:]
    array = array.reshape(lead + (rows // SUB, SUB, cells // LANES, LANES))
    return jnp.swapaxes(array, -3, -2).reshape(-1, LANES)


def accumulate(
    projections, images, transfer, pose_weights, pose_of, pose_blocks, pose_tiles,
    bank_size, n_owner,
):
    n_part, n_pose, n_tile, n_cell = projections.shape
    assert n_cell == SUB * LANES and n_pose == SUB and n_part % SUB == 0 and n_tile % UNROLL == 0 and UNROLL % N_BUF == 0
    n_row = n_owner * NB_DEV * bank_size * SUB
    n_acc = 4 if n_row * LANES * 4 <= 4 * MIB else 2
    projections = tiles_in_order(jnp.transpose(projections, (0, 2, 1, 3)))
    images = tiles_in_order(jnp.transpose(images, (1, 0, 2)))
    transfer = tiles_in_order(jnp.transpose(transfer, (1, 0, 2)))
    stay = functools.partial(pltpu.with_memory_space_constraint, memory_space=pltpu.HBM)
    hbm = pl.BlockSpec(memory_space=pltpu.HBM)
    vmem = pl.BlockSpec(memory_space=pltpu.VMEM)
    n_high = n_owner // 4
    a, d, b, e = (rows * SUB for rows in PART_ROWS)
    assert sum(PART_ROWS) == NB_DEV // 2 * bank_size

    away = 2 * n_high * (a + d + b) + 4 * (n_high - 1) * e

    def out(rows):
        return jax.ShapeDtypeStruct((rows, LANES), jnp.float32)

    sent_away, *accs = pl.pallas_call(
        functools.partial(accumulate_kernel, bank_size, n_owner, n_acc),
        out_shape=[out(away)] + [out(n_row)] * n_acc,
        in_specs=[hbm] * 7,
        out_specs=[vmem] * (1 + n_acc),
        scratch_shapes=[
            pltpu.VMEM(projections.shape, jnp.bfloat16),
            pltpu.VMEM(images.shape, jnp.bfloat16),
            pltpu.VMEM(transfer.shape, jnp.bfloat16),
            pltpu.SMEM((n_pose, n_part), jnp.float32),
            pltpu.VMEM((n_pose, n_part), jnp.int32),
            pltpu.VMEM(pose_blocks.shape[::-1], jnp.int32),
            pltpu.VMEM(pose_tiles.shape[::-1], jnp.int32),
            pltpu.VMEM((n_tile, n_part * n_pose), jnp.int32),
            pltpu.SMEM((n_tile, n_part * n_pose), jnp.int32),
            pltpu.VMEM(transfer.shape, jnp.float32),
            pltpu.VMEM(transfer.shape, jnp.float32),
        ]
        + [pltpu.VMEM((n_pose * SUB, LANES), jnp.float32)] * N_BUF
        + [
            pltpu.SemaphoreType.DMA((n_part,)),
            pltpu.SemaphoreType.DMA((3,)),
            pltpu.SemaphoreType.DMA((3,)),
            pltpu.SemaphoreType.DMA,
        ],
        compiler_params=pltpu.CompilerParams(vmem_limit_bytes=24 * MIB),
        name="accumulate",
    )(
        stay(projections), stay(images), stay(transfer),
        stay(pose_weights.T), stay(pose_of.T), stay(pose_blocks.T), stay(pose_tiles.T),
    )
    rows = 2 * n_high * (a + d + b) + 4 * e
    return sent_away, *in_vmem(functools.partial(rest_kernel, n_owner), "rest", [away, rows, rows], *accs)


def in_vmem(kernel, name, rows, *operands):
    vmem = pl.BlockSpec(memory_space=pltpu.VMEM)
    return pl.pallas_call(
        kernel,
        out_shape=[jax.ShapeDtypeStruct((n, LANES), jnp.float32) for n in rows],
        in_specs=[vmem] * len(operands),
        out_specs=[vmem] * len(rows),
        compiler_params=pltpu.CompilerParams(vmem_limit_bytes=32 * MIB),
        name=name,
    )(*operands)


def first_kernel(kept, got, *to):
    begin = 0
    for out in to:
        rows = slice(begin, begin + out.shape[0])
        out[...] = kept[rows, :] + got[rows, :]
        begin += out.shape[0]


def second_kernel(n_high, kept, got, got_y, got_l, *rest):
    got_h, (own_a, own_d, own_b, own_e, to_y, to_l, *to_h) = rest[: n_high - 1], rest[n_high - 1 :]
    a, d, b, e = (rows * SUB for rows in PART_ROWS)

    def put(out, at, begin, size, *arrivals):
        total = kept[begin : begin + size, :] + got[begin : begin + size, :]
        for array, first in arrivals:
            total += array[first : first + size, :]
        out[at : at + size, :] = total

    n = n_high * a
    put(own_a, 0, 0, n, (got_y, 0))
    put(to_l, 0, n, n, (got_y, n))
    begin, y_begin = 2 * n, 2 * n
    put(own_d, 0, begin, 2 * d, (got_y, y_begin))
    for i, out in enumerate(to_h):
        put(out, 0, begin + 2 * d * (i + 1), 2 * d, (got_y, y_begin + 2 * d * (i + 1)))
    begin, n = begin + 2 * n_high * d, n_high * b
    put(own_b, 0, begin, n, (got_l, 0))
    put(to_y, 0, begin + n, n, (got_l, n))
    begin += 2 * n
    put(own_e, 0, begin, 2 * e, *[(array, 0) for array in got_h])
    put(to_y, n, begin + 2 * e, 2 * e, *[(array, 2 * e) for array in got_h])


def third_kernel(n_high, own_a, own_d, own_b, own_e, got_y, got_l, *rest):
    got_h, (own, to_l, *to_h) = rest[: n_high - 1], rest[n_high - 1 :]
    a, d, b, e = (rows * SUB for rows in PART_ROWS)

    def put(out, at, source, begin, size, *arrivals):
        total = source[begin : begin + size, :]
        for array, first in arrivals:
            total += array[first : first + size, :]
        out[at : at + size, :] = total

    put(own, 0, own_a, 0, a, (got_l, 0))
    put(own, a, own_d, 0, d, *[(array, 0) for array in got_h])
    put(own, a + d, own_b, 0, b, (got_y, 0))
    put(own, a + d + b, own_e, 0, e, (got_y, n_high * b))
    put(to_l, 0, own_d, d, d, *[(array, d) for array in got_h])
    put(to_l, d, own_e, e, e, (got_y, n_high * b + e))
    for i, out in enumerate(to_h):
        put(out, 0, own_a, (i + 1) * a, a, (got_l, (i + 1) * a))
        put(out, a, own_b, (i + 1) * b, b, (got_y, (i + 1) * b))


def last_kernel(before, got_l, *rest):
    got_h, (own,) = rest[:-1], rest[-1:]
    a, d, b, e = (rows * SUB for rows in PART_ROWS)
    for at, size, arrivals in (
        (0, a, [(array, 0) for array in got_h]),
        (a, d, [(got_l, 0)]),
        (a + d, b, [(array, a) for array in got_h]),
        (a + d + b, e, [(got_l, d)]),
    ):
        total = before[at : at + size, :]
        for array, first in arrivals:
            total += array[first : first + size, :]
        own[at : at + size, :] = total


def bank_kernel(own, other, bank, out):
    bank_size, n_z, n_cell = bank.shape
    n_half = out.shape[0] // 2
    group = 2 * SUB

    def apply(halves):
        for c in range(n_cell // LANES):
            cols = slice(c * LANES, (c + 1) * LANES)

            @pl.loop(0, n_z // group)
            def _(g):
                rows = pl.ds(pl.multiple_of(g * group, group), group)
                weights = [bank[t, rows, cols] for t in range(bank_size)]
                for b in range(2 * n_half):
                    total = None
                    for t in range(bank_size):
                        value = weights[t] * halves[b // n_half][b % n_half, t, c : c + 1, :]
                        total = value if total is None else total + value
                    out[b, rows, cols] = total

    rep = position()[0]

    @pl.when(rep == 0)
    def _():
        apply((own, other))

    @pl.when(rep == 1)
    def _():
        apply((other, own))


def apply_bank(own, other, weight_bank):
    bank_size, n_z, n_cell = weight_bank.shape
    vmem = pl.BlockSpec(memory_space=pltpu.VMEM)
    own, other = [array.reshape(NB_DEV // 2, bank_size, SUB, LANES) for array in (own, other)]
    return pl.pallas_call(
        bank_kernel,
        out_shape=jax.ShapeDtypeStruct((NB_DEV, n_z, n_cell), jnp.float32),
        in_specs=[vmem] * 3,
        out_specs=vmem,
        compiler_params=pltpu.CompilerParams(vmem_limit_bytes=32 * MIB),
        name="apply_bank",
    )(own, other, weight_bank)


def body(
    projections, images, transfer, pose_weights, pose_of, pose_blocks, pose_tiles, weight_bank
):
    bank_size = weight_bank.shape[0]
    n_blk = lax.axis_size("blk")
    n_high = n_blk // 4
    sent_away, kept_away, sent_stay, kept_stay = accumulate(
        projections, images, transfer, pose_weights, pose_of, pose_blocks, pose_tiles,
        bank_size, n_blk,
    )
    a, d, b, e = (rows * SUB for rows in PART_ROWS)

    def over_rep(array):
        return lax.ppermute(array, "rep", [(0, 1), (1, 0)])

    def over_blk(array, bits):
        return lax.ppermute(array, "blk", [(i, i ^ bits) for i in range(n_blk)])

    def over_h(arrays):
        return [over_blk(array, 4 * (i + 1)) for i, array in enumerate(arrays)]

    n_h = n_high - 1
    got_away, got_stay = over_rep(sent_away), over_rep(sent_stay)
    to_y, to_l, *to_h = in_vmem(
        first_kernel, "first", [2 * n_high * (a + d), 2 * n_high * b] + [4 * e] * n_h, kept_away, got_away
    )
    got_y, got_l, got_h = over_blk(to_y, 1), over_blk(to_l, 2), over_h(to_h)
    own_a, own_d, own_b, own_e, to_y, to_l, *to_h = in_vmem(
        functools.partial(second_kernel, n_high), "second",
        [n_high * a, 2 * d, n_high * b, 2 * e, n_high * b + 2 * e, n_high * a] + [2 * d] * n_h,
        kept_stay, got_stay, got_y, got_l, *got_h,
    )
    got_y, got_l, got_h = over_blk(to_y, 1), over_blk(to_l, 2), over_h(to_h)
    own, to_l, *to_h = in_vmem(
        functools.partial(third_kernel, n_high), "third", [a + d + b + e, d + e] + [a + b] * n_h,
        own_a, own_d, own_b, own_e, got_y, got_l, *got_h,
    )
    got_l, got_h = over_blk(to_l, 2), over_h(to_h)
    (own,) = in_vmem(last_kernel, "last", [a + d + b + e], own, got_l, *got_h)
    return apply_bank(own, over_rep(own), weight_bank)


def solution(mesh):
    placed = (
        P(("groups", "blk", "rep"), None, None, None),
        P(("groups", "blk", "rep"), None, None),
        P(("groups", "blk", "rep"), None, None),
        P(("groups", "blk", "rep"), None),
        P(("groups", "blk", "rep"), None),
        P("groups", None),
        P("groups", None),
        P(),
    )
    return jax.shard_map(
        body,
        mesh=mesh,
        in_specs=placed,
        out_specs=P(("groups", "blk"), None, None),
        check_vma=False,
    )
```

```python
import functools

import jax
import jax.numpy as jnp
from jax import lax
from jax.experimental import pallas as pl
from jax.experimental.pallas import tpu as pltpu
from jax.sharding import PartitionSpec as P

NB_DEV = 8
LANES = 128
SUB = 8
MIB = 1 << 20
UNROLL = 12
N_BUF = 4
ORDERS = ("ylh", "yhl", "lyh", "hyl")
PART_ROWS = (16, 16, 16, 16)


def position():
    here = lax.axis_index("blk")
    return lax.axis_index("rep"), here & 1, (here >> 1) & 1, here >> 2


def accumulate_kernel(
    bank_size, n_owner, n_acc,
    proj_hbm, img_hbm, tra_hbm, w_hbm, pose_hbm, blocks_hbm, tiles_hbm,
    sent_away, kept_away, sent_stay, kept_stay, *rest,
):
    proj, img, tra, weight, pose, blocks, tiles, idx_v, idx_s, square, cross = rest[:11]
    parts, accs = rest[11 : 11 + N_BUF], rest[11 + N_BUF : 11 + N_BUF + n_acc]
    proj_sem, small_sem, table_sem, idx_sem = rest[11 + N_BUF + n_acc :]
    n_pose, n_part = pose.shape
    n_tile, n_table = blocks.shape
    n_row = accs[0].shape[0]
    tile_rows = SUB * SUB
    part_rows = n_tile * tile_rows

    table_copies = [
        pltpu.make_async_copy(src, dst, table_sem.at[i])
        for i, (src, dst) in enumerate(((pose_hbm, pose), (blocks_hbm, blocks), (tiles_hbm, tiles)))
    ]
    small_copies = [
        pltpu.make_async_copy(img_hbm, img, small_sem.at[0]),
        pltpu.make_async_copy(tra_hbm, tra, small_sem.at[1]),
        pltpu.make_async_copy(w_hbm, weight, small_sem.at[2]),
    ]
    for copy in table_copies + small_copies:
        copy.start()

    def proj_copy(p):
        rows = pl.ds(pl.multiple_of(p * part_rows, part_rows), part_rows)
        return pltpu.make_async_copy(proj_hbm.at[rows, :], proj.at[rows, :], proj_sem.at[p])

    for p in range(n_part):
        proj_copy(p).start()

    zero = jnp.zeros((8 * SUB, LANES), jnp.float32)

    @pl.loop(0, n_row // (8 * SUB))
    def _(i):
        rows = pl.ds(pl.multiple_of(i * (8 * SUB), 8 * SUB), 8 * SUB)
        for acc in accs:
            acc[rows, :] = zero

    for copy in table_copies:
        copy.wait()
    lane = lax.broadcasted_iota(jnp.int32, (n_pose, n_table), 1)
    chosen = jnp.concatenate(
        [(pose[:, p : p + 1] == lane).astype(jnp.float32) for p in range(n_part)], axis=0
    ).astype(jnp.bfloat16)

    def look_up(table):
        return lax.dot_general(
            table[...].astype(jnp.float32).astype(jnp.bfloat16), chosen,
            (((1,), (1,)), ((), ())), preferred_element_type=jnp.float32,
        )

    idx_v[...] = ((look_up(blocks) * bank_size + look_up(tiles)) * SUB).astype(jnp.int32)
    idx_copy = pltpu.make_async_copy(idx_v, idx_s, idx_sem)
    idx_copy.start()

    for copy in small_copies:
        copy.wait()

    @pl.loop(0, square.shape[0] // tile_rows)
    def _(i):
        rows = pl.ds(pl.multiple_of(i * tile_rows, tile_rows), tile_rows)
        t = tra[rows, :].astype(jnp.float32)
        square[rows, :] = t * t
        cross[rows, :] = t * img[rows, :].astype(jnp.float32)

    sublane = lax.broadcasted_iota(jnp.int32, (SUB, LANES), 0)
    bits = [(sublane & (1 << t)) != 0 for t in range(3)]

    def stage(p, j, part):
        first = pl.multiple_of((p * n_tile + j) * tile_rows, tile_rows)
        part[...] = proj[pl.ds(first, tile_rows), :].astype(jnp.float32)

    def staged(part):
        return [part[pl.ds(k, SUB, stride=SUB), :] for k in range(n_pose)]

    def rolled(p, j):
        first = (p * n_tile + j) * tile_rows
        cells = []
        for c in range(0, SUB, 2):
            pair = proj[pl.ds(pl.multiple_of(first + c * SUB, 2 * SUB), 2 * SUB), :].astype(jnp.float32)
            cells += [pair[:SUB], pair[SUB:]]
        cells = [pltpu.roll(x, c, 0) if c else x for c, x in enumerate(cells)]
        for t, bit in enumerate(bits):
            cells = [jnp.where(bit, cells[(i + (1 << t)) % SUB], cells[i]) for i in range(SUB)]
        return [pltpu.roll(cells[-k % SUB], SUB - k, 0) if k else cells[0] for k in range(n_pose)]

    def terms(p, j, cells, weights):
        cell = pl.ds((j * (n_part // SUB) + p // SUB) * tile_rows + p % SUB, SUB, stride=SUB)
        tt, ti = square[cell, :], cross[cell, :]
        return [(tt * cells[k] - ti) * weights[k] for k in range(n_pose)]

    def add_rows(p, j, values):
        for first in range(0, n_pose, n_acc):
            group = range(first, first + n_acc)
            rows = [pl.ds(pl.multiple_of(idx_s[j, p * n_pose + k], SUB), SUB) for k in group]
            old = [accs[i][rows[i], :] for i in range(n_acc)]
            for i, k in enumerate(group):
                accs[i][rows[i], :] = old[i] + values[k]

    idx_copy.wait()

    @pl.loop(0, n_part)
    def _(p):
        proj_copy(p).wait()
        weights = [jnp.full((SUB, LANES), weight[k, p], jnp.float32) for k in range(n_pose)]

        stage(p, 0, parts[0])
        stage(p, 1, parts[1])

        @pl.loop(0, n_tile, step=UNROLL, init_carry=tuple(terms(p, 0, staged(parts[0]), weights)))
        def _(j, values):
            def tile(u):
                return jnp.minimum(j + u, n_tile - 1) if u >= UNROLL else j + u

            for u in range(UNROLL):
                if (u + 2) % 3 != 2:
                    stage(p, tile(u + 2), parts[(u + 2) % N_BUF])
                cells = staged(parts[(u + 1) % N_BUF]) if (u + 1) % 3 != 2 else rolled(p, tile(u + 1))
                later = terms(p, tile(u + 1), cells, weights)
                add_rows(p, j + u, values)
                values = later
            return tuple(values)

    sums = Sums(n_owner, accs)
    sums.pieces_away(sent_away, sent=True)
    sums.pieces_away(kept_away, sent=False)
    sums.pieces_stay(sent_stay, sent=True)
    sums.pieces_stay(kept_stay, sent=False)


class Sums:
    def __init__(self, n_owner, accs):
        self.accs = accs
        self.half_rows = accs[0].shape[0] // (n_owner * 2)
        self.sizes = {"y": 2, "l": 2, "h": n_owner // 4}

    def pieces(self, out, begin, part, firsts, sent):
        rep, near, low, high = position()
        order = ORDERS[part]
        inner = self.sizes[order[1]] * self.sizes[order[2]]
        size = PART_ROWS[part] * SUB
        within = sum(PART_ROWS[:part]) * SUB
        half = 1 - rep if sent else rep

        @pl.loop(0, len(firsts) * inner)
        def _(i):
            off = {order[0]: firsts[0] + i // inner}
            off[order[1]] = i % inner // self.sizes[order[2]]
            off[order[2]] = i % self.sizes[order[2]]
            owner = ((high ^ off["h"]) * 2 + (low ^ off["l"])) * 2 + (near ^ off["y"])
            first = pl.multiple_of((owner * 2 + half) * self.half_rows + within, SUB)
            total = self.accs[0][pl.ds(first, size), :]
            for acc in self.accs[1:]:
                total += acc[pl.ds(first, size), :]
            out[pl.ds(pl.multiple_of(begin + i * size, SUB), size), :] = total

        return begin + len(firsts) * inner * size

    def pieces_away(self, out, sent):
        begin = 0
        for part, order in enumerate(ORDERS):
            begin = self.pieces(out, begin, part, range(1, self.sizes[order[0]]), sent)

    def pieces_stay(self, out, sent):
        begin = 0
        for part in range(len(ORDERS)):
            begin = self.pieces(out, begin, part, range(1), sent)


def tiles_in_order(array):
    lead = array.shape[:-2]
    rows, cells = array.shape[-2:]
    array = array.reshape(lead + (rows // SUB, SUB, cells // LANES, LANES))
    return jnp.swapaxes(array, -3, -2).reshape(-1, LANES)


def accumulate(
    projections, images, transfer, pose_weights, pose_of, pose_blocks, pose_tiles,
    bank_size, n_owner,
):
    n_part, n_pose, n_tile, n_cell = projections.shape
    assert n_cell == SUB * LANES and n_pose == SUB and n_part % SUB == 0 and n_tile % UNROLL == 0 and UNROLL % (3 * N_BUF) == 0
    n_row = n_owner * NB_DEV * bank_size * SUB
    n_acc = 4 if n_row * LANES * 4 <= 4 * MIB else 2
    projections = tiles_in_order(jnp.transpose(projections, (0, 2, 1, 3)))
    images = tiles_in_order(jnp.transpose(images, (1, 0, 2)))
    transfer = tiles_in_order(jnp.transpose(transfer, (1, 0, 2)))
    stay = functools.partial(pltpu.with_memory_space_constraint, memory_space=pltpu.HBM)
    hbm = pl.BlockSpec(memory_space=pltpu.HBM)
    vmem = pl.BlockSpec(memory_space=pltpu.VMEM)
    n_high = n_owner // 4
    a, d, b, e = (rows * SUB for rows in PART_ROWS)
    assert sum(PART_ROWS) == NB_DEV // 2 * bank_size

    away = 2 * n_high * (a + d + b) + 4 * (n_high - 1) * e
    stays = 2 * n_high * (a + d + b) + 4 * e

    def out(rows):
        return jax.ShapeDtypeStruct((rows, LANES), jnp.float32)

    return pl.pallas_call(
        functools.partial(accumulate_kernel, bank_size, n_owner, n_acc),
        out_shape=[out(away)] * 2 + [out(stays)] * 2,
        in_specs=[hbm] * 7,
        out_specs=[vmem] * 4,
        scratch_shapes=[
            pltpu.VMEM(projections.shape, jnp.bfloat16),
            pltpu.VMEM(images.shape, jnp.bfloat16),
            pltpu.VMEM(transfer.shape, jnp.bfloat16),
            pltpu.SMEM((n_pose, n_part), jnp.float32),
            pltpu.VMEM((n_pose, n_part), jnp.int32),
            pltpu.VMEM(pose_blocks.shape[::-1], jnp.int32),
            pltpu.VMEM(pose_tiles.shape[::-1], jnp.int32),
            pltpu.VMEM((n_tile, n_part * n_pose), jnp.int32),
            pltpu.SMEM((n_tile, n_part * n_pose), jnp.int32),
            pltpu.VMEM(transfer.shape, jnp.float32),
            pltpu.VMEM(transfer.shape, jnp.float32),
        ]
        + [pltpu.VMEM((n_pose * SUB, LANES), jnp.float32)] * N_BUF
        + [pltpu.VMEM((n_row, LANES), jnp.float32)] * n_acc
        + [
            pltpu.SemaphoreType.DMA((n_part,)),
            pltpu.SemaphoreType.DMA((3,)),
            pltpu.SemaphoreType.DMA((3,)),
            pltpu.SemaphoreType.DMA,
        ],
        compiler_params=pltpu.CompilerParams(vmem_limit_bytes=(40 if n_acc == 4 else 56) * MIB),
        name="accumulate",
    )(
        stay(projections), stay(images), stay(transfer),
        stay(pose_weights.T), stay(pose_of.T), stay(pose_blocks.T), stay(pose_tiles.T),
    )


def in_vmem(kernel, name, rows, *operands):
    vmem = pl.BlockSpec(memory_space=pltpu.VMEM)
    return pl.pallas_call(
        kernel,
        out_shape=[jax.ShapeDtypeStruct((n, LANES), jnp.float32) for n in rows],
        in_specs=[vmem] * len(operands),
        out_specs=[vmem] * len(rows),
        compiler_params=pltpu.CompilerParams(vmem_limit_bytes=32 * MIB),
        name=name,
    )(*operands)


def first_kernel(kept, got, *to):
    begin = 0
    for out in to:
        rows = slice(begin, begin + out.shape[0])
        out[...] = kept[rows, :] + got[rows, :]
        begin += out.shape[0]


def second_kernel(n_high, kept, got, got_y, got_l, *rest):
    got_h, (own_a, own_d, own_b, own_e, to_y, to_l, *to_h) = rest[: n_high - 1], rest[n_high - 1 :]
    a, d, b, e = (rows * SUB for rows in PART_ROWS)

    def put(out, at, begin, size, *arrivals):
        total = kept[begin : begin + size, :] + got[begin : begin + size, :]
        for array, first in arrivals:
            total += array[first : first + size, :]
        out[at : at + size, :] = total

    n = n_high * a
    put(own_a, 0, 0, n, (got_y, 0))
    put(to_l, 0, n, n, (got_y, n))
    begin, y_begin = 2 * n, 2 * n
    put(own_d, 0, begin, 2 * d, (got_y, y_begin))
    for i, out in enumerate(to_h):
        put(out, 0, begin + 2 * d * (i + 1), 2 * d, (got_y, y_begin + 2 * d * (i + 1)))
    begin, n = begin + 2 * n_high * d, n_high * b
    put(own_b, 0, begin, n, (got_l, 0))
    put(to_y, 0, begin + n, n, (got_l, n))
    begin += 2 * n
    put(own_e, 0, begin, 2 * e, *[(array, 0) for array in got_h])
    put(to_y, n, begin + 2 * e, 2 * e, *[(array, 2 * e) for array in got_h])


def third_kernel(n_high, own_a, own_d, own_b, own_e, got_y, got_l, *rest):
    got_h, (own, to_l, *to_h) = rest[: n_high - 1], rest[n_high - 1 :]
    a, d, b, e = (rows * SUB for rows in PART_ROWS)

    def put(out, at, source, begin, size, *arrivals):
        total = source[begin : begin + size, :]
        for array, first in arrivals:
            total += array[first : first + size, :]
        out[at : at + size, :] = total

    put(own, 0, own_a, 0, a, (got_l, 0))
    put(own, a, own_d, 0, d, *[(array, 0) for array in got_h])
    put(own, a + d, own_b, 0, b, (got_y, 0))
    put(own, a + d + b, own_e, 0, e, (got_y, n_high * b))
    put(to_l, 0, own_d, d, d, *[(array, d) for array in got_h])
    put(to_l, d, own_e, e, e, (got_y, n_high * b + e))
    for i, out in enumerate(to_h):
        put(out, 0, own_a, (i + 1) * a, a, (got_l, (i + 1) * a))
        put(out, a, own_b, (i + 1) * b, b, (got_y, (i + 1) * b))


def last_kernel(before, got_l, *rest):
    got_h, (own,) = rest[:-1], rest[-1:]
    a, d, b, e = (rows * SUB for rows in PART_ROWS)
    for at, size, arrivals in (
        (0, a, [(array, 0) for array in got_h]),
        (a, d, [(got_l, 0)]),
        (a + d, b, [(array, a) for array in got_h]),
        (a + d + b, e, [(got_l, d)]),
    ):
        total = before[at : at + size, :]
        for array, first in arrivals:
            total += array[first : first + size, :]
        own[at : at + size, :] = total


def bank_kernel(own, other, bank, out):
    bank_size, n_z, n_cell = bank.shape
    n_half = out.shape[0] // 2
    group = 2 * SUB

    def apply(halves):
        for c in range(n_cell // LANES):
            cols = slice(c * LANES, (c + 1) * LANES)

            @pl.loop(0, n_z // group)
            def _(g):
                rows = pl.ds(pl.multiple_of(g * group, group), group)
                weights = [bank[t, rows, cols] for t in range(bank_size)]
                for b in range(2 * n_half):
                    total = None
                    for t in range(bank_size):
                        value = weights[t] * halves[b // n_half][b % n_half, t, c : c + 1, :]
                        total = value if total is None else total + value
                    out[b, rows, cols] = total

    rep = position()[0]

    @pl.when(rep == 0)
    def _():
        apply((own, other))

    @pl.when(rep == 1)
    def _():
        apply((other, own))


def apply_bank(own, other, weight_bank):
    bank_size, n_z, n_cell = weight_bank.shape
    vmem = pl.BlockSpec(memory_space=pltpu.VMEM)
    own, other = [array.reshape(NB_DEV // 2, bank_size, SUB, LANES) for array in (own, other)]
    return pl.pallas_call(
        bank_kernel,
        out_shape=jax.ShapeDtypeStruct((NB_DEV, n_z, n_cell), jnp.float32),
        in_specs=[vmem] * 3,
        out_specs=vmem,
        compiler_params=pltpu.CompilerParams(vmem_limit_bytes=32 * MIB),
        name="apply_bank",
    )(own, other, weight_bank)


def body(
    projections, images, transfer, pose_weights, pose_of, pose_blocks, pose_tiles, weight_bank
):
    bank_size = weight_bank.shape[0]
    n_blk = lax.axis_size("blk")
    n_high = n_blk // 4
    sent_away, kept_away, sent_stay, kept_stay = accumulate(
        projections, images, transfer, pose_weights, pose_of, pose_blocks, pose_tiles,
        bank_size, n_blk,
    )
    a, d, b, e = (rows * SUB for rows in PART_ROWS)

    def over_rep(array):
        return lax.ppermute(array, "rep", [(0, 1), (1, 0)])

    def over_blk(array, bits):
        return lax.ppermute(array, "blk", [(i, i ^ bits) for i in range(n_blk)])

    def over_h(arrays):
        return [over_blk(array, 4 * (i + 1)) for i, array in enumerate(arrays)]

    n_h = n_high - 1
    got_away, got_stay = over_rep(sent_away), over_rep(sent_stay)
    to_y, to_l, *to_h = in_vmem(
        first_kernel, "first", [2 * n_high * (a + d), 2 * n_high * b] + [4 * e] * n_h, kept_away, got_away
    )
    got_y, got_l, got_h = over_blk(to_y, 1), over_blk(to_l, 2), over_h(to_h)
    own_a, own_d, own_b, own_e, to_y, to_l, *to_h = in_vmem(
        functools.partial(second_kernel, n_high), "second",
        [n_high * a, 2 * d, n_high * b, 2 * e, n_high * b + 2 * e, n_high * a] + [2 * d] * n_h,
        kept_stay, got_stay, got_y, got_l, *got_h,
    )
    got_y, got_l, got_h = over_blk(to_y, 1), over_blk(to_l, 2), over_h(to_h)
    own, to_l, *to_h = in_vmem(
        functools.partial(third_kernel, n_high), "third", [a + d + b + e, d + e] + [a + b] * n_h,
        own_a, own_d, own_b, own_e, got_y, got_l, *got_h,
    )
    got_l, got_h = over_blk(to_l, 2), over_h(to_h)
    (own,) = in_vmem(last_kernel, "last", [a + d + b + e], own, got_l, *got_h)
    return apply_bank(own, over_rep(own), weight_bank)


def solution(mesh):
    placed = (
        P(("groups", "blk", "rep"), None, None, None),
        P(("groups", "blk", "rep"), None, None),
        P(("groups", "blk", "rep"), None, None),
        P(("groups", "blk", "rep"), None),
        P(("groups", "blk", "rep"), None),
        P("groups", None),
        P("groups", None),
        P(),
    )
    return jax.shard_map(
        body,
        mesh=mesh,
        in_specs=placed,
        out_specs=P(("groups", "blk"), None, None),
        check_vma=False,
    )
```

```python
import functools

import jax
import jax.numpy as jnp
from jax import lax
from jax.experimental import pallas as pl
from jax.experimental.pallas import tpu as pltpu
from jax.sharding import PartitionSpec as P

NB_DEV = 8
LANES = 128
SUB = 8
MIB = 1 << 20
UNROLL = 12
N_BUF = 4
ORDERS = ("ylh", "yhl", "lyh", "hyl")
PART_ROWS = (16, 16, 16, 16)


def position():
    here = lax.axis_index("blk")
    return lax.axis_index("rep"), here & 1, (here >> 1) & 1, here >> 2


def accumulate_kernel(
    bank_size, n_owner, n_acc,
    proj_hbm, img_hbm, tra_hbm, w_hbm, pose_hbm, blocks_hbm, tiles_hbm,
    sent_away, *rest,
):
    accs, rest = rest[:n_acc], rest[n_acc:]
    proj, img, tra, weight, pose, blocks, tiles, idx_v, idx_s, square, cross = rest[:11]
    parts = rest[11 : 11 + N_BUF]
    proj_sem, small_sem, table_sem, idx_sem = rest[11 + N_BUF :]
    n_pose, n_part = pose.shape
    n_tile, n_table = blocks.shape
    n_row = accs[0].shape[0]
    tile_rows = SUB * SUB
    part_rows = n_tile * tile_rows

    table_copies = [
        pltpu.make_async_copy(src, dst, table_sem.at[i])
        for i, (src, dst) in enumerate(((pose_hbm, pose), (blocks_hbm, blocks), (tiles_hbm, tiles)))
    ]
    small_copies = [
        pltpu.make_async_copy(img_hbm, img, small_sem.at[0]),
        pltpu.make_async_copy(tra_hbm, tra, small_sem.at[1]),
        pltpu.make_async_copy(w_hbm, weight, small_sem.at[2]),
    ]
    for copy in table_copies + small_copies:
        copy.start()

    def proj_copy(p):
        rows = pl.ds(pl.multiple_of(p * part_rows, part_rows), part_rows)
        return pltpu.make_async_copy(proj_hbm.at[rows, :], proj.at[rows, :], proj_sem.at[p])

    for p in range(n_part):
        proj_copy(p).start()

    zero = jnp.zeros((8 * SUB, LANES), jnp.float32)

    @pl.loop(0, n_row // (8 * SUB))
    def _(i):
        rows = pl.ds(pl.multiple_of(i * (8 * SUB), 8 * SUB), 8 * SUB)
        for acc in accs:
            acc[rows, :] = zero

    for copy in table_copies:
        copy.wait()
    lane = lax.broadcasted_iota(jnp.int32, (n_pose, n_table), 1)
    chosen = jnp.concatenate(
        [(pose[:, p : p + 1] == lane).astype(jnp.float32) for p in range(n_part)], axis=0
    ).astype(jnp.bfloat16)

    def look_up(table):
        return lax.dot_general(
            table[...].astype(jnp.float32).astype(jnp.bfloat16), chosen,
            (((1,), (1,)), ((), ())), preferred_element_type=jnp.float32,
        )

    idx_v[...] = ((look_up(blocks) * bank_size + look_up(tiles)) * SUB).astype(jnp.int32)
    idx_copy = pltpu.make_async_copy(idx_v, idx_s, idx_sem)
    idx_copy.start()

    for copy in small_copies:
        copy.wait()

    @pl.loop(0, square.shape[0] // tile_rows)
    def _(i):
        rows = pl.ds(pl.multiple_of(i * tile_rows, tile_rows), tile_rows)
        t = tra[rows, :].astype(jnp.float32)
        square[rows, :] = t * t
        cross[rows, :] = t * img[rows, :].astype(jnp.float32)

    def stage(p, j, part):
        first = pl.multiple_of((p * n_tile + j) * tile_rows, tile_rows)
        part[...] = proj[pl.ds(first, tile_rows), :].astype(jnp.float32)

    def staged(part):
        return [part[pl.ds(k, SUB, stride=SUB), :] for k in range(n_pose)]

    def terms(p, j, cells, weights):
        cell = pl.ds((j * (n_part // SUB) + p // SUB) * tile_rows + p % SUB, SUB, stride=SUB)
        tt, ti = square[cell, :], cross[cell, :]
        return [(tt * cells[k] - ti) * weights[k] for k in range(n_pose)]

    def add_rows(p, j, values):
        for first in range(0, n_pose, n_acc):
            group = range(first, first + n_acc)
            rows = [pl.ds(pl.multiple_of(idx_s[j, p * n_pose + k], SUB), SUB) for k in group]
            old = [accs[i][rows[i], :] for i in range(n_acc)]
            for i, k in enumerate(group):
                accs[i][rows[i], :] = old[i] + values[k]

    idx_copy.wait()

    @pl.loop(0, n_part)
    def _(p):
        proj_copy(p).wait()
        weights = [jnp.full((SUB, LANES), weight[k, p], jnp.float32) for k in range(n_pose)]

        stage(p, 0, parts[0])
        stage(p, 1, parts[1])

        @pl.loop(0, n_tile, step=UNROLL, init_carry=tuple(terms(p, 0, staged(parts[0]), weights)))
        def _(j, values):
            def tile(u):
                return jnp.minimum(j + u, n_tile - 1) if u >= UNROLL else j + u

            for u in range(UNROLL):
                stage(p, tile(u + 2), parts[(u + 2) % N_BUF])
                later = terms(p, tile(u + 1), staged(parts[(u + 1) % N_BUF]), weights)
                add_rows(p, j + u, values)
                values = later
            return tuple(values)

    Sums(n_owner, accs).pieces_away(sent_away, sent=True)


class Sums:
    def __init__(self, n_owner, accs):
        self.accs = accs
        self.half_rows = accs[0].shape[0] // (n_owner * 2)
        self.sizes = {"y": 2, "l": 2, "h": n_owner // 4}

    def pieces(self, out, begin, part, firsts, sent):
        rep, near, low, high = position()
        order = ORDERS[part]
        inner = self.sizes[order[1]] * self.sizes[order[2]]
        size = PART_ROWS[part] * SUB
        within = sum(PART_ROWS[:part]) * SUB
        half = 1 - rep if sent else rep

        @pl.loop(0, len(firsts) * inner)
        def _(i):
            off = {order[0]: firsts[0] + i // inner}
            off[order[1]] = i % inner // self.sizes[order[2]]
            off[order[2]] = i % self.sizes[order[2]]
            owner = ((high ^ off["h"]) * 2 + (low ^ off["l"])) * 2 + (near ^ off["y"])
            first = pl.multiple_of((owner * 2 + half) * self.half_rows + within, SUB)
            total = self.accs[0][pl.ds(first, size), :]
            for acc in self.accs[1:]:
                total += acc[pl.ds(first, size), :]
            out[pl.ds(pl.multiple_of(begin + i * size, SUB), size), :] = total

        return begin + len(firsts) * inner * size

    def pieces_away(self, out, sent):
        begin = 0
        for part, order in enumerate(ORDERS):
            begin = self.pieces(out, begin, part, range(1, self.sizes[order[0]]), sent)

    def pieces_stay(self, out, sent):
        begin = 0
        for part in range(len(ORDERS)):
            begin = self.pieces(out, begin, part, range(1), sent)


def rest_kernel(n_owner, *refs):
    accs, (kept_away, sent_stay, kept_stay) = refs[:-3], refs[-3:]
    sums = Sums(n_owner, accs)
    sums.pieces_away(kept_away, sent=False)
    sums.pieces_stay(sent_stay, sent=True)
    sums.pieces_stay(kept_stay, sent=False)


def tiles_in_order(array):
    lead = array.shape[:-2]
    rows, cells = array.shape[-2:]
    array = array.reshape(lead + (rows // SUB, SUB, cells // LANES, LANES))
    return jnp.swapaxes(array, -3, -2).reshape(-1, LANES)


def accumulate(
    projections, images, transfer, pose_weights, pose_of, pose_blocks, pose_tiles,
    bank_size, n_owner,
):
    n_part, n_pose, n_tile, n_cell = projections.shape
    assert n_cell == SUB * LANES and n_pose == SUB and n_part % SUB == 0 and n_tile % UNROLL == 0 and UNROLL % N_BUF == 0
    n_row = n_owner * NB_DEV * bank_size * SUB
    n_acc = 4 if n_row * LANES * 4 <= 4 * MIB else 2
    projections = tiles_in_order(jnp.transpose(projections, (0, 2, 1, 3)))
    images = tiles_in_order(jnp.transpose(images, (1, 0, 2)))
    transfer = tiles_in_order(jnp.transpose(transfer, (1, 0, 2)))
    stay = functools.partial(pltpu.with_memory_space_constraint, memory_space=pltpu.HBM)
    hbm = pl.BlockSpec(memory_space=pltpu.HBM)
    vmem = pl.BlockSpec(memory_space=pltpu.VMEM)
    n_high = n_owner // 4
    a, d, b, e = (rows * SUB for rows in PART_ROWS)
    assert sum(PART_ROWS) == NB_DEV // 2 * bank_size

    away = 2 * n_high * (a + d + b) + 4 * (n_high - 1) * e

    def out(rows):
        return jax.ShapeDtypeStruct((rows, LANES), jnp.float32)

    sent_away, *accs = pl.pallas_call(
        functools.partial(accumulate_kernel, bank_size, n_owner, n_acc),
        out_shape=[out(away)] + [out(n_row)] * n_acc,
        in_specs=[hbm] * 7,
        out_specs=[vmem] * (1 + n_acc),
        scratch_shapes=[
            pltpu.VMEM(projections.shape, jnp.bfloat16),
            pltpu.VMEM(images.shape, jnp.bfloat16),
            pltpu.VMEM(transfer.shape, jnp.bfloat16),
            pltpu.SMEM((n_pose, n_part), jnp.float32),
            pltpu.VMEM((n_pose, n_part), jnp.int32),
            pltpu.VMEM(pose_blocks.shape[::-1], jnp.int32),
            pltpu.VMEM(pose_tiles.shape[::-1], jnp.int32),
            pltpu.VMEM((n_tile, n_part * n_pose), jnp.int32),
            pltpu.SMEM((n_tile, n_part * n_pose), jnp.int32),
            pltpu.VMEM(transfer.shape, jnp.float32),
            pltpu.VMEM(transfer.shape, jnp.float32),
        ]
        + [pltpu.VMEM((n_pose * SUB, LANES), jnp.float32)] * N_BUF
        + [
            pltpu.SemaphoreType.DMA((n_part,)),
            pltpu.SemaphoreType.DMA((3,)),
            pltpu.SemaphoreType.DMA((3,)),
            pltpu.SemaphoreType.DMA,
        ],
        compiler_params=pltpu.CompilerParams(vmem_limit_bytes=24 * MIB),
        name="accumulate",
    )(
        stay(projections), stay(images), stay(transfer),
        stay(pose_weights.T), stay(pose_of.T), stay(pose_blocks.T), stay(pose_tiles.T),
    )
    rows = 2 * n_high * (a + d + b) + 4 * e
    return sent_away, *in_vmem(functools.partial(rest_kernel, n_owner), "rest", [away, rows, rows], *accs)


def in_vmem(kernel, name, rows, *operands):
    vmem = pl.BlockSpec(memory_space=pltpu.VMEM)
    return pl.pallas_call(
        kernel,
        out_shape=[jax.ShapeDtypeStruct((n, LANES), jnp.float32) for n in rows],
        in_specs=[vmem] * len(operands),
        out_specs=[vmem] * len(rows),
        compiler_params=pltpu.CompilerParams(vmem_limit_bytes=32 * MIB),
        name=name,
    )(*operands)


def first_kernel(kept, got, *to):
    begin = 0
    for out in to:
        rows = slice(begin, begin + out.shape[0])
        out[...] = kept[rows, :] + got[rows, :]
        begin += out.shape[0]


def add_up(out, at, begin, size, *sources):
    total = None
    for array, offset in sources:
        value = array[offset + begin : offset + begin + size, :]
        total = value if total is None else total + value
    out[at : at + size, :] = total


def second_y_kernel(n_high, kept, got, got_y, own_a, own_d, to_l, *to_h):
    a, d, b, e = (rows * SUB for rows in PART_ROWS)
    sources = ((kept, 0), (got, 0), (got_y, 0))
    n = n_high * a
    add_up(to_l, 0, n, n, *sources)
    for i, out in enumerate(to_h):
        add_up(out, 0, 2 * n + 2 * d * (i + 1), 2 * d, *sources)
    add_up(own_a, 0, 0, n, *sources)
    add_up(own_d, 0, 2 * n, 2 * d, *sources)


def second_z_kernel(n_high, kept, got, got_l, *rest):
    got_h, (before, own_b, own_e, to_y) = rest[: n_high - 1], rest[n_high - 1 :]
    a, d, b, e = (rows * SUB for rows in PART_ROWS)
    begin, n = 2 * n_high * (a + d), n_high * b
    sources = ((kept, begin), (got, begin), (got_l, 0))
    add_up(to_y, 0, n, n, *sources)
    add_up(own_b, 0, 0, n, *sources)
    begin += 2 * n
    sources = ((kept, begin), (got, begin)) + tuple((array, 0) for array in got_h)
    add_up(to_y, n, 2 * e, 2 * e, *sources)
    add_up(own_e, 0, 0, 2 * e, *sources)


def third_kernel(size, sources, *refs):
    operands, outs = refs[: len(sources)], refs[len(sources) :]
    for i, out in enumerate(outs):
        add_up(out, 0, i * size, size, *[(array, offset) for array, offset in zip(operands, sources)])


def last_kernel(n_high, own_a, own_d, own_b, own_e, got_d, got_e, *rest):
    got_a, got_b, own = rest[: n_high - 1], rest[n_high - 1 : -1], rest[-1]
    at = 0
    for mine, arrivals in ((own_a, got_a), (own_d, (got_d,)), (own_b, got_b), (own_e, (got_e,))):
        size = mine.shape[0]
        add_up(own, at, 0, size, (mine, 0), *[(array, 0) for array in arrivals])
        at += size


def bank_kernel(own, other, bank, out):
    bank_size, n_z, n_cell = bank.shape
    n_half = out.shape[0] // 2
    group = 2 * SUB

    def apply(halves):
        for c in range(n_cell // LANES):
            cols = slice(c * LANES, (c + 1) * LANES)

            @pl.loop(0, n_z // group)
            def _(g):
                rows = pl.ds(pl.multiple_of(g * group, group), group)
                weights = [bank[t, rows, cols] for t in range(bank_size)]
                for b in range(2 * n_half):
                    total = None
                    for t in range(bank_size):
                        value = weights[t] * halves[b // n_half][b % n_half, t, c : c + 1, :]
                        total = value if total is None else total + value
                    out[b, rows, cols] = total

    rep = position()[0]

    @pl.when(rep == 0)
    def _():
        apply((own, other))

    @pl.when(rep == 1)
    def _():
        apply((other, own))


def apply_bank(own, other, weight_bank):
    bank_size, n_z, n_cell = weight_bank.shape
    vmem = pl.BlockSpec(memory_space=pltpu.VMEM)
    own, other = [array.reshape(NB_DEV // 2, bank_size, SUB, LANES) for array in (own, other)]
    return pl.pallas_call(
        bank_kernel,
        out_shape=jax.ShapeDtypeStruct((NB_DEV, n_z, n_cell), jnp.float32),
        in_specs=[vmem] * 3,
        out_specs=vmem,
        compiler_params=pltpu.CompilerParams(vmem_limit_bytes=32 * MIB),
        name="apply_bank",
    )(own, other, weight_bank)


def body(
    projections, images, transfer, pose_weights, pose_of, pose_blocks, pose_tiles, weight_bank
):
    bank_size = weight_bank.shape[0]
    n_blk = lax.axis_size("blk")
    n_high = n_blk // 4
    sent_away, kept_away, sent_stay, kept_stay = accumulate(
        projections, images, transfer, pose_weights, pose_of, pose_blocks, pose_tiles,
        bank_size, n_blk,
    )
    a, d, b, e = (rows * SUB for rows in PART_ROWS)

    def over_rep(array):
        return lax.ppermute(array, "rep", [(0, 1), (1, 0)])

    def over_blk(array, bits):
        return lax.ppermute(array, "blk", [(i, i ^ bits) for i in range(n_blk)])

    def over_h(arrays):
        return [over_blk(array, 4 * (i + 1)) for i, array in enumerate(arrays)]

    n_h = n_high - 1
    got_away, got_stay = over_rep(sent_away), over_rep(sent_stay)
    to_y, to_l, *to_h = in_vmem(
        first_kernel, "first", [2 * n_high * (a + d), 2 * n_high * b] + [4 * e] * n_h, kept_away, got_away
    )
    got_y, got_l, got_h = over_blk(to_y, 1), over_blk(to_l, 2), over_h(to_h)
    own_a, own_d, to_l, *to_h = in_vmem(
        functools.partial(second_y_kernel, n_high), "second_y",
        [n_high * a, 2 * d, n_high * a] + [2 * d] * n_h, kept_stay, got_stay, got_y,
    )
    next_l, next_h = over_blk(to_l, 2), over_h(to_h)

    def third(name, size, count, *sources):
        kernel = functools.partial(third_kernel, size, [offset for _, offset in sources])
        return in_vmem(kernel, name, [size] * count, *[array for array, _ in sources])

    own_a, *to_h = third("third_a", a, n_high, (own_a, 0), (next_l, 0))
    last_a = over_h(to_h)
    own_b, own_e, to_y = in_vmem(
        functools.partial(second_z_kernel, n_high), "second_z",
        [n_high * b, 2 * e, n_high * b + 2 * e], kept_stay, got_stay, got_l, *got_h, own_a,
    )
    next_y = over_blk(to_y, 1)

    own_d, to_l = third("third_d", d, 2, (own_d, 0), *[(array, 0) for array in next_h])
    last_d = over_blk(to_l, 2)
    own_b, *to_h = third("third_b", b, n_high, (own_b, 0), (next_y, 0))
    last_b = over_h(to_h)
    own_e, to_l = third("third_e", e, 2, (own_e, 0), (next_y, n_high * b))
    last_e = over_blk(to_l, 2)
    (own,) = in_vmem(
        functools.partial(last_kernel, n_high), "last", [a + d + b + e],
        own_a, own_d, own_b, own_e, last_d, last_e, *last_a, *last_b,
    )
    return apply_bank(own, over_rep(own), weight_bank)


def solution(mesh):
    placed = (
        P(("groups", "blk", "rep"), None, None, None),
        P(("groups", "blk", "rep"), None, None),
        P(("groups", "blk", "rep"), None, None),
        P(("groups", "blk", "rep"), None),
        P(("groups", "blk", "rep"), None),
        P("groups", None),
        P("groups", None),
        P(),
    )
    return jax.shard_map(
        body,
        mesh=mesh,
        in_specs=placed,
        out_specs=P(("groups", "blk"), None, None),
        check_vma=False,
    )
```

```python
import functools

import jax
import jax.numpy as jnp
from jax import lax
from jax.experimental import pallas as pl
from jax.experimental.pallas import tpu as pltpu
from jax.sharding import PartitionSpec as P

NB_DEV = 8
LANES = 128
SUB = 8
MIB = 1 << 20
UNROLL = 12
N_BUF = 4
ORDERS = ("ylh", "yhl", "lyh", "hyl")
PART_ROWS = (16, 16, 16, 16)


def position():
    here = lax.axis_index("blk")
    return lax.axis_index("rep"), here & 1, (here >> 1) & 1, here >> 2


def accumulate_kernel(
    bank_size, n_owner, n_acc,
    proj_hbm, img_hbm, tra_hbm, w_hbm, pose_hbm, blocks_hbm, tiles_hbm,
    sent_away, kept_away, sent_stay, kept_stay, *rest,
):
    proj, img, tra, weight, pose, blocks, tiles, idx_v, idx_s, square, cross = rest[:11]
    parts, accs = rest[11 : 11 + N_BUF], rest[11 + N_BUF : 11 + N_BUF + n_acc]
    proj_sem, small_sem, table_sem, idx_sem = rest[11 + N_BUF + n_acc :]
    n_pose, n_part = pose.shape
    n_tile, n_table = blocks.shape
    n_row = accs[0].shape[0]
    tile_rows = SUB * SUB
    part_rows = n_tile * tile_rows

    table_copies = [
        pltpu.make_async_copy(src, dst, table_sem.at[i])
        for i, (src, dst) in enumerate(((pose_hbm, pose), (blocks_hbm, blocks), (tiles_hbm, tiles)))
    ]
    small_copies = [
        pltpu.make_async_copy(img_hbm, img, small_sem.at[0]),
        pltpu.make_async_copy(tra_hbm, tra, small_sem.at[1]),
        pltpu.make_async_copy(w_hbm, weight, small_sem.at[2]),
    ]
    for copy in table_copies + small_copies:
        copy.start()

    def proj_copy(p):
        rows = pl.ds(pl.multiple_of(p * part_rows, part_rows), part_rows)
        return pltpu.make_async_copy(proj_hbm.at[rows, :], proj.at[rows, :], proj_sem.at[p])

    for p in range(n_part):
        proj_copy(p).start()

    zero = jnp.zeros((8 * SUB, LANES), jnp.float32)

    @pl.loop(0, n_row // (8 * SUB))
    def _(i):
        rows = pl.ds(pl.multiple_of(i * (8 * SUB), 8 * SUB), 8 * SUB)
        for acc in accs:
            acc[rows, :] = zero

    for copy in table_copies:
        copy.wait()
    lane = lax.broadcasted_iota(jnp.int32, (n_pose, n_table), 1)
    chosen = jnp.concatenate(
        [(pose[:, p : p + 1] == lane).astype(jnp.float32) for p in range(n_part)], axis=0
    ).astype(jnp.bfloat16)

    def look_up(table):
        return lax.dot_general(
            table[...].astype(jnp.float32).astype(jnp.bfloat16), chosen,
            (((1,), (1,)), ((), ())), preferred_element_type=jnp.float32,
        )

    idx_v[...] = ((look_up(blocks) * bank_size + look_up(tiles)) * SUB).astype(jnp.int32)
    idx_copy = pltpu.make_async_copy(idx_v, idx_s, idx_sem)
    idx_copy.start()

    for copy in small_copies:
        copy.wait()

    @pl.loop(0, square.shape[0] // tile_rows)
    def _(i):
        rows = pl.ds(pl.multiple_of(i * tile_rows, tile_rows), tile_rows)
        t = tra[rows, :].astype(jnp.float32)
        square[rows, :] = t * t
        cross[rows, :] = t * img[rows, :].astype(jnp.float32)

    def stage(p, j, part):
        first = pl.multiple_of((p * n_tile + j) * tile_rows, tile_rows)
        part[...] = proj[pl.ds(first, tile_rows), :].astype(jnp.float32)

    def staged(part):
        return [part[pl.ds(k, SUB, stride=SUB), :] for k in range(n_pose)]

    def terms(p, j, cells, weights):
        cell = pl.ds((j * (n_part // SUB) + p // SUB) * tile_rows + p % SUB, SUB, stride=SUB)
        tt, ti = square[cell, :], cross[cell, :]
        return [(tt * cells[k] - ti) * weights[k] for k in range(n_pose)]

    def add_rows(p, j, values):
        for first in range(0, n_pose, n_acc):
            group = range(first, first + n_acc)
            rows = [pl.ds(pl.multiple_of(idx_s[j, p * n_pose + k], SUB), SUB) for k in group]
            old = [accs[i][rows[i], :] for i in range(n_acc)]
            for i, k in enumerate(group):
                accs[i][rows[i], :] = old[i] + values[k]

    idx_copy.wait()

    def spread(p):
        return [jnp.full((SUB, LANES), weight[k, p], jnp.float32) for k in range(n_pose)]

    proj_copy(0).wait()
    stage(0, 0, parts[0])
    stage(0, 1, parts[1])

    @pl.loop(0, n_part, init_carry=tuple(terms(0, 0, staged(parts[0]), spread(0))))
    def _(p, carry):
        @pl.when(p + 1 < n_part)
        def _():
            proj_copy(p + 1).wait()

        weights = spread(p)

        @pl.loop(0, n_tile, step=UNROLL, init_carry=carry)
        def done(j, values):
            ends = j + UNROLL == n_tile
            next_p = jnp.where(ends, jnp.minimum(p + 1, n_part - 1), p)
            next_j = jnp.where(ends, 0, j + UNROLL)

            def tile(u):
                return (p, j + u) if u < UNROLL else (next_p, next_j + u - UNROLL)

            for u in range(UNROLL):
                stage(*tile(u + 2), parts[(u + 2) % N_BUF])
                scale = weights if u + 1 < UNROLL else spread(next_p)
                later = terms(*tile(u + 1), staged(parts[(u + 1) % N_BUF]), scale)
                add_rows(p, j + u, values)
                values = later
            return tuple(values)

        return done

    sums = Sums(n_owner, accs)
    sums.pieces_away(sent_away, sent=True)
    sums.pieces_away(kept_away, sent=False)
    sums.pieces_stay(sent_stay, sent=True)
    sums.pieces_stay(kept_stay, sent=False)


class Sums:
    def __init__(self, n_owner, accs):
        self.accs = accs
        self.half_rows = accs[0].shape[0] // (n_owner * 2)
        self.sizes = {"y": 2, "l": 2, "h": n_owner // 4}

    def pieces(self, out, begin, part, firsts, sent):
        rep, near, low, high = position()
        order = ORDERS[part]
        inner = self.sizes[order[1]] * self.sizes[order[2]]
        size = PART_ROWS[part] * SUB
        within = sum(PART_ROWS[:part]) * SUB
        half = 1 - rep if sent else rep

        @pl.loop(0, len(firsts) * inner)
        def _(i):
            off = {order[0]: firsts[0] + i // inner}
            off[order[1]] = i % inner // self.sizes[order[2]]
            off[order[2]] = i % self.sizes[order[2]]
            owner = ((high ^ off["h"]) * 2 + (low ^ off["l"])) * 2 + (near ^ off["y"])
            first = pl.multiple_of((owner * 2 + half) * self.half_rows + within, SUB)
            total = self.accs[0][pl.ds(first, size), :]
            for acc in self.accs[1:]:
                total += acc[pl.ds(first, size), :]
            out[pl.ds(pl.multiple_of(begin + i * size, SUB), size), :] = total

        return begin + len(firsts) * inner * size

    def pieces_away(self, out, sent):
        begin = 0
        for part, order in enumerate(ORDERS):
            begin = self.pieces(out, begin, part, range(1, self.sizes[order[0]]), sent)

    def pieces_stay(self, out, sent):
        begin = 0
        for part in range(len(ORDERS)):
            begin = self.pieces(out, begin, part, range(1), sent)


def tiles_in_order(array):
    lead = array.shape[:-2]
    rows, cells = array.shape[-2:]
    array = array.reshape(lead + (rows // SUB, SUB, cells // LANES, LANES))
    return jnp.swapaxes(array, -3, -2).reshape(-1, LANES)


def accumulate(
    projections, images, transfer, pose_weights, pose_of, pose_blocks, pose_tiles,
    bank_size, n_owner,
):
    n_part, n_pose, n_tile, n_cell = projections.shape
    assert n_cell == SUB * LANES and n_pose == SUB and n_part % SUB == 0 and n_tile % UNROLL == 0 and UNROLL % N_BUF == 0
    n_row = n_owner * NB_DEV * bank_size * SUB
    n_acc = 4 if n_row * LANES * 4 <= 4 * MIB else 2
    projections = tiles_in_order(jnp.transpose(projections, (0, 2, 1, 3)))
    images = tiles_in_order(jnp.transpose(images, (1, 0, 2)))
    transfer = tiles_in_order(jnp.transpose(transfer, (1, 0, 2)))
    stay = functools.partial(pltpu.with_memory_space_constraint, memory_space=pltpu.HBM)
    hbm = pl.BlockSpec(memory_space=pltpu.HBM)
    vmem = pl.BlockSpec(memory_space=pltpu.VMEM)
    n_high = n_owner // 4
    a, d, b, e = (rows * SUB for rows in PART_ROWS)
    assert sum(PART_ROWS) == NB_DEV // 2 * bank_size

    away = 2 * n_high * (a + d + b) + 4 * (n_high - 1) * e
    stays = 2 * n_high * (a + d + b) + 4 * e

    def out(rows):
        return jax.ShapeDtypeStruct((rows, LANES), jnp.float32)

    return pl.pallas_call(
        functools.partial(accumulate_kernel, bank_size, n_owner, n_acc),
        out_shape=[out(away)] * 2 + [out(stays)] * 2,
        in_specs=[hbm] * 7,
        out_specs=[vmem] * 4,
        scratch_shapes=[
            pltpu.VMEM(projections.shape, jnp.bfloat16),
            pltpu.VMEM(images.shape, jnp.bfloat16),
            pltpu.VMEM(transfer.shape, jnp.bfloat16),
            pltpu.SMEM((n_pose, n_part), jnp.float32),
            pltpu.VMEM((n_pose, n_part), jnp.int32),
            pltpu.VMEM(pose_blocks.shape[::-1], jnp.int32),
            pltpu.VMEM(pose_tiles.shape[::-1], jnp.int32),
            pltpu.VMEM((n_tile, n_part * n_pose), jnp.int32),
            pltpu.SMEM((n_tile, n_part * n_pose), jnp.int32),
            pltpu.VMEM(transfer.shape, jnp.float32),
            pltpu.VMEM(transfer.shape, jnp.float32),
        ]
        + [pltpu.VMEM((n_pose * SUB, LANES), jnp.float32)] * N_BUF
        + [pltpu.VMEM((n_row, LANES), jnp.float32)] * n_acc
        + [
            pltpu.SemaphoreType.DMA((n_part,)),
            pltpu.SemaphoreType.DMA((3,)),
            pltpu.SemaphoreType.DMA((3,)),
            pltpu.SemaphoreType.DMA,
        ],
        compiler_params=pltpu.CompilerParams(vmem_limit_bytes=(40 if n_acc == 4 else 56) * MIB),
        name="accumulate",
    )(
        stay(projections), stay(images), stay(transfer),
        stay(pose_weights.T), stay(pose_of.T), stay(pose_blocks.T), stay(pose_tiles.T),
    )


def in_vmem(kernel, name, rows, *operands):
    vmem = pl.BlockSpec(memory_space=pltpu.VMEM)
    return pl.pallas_call(
        kernel,
        out_shape=[jax.ShapeDtypeStruct((n, LANES), jnp.float32) for n in rows],
        in_specs=[vmem] * len(operands),
        out_specs=[vmem] * len(rows),
        compiler_params=pltpu.CompilerParams(vmem_limit_bytes=32 * MIB),
        name=name,
    )(*operands)


def first_kernel(kept, got, *to):
    begin = 0
    for out in to:
        rows = slice(begin, begin + out.shape[0])
        out[...] = kept[rows, :] + got[rows, :]
        begin += out.shape[0]


def second_kernel(n_high, kept, got, got_y, got_l, *rest):
    got_h, (own_a, own_d, own_b, own_e, to_y, to_l, *to_h) = rest[: n_high - 1], rest[n_high - 1 :]
    a, d, b, e = (rows * SUB for rows in PART_ROWS)

    def put(out, at, begin, size, *arrivals):
        total = kept[begin : begin + size, :] + got[begin : begin + size, :]
        for array, first in arrivals:
            total += array[first : first + size, :]
        out[at : at + size, :] = total

    n = n_high * a
    put(own_a, 0, 0, n, (got_y, 0))
    put(to_l, 0, n, n, (got_y, n))
    begin, y_begin = 2 * n, 2 * n
    put(own_d, 0, begin, 2 * d, (got_y, y_begin))
    for i, out in enumerate(to_h):
        put(out, 0, begin + 2 * d * (i + 1), 2 * d, (got_y, y_begin + 2 * d * (i + 1)))
    begin, n = begin + 2 * n_high * d, n_high * b
    put(own_b, 0, begin, n, (got_l, 0))
    put(to_y, 0, begin + n, n, (got_l, n))
    begin += 2 * n
    put(own_e, 0, begin, 2 * e, *[(array, 0) for array in got_h])
    put(to_y, n, begin + 2 * e, 2 * e, *[(array, 2 * e) for array in got_h])


def third_kernel(n_high, own_a, own_d, own_b, own_e, got_y, got_l, *rest):
    got_h, (own, to_l, *to_h) = rest[: n_high - 1], rest[n_high - 1 :]
    a, d, b, e = (rows * SUB for rows in PART_ROWS)

    def put(out, at, source, begin, size, *arrivals):
        total = source[begin : begin + size, :]
        for array, first in arrivals:
            total += array[first : first + size, :]
        out[at : at + size, :] = total

    put(own, 0, own_a, 0, a, (got_l, 0))
    put(own, a, own_d, 0, d, *[(array, 0) for array in got_h])
    put(own, a + d, own_b, 0, b, (got_y, 0))
    put(own, a + d + b, own_e, 0, e, (got_y, n_high * b))
    put(to_l, 0, own_d, d, d, *[(array, d) for array in got_h])
    put(to_l, d, own_e, e, e, (got_y, n_high * b + e))
    for i, out in enumerate(to_h):
        put(out, 0, own_a, (i + 1) * a, a, (got_l, (i + 1) * a))
        put(out, a, own_b, (i + 1) * b, b, (got_y, (i + 1) * b))


def last_kernel(before, got_l, *rest):
    got_h, (own,) = rest[:-1], rest[-1:]
    a, d, b, e = (rows * SUB for rows in PART_ROWS)
    for at, size, arrivals in (
        (0, a, [(array, 0) for array in got_h]),
        (a, d, [(got_l, 0)]),
        (a + d, b, [(array, a) for array in got_h]),
        (a + d + b, e, [(got_l, d)]),
    ):
        total = before[at : at + size, :]
        for array, first in arrivals:
            total += array[first : first + size, :]
        own[at : at + size, :] = total


def weigh(source, bank, out):
    bank_size, n_z, n_cell = bank.shape
    group = 2 * SUB

    for c in range(n_cell // LANES):
        cols = slice(c * LANES, (c + 1) * LANES)

        @pl.loop(0, n_z // group)
        def _(g):
            rows = pl.ds(pl.multiple_of(g * group, group), group)
            weights = [bank[t, rows, cols] for t in range(bank_size)]
            for b in range(out.shape[0]):
                total = None
                for t in range(bank_size):
                    value = weights[t] * source[b, t, c : c + 1, :]
                    total = value if total is None else total + value
                out[b, rows, cols] = total


def bank_rest_kernel(done, other, bank, out_hbm, block, sem):
    n_half = block.shape[0]
    rep = position()[0]
    first = pltpu.make_async_copy(done, out_hbm.at[pl.ds(rep * n_half, n_half)], sem.at[0])
    first.start()
    weigh(other, bank, block)
    second = pltpu.make_async_copy(block, out_hbm.at[pl.ds((1 - rep) * n_half, n_half)], sem.at[1])
    second.start()
    first.wait()
    second.wait()


def apply_bank(own, other, weight_bank):
    bank_size, n_z, n_cell = weight_bank.shape
    n_half = NB_DEV // 2
    vmem = pl.BlockSpec(memory_space=pltpu.VMEM)
    own, other = [array.reshape(n_half, bank_size, SUB, LANES) for array in (own, other)]
    params = pltpu.CompilerParams(vmem_limit_bytes=32 * MIB)
    done = pl.pallas_call(
        weigh,
        out_shape=jax.ShapeDtypeStruct((n_half, n_z, n_cell), jnp.float32),
        in_specs=[vmem] * 2,
        out_specs=vmem,
        compiler_params=params,
        name="bank_own",
    )(own, weight_bank)
    return pl.pallas_call(
        bank_rest_kernel,
        out_shape=jax.ShapeDtypeStruct((NB_DEV, n_z, n_cell), jnp.float32),
        in_specs=[vmem] * 3,
        out_specs=pl.BlockSpec(memory_space=pl.ANY),
        scratch_shapes=[
            pltpu.VMEM((n_half, n_z, n_cell), jnp.float32),
            pltpu.SemaphoreType.DMA((2,)),
        ],
        compiler_params=params,
        name="bank_rest",
    )(done, other, weight_bank)


def body(
    projections, images, transfer, pose_weights, pose_of, pose_blocks, pose_tiles, weight_bank
):
    bank_size = weight_bank.shape[0]
    n_blk = lax.axis_size("blk")
    n_high = n_blk // 4
    sent_away, kept_away, sent_stay, kept_stay = accumulate(
        projections, images, transfer, pose_weights, pose_of, pose_blocks, pose_tiles,
        bank_size, n_blk,
    )
    a, d, b, e = (rows * SUB for rows in PART_ROWS)

    def over_rep(array):
        return lax.ppermute(array, "rep", [(0, 1), (1, 0)])

    def over_blk(array, bits):
        return lax.ppermute(array, "blk", [(i, i ^ bits) for i in range(n_blk)])

    def over_h(arrays):
        return [over_blk(array, 4 * (i + 1)) for i, array in enumerate(arrays)]

    n_h = n_high - 1
    got_away, got_stay = over_rep(sent_away), over_rep(sent_stay)
    to_y, to_l, *to_h = in_vmem(
        first_kernel, "first", [2 * n_high * (a + d), 2 * n_high * b] + [4 * e] * n_h, kept_away, got_away
    )
    got_y, got_l, got_h = over_blk(to_y, 1), over_blk(to_l, 2), over_h(to_h)
    own_a, own_d, own_b, own_e, to_y, to_l, *to_h = in_vmem(
        functools.partial(second_kernel, n_high), "second",
        [n_high * a, 2 * d, n_high * b, 2 * e, n_high * b + 2 * e, n_high * a] + [2 * d] * n_h,
        kept_stay, got_stay, got_y, got_l, *got_h,
    )
    got_y, got_l, got_h = over_blk(to_y, 1), over_blk(to_l, 2), over_h(to_h)
    own, to_l, *to_h = in_vmem(
        functools.partial(third_kernel, n_high), "third", [a + d + b + e, d + e] + [a + b] * n_h,
        own_a, own_d, own_b, own_e, got_y, got_l, *got_h,
    )
    got_l, got_h = over_blk(to_l, 2), over_h(to_h)
    (own,) = in_vmem(last_kernel, "last", [a + d + b + e], own, got_l, *got_h)
    return apply_bank(own, over_rep(own), weight_bank)


def solution(mesh):
    placed = (
        P(("groups", "blk", "rep"), None, None, None),
        P(("groups", "blk", "rep"), None, None),
        P(("groups", "blk", "rep"), None, None),
        P(("groups", "blk", "rep"), None),
        P(("groups", "blk", "rep"), None),
        P("groups", None),
        P("groups", None),
        P(),
    )
    return jax.shard_map(
        body,
        mesh=mesh,
        in_specs=placed,
        out_specs=P(("groups", "blk"), None, None),
        check_vma=False,
    )
```

```python
import functools

import jax
import jax.numpy as jnp
from jax import lax
from jax.experimental import pallas as pl
from jax.experimental.pallas import tpu as pltpu
from jax.sharding import PartitionSpec as P

NB_DEV = 8
LANES = 128
SUB = 8
MIB = 1 << 20
UNROLL = 12
N_BUF = 4
ORDERS = ("ylh", "yhl", "lyh", "hyl")
PART_ROWS = (16, 16, 16, 16)


def position():
    here = lax.axis_index("blk")
    return lax.axis_index("rep"), here & 1, (here >> 1) & 1, here >> 2


def accumulate_kernel(
    bank_size, n_owner, n_acc,
    proj_hbm, img_hbm, tra_hbm, w_hbm, pose_hbm, blocks_hbm, tiles_hbm,
    sent_away, *rest,
):
    accs, rest = rest[:n_acc], rest[n_acc:]
    proj, img, tra, weight, pose, blocks, tiles, idx_v, idx_s, square, cross = rest[:11]
    parts = rest[11 : 11 + N_BUF]
    proj_sem, small_sem, table_sem, idx_sem = rest[11 + N_BUF :]
    n_pose, n_part = pose.shape
    n_tile, n_table = blocks.shape
    n_row = accs[0].shape[0]
    tile_rows = SUB * SUB
    part_rows = n_tile * tile_rows

    table_copies = [
        pltpu.make_async_copy(src, dst, table_sem.at[i])
        for i, (src, dst) in enumerate(((pose_hbm, pose), (blocks_hbm, blocks), (tiles_hbm, tiles)))
    ]
    small_copies = [
        pltpu.make_async_copy(img_hbm, img, small_sem.at[0]),
        pltpu.make_async_copy(tra_hbm, tra, small_sem.at[1]),
        pltpu.make_async_copy(w_hbm, weight, small_sem.at[2]),
    ]
    for copy in table_copies + small_copies:
        copy.start()

    def proj_copy(p):
        rows = pl.ds(pl.multiple_of(p * part_rows, part_rows), part_rows)
        return pltpu.make_async_copy(proj_hbm.at[rows, :], proj.at[rows, :], proj_sem.at[p])

    for p in range(n_part):
        proj_copy(p).start()

    zero = jnp.zeros((8 * SUB, LANES), jnp.float32)

    @pl.loop(0, n_row // (8 * SUB))
    def _(i):
        rows = pl.ds(pl.multiple_of(i * (8 * SUB), 8 * SUB), 8 * SUB)
        for acc in accs:
            acc[rows, :] = zero

    for copy in table_copies:
        copy.wait()
    lane = lax.broadcasted_iota(jnp.int32, (n_pose, n_table), 1)
    chosen = jnp.concatenate(
        [(pose[:, p : p + 1] == lane).astype(jnp.float32) for p in range(n_part)], axis=0
    ).astype(jnp.bfloat16)

    def look_up(table):
        return lax.dot_general(
            table[...].astype(jnp.float32).astype(jnp.bfloat16), chosen,
            (((1,), (1,)), ((), ())), preferred_element_type=jnp.float32,
        )

    idx_v[...] = ((look_up(blocks) * bank_size + look_up(tiles)) * SUB).astype(jnp.int32)
    idx_copy = pltpu.make_async_copy(idx_v, idx_s, idx_sem)
    idx_copy.start()

    for copy in small_copies:
        copy.wait()

    @pl.loop(0, square.shape[0] // tile_rows)
    def _(i):
        rows = pl.ds(pl.multiple_of(i * tile_rows, tile_rows), tile_rows)
        t = tra[rows, :].astype(jnp.float32)
        square[rows, :] = t * t
        cross[rows, :] = t * img[rows, :].astype(jnp.float32)

    def stage(p, j, part):
        first = pl.multiple_of((p * n_tile + j) * tile_rows, tile_rows)
        part[...] = proj[pl.ds(first, tile_rows), :].astype(jnp.float32)

    def staged(part):
        return [part[pl.ds(k, SUB, stride=SUB), :] for k in range(n_pose)]

    def terms(p, j, cells, weights):
        cell = pl.ds((j * (n_part // SUB) + p // SUB) * tile_rows + p % SUB, SUB, stride=SUB)
        tt, ti = square[cell, :], cross[cell, :]
        return [(tt * cells[k] - ti) * weights[k] for k in range(n_pose)]

    def add_rows(p, j, values):
        for first in range(0, n_pose, n_acc):
            group = range(first, first + n_acc)
            rows = [pl.ds(pl.multiple_of(idx_s[j, p * n_pose + k], SUB), SUB) for k in group]
            old = [accs[i][rows[i], :] for i in range(n_acc)]
            for i, k in enumerate(group):
                accs[i][rows[i], :] = old[i] + values[k]

    idx_copy.wait()

    @pl.loop(0, n_part)
    def _(p):
        proj_copy(p).wait()
        weights = [jnp.full((SUB, LANES), weight[k, p], jnp.float32) for k in range(n_pose)]

        stage(p, 0, parts[0])
        stage(p, 1, parts[1])

        @pl.loop(0, n_tile, step=UNROLL, init_carry=tuple(terms(p, 0, staged(parts[0]), weights)))
        def _(j, values):
            def tile(u):
                return jnp.minimum(j + u, n_tile - 1) if u >= UNROLL else j + u

            for u in range(UNROLL):
                stage(p, tile(u + 2), parts[(u + 2) % N_BUF])
                later = terms(p, tile(u + 1), staged(parts[(u + 1) % N_BUF]), weights)
                add_rows(p, j + u, values)
                values = later
            return tuple(values)

    Sums(n_owner, accs).pieces_away(sent_away, sent=True)


class Sums:
    def __init__(self, n_owner, accs):
        self.accs = accs
        self.half_rows = accs[0].shape[0] // (n_owner * 2)
        self.sizes = {"y": 2, "l": 2, "h": n_owner // 4}

    def pieces(self, out, begin, part, firsts, sent):
        rep, near, low, high = position()
        order = ORDERS[part]
        n_second, n_third = self.sizes[order[1]], self.sizes[order[2]]
        size = PART_ROWS[part] * SUB
        within = sum(PART_ROWS[:part]) * SUB
        half = 1 - rep if sent else rep

        def piece(x, y, z):
            off = {order[0]: firsts[0] + x, order[1]: y, order[2]: z}
            owner = ((high ^ off["h"]) * 2 + (low ^ off["l"])) * 2 + (near ^ off["y"])
            first = pl.multiple_of((owner * 2 + half) * self.half_rows + within, SUB)
            total = self.accs[0][pl.ds(first, size), :]
            for acc in self.accs[1:]:
                total += acc[pl.ds(first, size), :]
            at = begin + ((x * n_second + y) * n_third + z) * size
            out[pl.ds(pl.multiple_of(at, SUB), size), :] = total

        @pl.loop(0, len(firsts))
        def _(x):
            @pl.loop(0, n_second)
            def _(y):
                for z in range(n_third):
                    piece(x, y, z)

        return begin + len(firsts) * n_second * n_third * size

    def pieces_away(self, out, sent):
        begin = 0
        for part, order in enumerate(ORDERS):
            begin = self.pieces(out, begin, part, range(1, self.sizes[order[0]]), sent)

    def pieces_stay(self, out, sent):
        begin = 0
        for part in range(len(ORDERS)):
            begin = self.pieces(out, begin, part, range(1), sent)


def rest_kernel(n_owner, *refs):
    accs, (kept_away, sent_stay, kept_stay) = refs[:-3], refs[-3:]
    sums = Sums(n_owner, accs)
    sums.pieces_away(kept_away, sent=False)
    sums.pieces_stay(sent_stay, sent=True)
    sums.pieces_stay(kept_stay, sent=False)


def tiles_in_order(array):
    lead = array.shape[:-2]
    rows, cells = array.shape[-2:]
    array = array.reshape(lead + (rows // SUB, SUB, cells // LANES, LANES))
    return jnp.swapaxes(array, -3, -2).reshape(-1, LANES)


def accumulate(
    projections, images, transfer, pose_weights, pose_of, pose_blocks, pose_tiles,
    bank_size, n_owner,
):
    n_part, n_pose, n_tile, n_cell = projections.shape
    assert n_cell == SUB * LANES and n_pose == SUB and n_part % SUB == 0 and n_tile % UNROLL == 0 and UNROLL % N_BUF == 0
    n_row = n_owner * NB_DEV * bank_size * SUB
    n_acc = 4 if n_row * LANES * 4 <= 4 * MIB else 2
    projections = tiles_in_order(jnp.transpose(projections, (0, 2, 1, 3)))
    images = tiles_in_order(jnp.transpose(images, (1, 0, 2)))
    transfer = tiles_in_order(jnp.transpose(transfer, (1, 0, 2)))
    stay = functools.partial(pltpu.with_memory_space_constraint, memory_space=pltpu.HBM)
    hbm = pl.BlockSpec(memory_space=pltpu.HBM)
    vmem = pl.BlockSpec(memory_space=pltpu.VMEM)
    n_high = n_owner // 4
    a, d, b, e = (rows * SUB for rows in PART_ROWS)
    assert sum(PART_ROWS) == NB_DEV // 2 * bank_size

    away = 2 * n_high * (a + d + b) + 4 * (n_high - 1) * e

    def out(rows):
        return jax.ShapeDtypeStruct((rows, LANES), jnp.float32)

    sent_away, *accs = pl.pallas_call(
        functools.partial(accumulate_kernel, bank_size, n_owner, n_acc),
        out_shape=[out(away)] + [out(n_row)] * n_acc,
        in_specs=[hbm] * 7,
        out_specs=[vmem] * (1 + n_acc),
        scratch_shapes=[
            pltpu.VMEM(projections.shape, jnp.bfloat16),
            pltpu.VMEM(images.shape, jnp.bfloat16),
            pltpu.VMEM(transfer.shape, jnp.bfloat16),
            pltpu.SMEM((n_pose, n_part), jnp.float32),
            pltpu.VMEM((n_pose, n_part), jnp.int32),
            pltpu.VMEM(pose_blocks.shape[::-1], jnp.int32),
            pltpu.VMEM(pose_tiles.shape[::-1], jnp.int32),
            pltpu.VMEM((n_tile, n_part * n_pose), jnp.int32),
            pltpu.SMEM((n_tile, n_part * n_pose), jnp.int32),
            pltpu.VMEM(transfer.shape, jnp.float32),
            pltpu.VMEM(transfer.shape, jnp.float32),
        ]
        + [pltpu.VMEM((n_pose * SUB, LANES), jnp.float32)] * N_BUF
        + [
            pltpu.SemaphoreType.DMA((n_part,)),
            pltpu.SemaphoreType.DMA((3,)),
            pltpu.SemaphoreType.DMA((3,)),
            pltpu.SemaphoreType.DMA,
        ],
        compiler_params=pltpu.CompilerParams(vmem_limit_bytes=24 * MIB),
        name="accumulate",
    )(
        stay(projections), stay(images), stay(transfer),
        stay(pose_weights.T), stay(pose_of.T), stay(pose_blocks.T), stay(pose_tiles.T),
    )
    rows = 2 * n_high * (a + d + b) + 4 * e
    return sent_away, *in_vmem(functools.partial(rest_kernel, n_owner), "rest", [away, rows, rows], *accs)


def in_vmem(kernel, name, rows, *operands):
    vmem = pl.BlockSpec(memory_space=pltpu.VMEM)
    return pl.pallas_call(
        kernel,
        out_shape=[jax.ShapeDtypeStruct((n, LANES), jnp.float32) for n in rows],
        in_specs=[vmem] * len(operands),
        out_specs=[vmem] * len(rows),
        compiler_params=pltpu.CompilerParams(vmem_limit_bytes=32 * MIB),
        name=name,
    )(*operands)


def first_kernel(kept, got, *to):
    begin = 0
    for out in to:
        rows = slice(begin, begin + out.shape[0])
        out[...] = kept[rows, :] + got[rows, :]
        begin += out.shape[0]


def second_kernel(n_high, kept, got, got_y, got_l, *rest):
    got_h, (own_a, own_d, own_b, own_e, to_y, to_l, *to_h) = rest[: n_high - 1], rest[n_high - 1 :]
    a, d, b, e = (rows * SUB for rows in PART_ROWS)

    def put(out, at, begin, size, *arrivals):
        total = kept[begin : begin + size, :] + got[begin : begin + size, :]
        for array, first in arrivals:
            total += array[first : first + size, :]
        out[at : at + size, :] = total

    n = n_high * a
    put(own_a, 0, 0, n, (got_y, 0))
    put(to_l, 0, n, n, (got_y, n))
    begin, y_begin = 2 * n, 2 * n
    put(own_d, 0, begin, 2 * d, (got_y, y_begin))
    for i, out in enumerate(to_h):
        put(out, 0, begin + 2 * d * (i + 1), 2 * d, (got_y, y_begin + 2 * d * (i + 1)))
    begin, n = begin + 2 * n_high * d, n_high * b
    put(own_b, 0, begin, n, (got_l, 0))
    put(to_y, 0, begin + n, n, (got_l, n))
    begin += 2 * n
    put(own_e, 0, begin, 2 * e, *[(array, 0) for array in got_h])
    put(to_y, n, begin + 2 * e, 2 * e, *[(array, 2 * e) for array in got_h])


def third_kernel(n_high, own_a, own_d, own_b, own_e, got_y, got_l, *rest):
    got_h, (own, to_l, *to_h) = rest[: n_high - 1], rest[n_high - 1 :]
    a, d, b, e = (rows * SUB for rows in PART_ROWS)

    def put(out, at, source, begin, size, *arrivals):
        total = source[begin : begin + size, :]
        for array, first in arrivals:
            total += array[first : first + size, :]
        out[at : at + size, :] = total

    put(own, 0, own_a, 0, a, (got_l, 0))
    put(own, a, own_d, 0, d, *[(array, 0) for array in got_h])
    put(own, a + d, own_b, 0, b, (got_y, 0))
    put(own, a + d + b, own_e, 0, e, (got_y, n_high * b))
    put(to_l, 0, own_d, d, d, *[(array, d) for array in got_h])
    put(to_l, d, own_e, e, e, (got_y, n_high * b + e))
    for i, out in enumerate(to_h):
        put(out, 0, own_a, (i + 1) * a, a, (got_l, (i + 1) * a))
        put(out, a, own_b, (i + 1) * b, b, (got_y, (i + 1) * b))


def last_kernel(before, got_l, *rest):
    got_h, (own,) = rest[:-1], rest[-1:]
    a, d, b, e = (rows * SUB for rows in PART_ROWS)
    for at, size, arrivals in (
        (0, a, [(array, 0) for array in got_h]),
        (a, d, [(got_l, 0)]),
        (a + d, b, [(array, a) for array in got_h]),
        (a + d + b, e, [(got_l, d)]),
    ):
        total = before[at : at + size, :]
        for array, first in arrivals:
            total += array[first : first + size, :]
        own[at : at + size, :] = total


def weigh(source, bank, out):
    bank_size, n_z, n_cell = bank.shape
    group = 2 * SUB

    for c in range(n_cell // LANES):
        cols = slice(c * LANES, (c + 1) * LANES)

        @pl.loop(0, n_z // group)
        def _(g):
            rows = pl.ds(pl.multiple_of(g * group, group), group)
            weights = [bank[t, rows, cols] for t in range(bank_size)]
            for b in range(out.shape[0]):
                total = None
                for t in range(bank_size):
                    value = weights[t] * source[b, t, c : c + 1, :]
                    total = value if total is None else total + value
                out[b, rows, cols] = total


def bank_rest_kernel(done, other, bank, out_hbm, block, sem):
    n_half = block.shape[0]
    rep = position()[0]
    first = pltpu.make_async_copy(done, out_hbm.at[pl.ds(rep * n_half, n_half)], sem.at[0])
    first.start()
    weigh(other, bank, block)
    second = pltpu.make_async_copy(block, out_hbm.at[pl.ds((1 - rep) * n_half, n_half)], sem.at[1])
    second.start()
    first.wait()
    second.wait()


def apply_bank(own, other, weight_bank):
    bank_size, n_z, n_cell = weight_bank.shape
    n_half = NB_DEV // 2
    vmem = pl.BlockSpec(memory_space=pltpu.VMEM)
    own, other = [array.reshape(n_half, bank_size, SUB, LANES) for array in (own, other)]
    params = pltpu.CompilerParams(vmem_limit_bytes=32 * MIB)
    done = pl.pallas_call(
        weigh,
        out_shape=jax.ShapeDtypeStruct((n_half, n_z, n_cell), jnp.float32),
        in_specs=[vmem] * 2,
        out_specs=vmem,
        compiler_params=params,
        name="bank_own",
    )(own, weight_bank)
    return pl.pallas_call(
        bank_rest_kernel,
        out_shape=jax.ShapeDtypeStruct((NB_DEV, n_z, n_cell), jnp.float32),
        in_specs=[vmem] * 3,
        out_specs=pl.BlockSpec(memory_space=pl.ANY),
        scratch_shapes=[
            pltpu.VMEM((n_half, n_z, n_cell), jnp.float32),
            pltpu.SemaphoreType.DMA((2,)),
        ],
        compiler_params=params,
        name="bank_rest",
    )(done, other, weight_bank)


def body(
    projections, images, transfer, pose_weights, pose_of, pose_blocks, pose_tiles, weight_bank
):
    bank_size = weight_bank.shape[0]
    n_blk = lax.axis_size("blk")
    n_high = n_blk // 4
    sent_away, kept_away, sent_stay, kept_stay = accumulate(
        projections, images, transfer, pose_weights, pose_of, pose_blocks, pose_tiles,
        bank_size, n_blk,
    )
    a, d, b, e = (rows * SUB for rows in PART_ROWS)

    def over_rep(array):
        return lax.ppermute(array, "rep", [(0, 1), (1, 0)])

    def over_blk(array, bits):
        return lax.ppermute(array, "blk", [(i, i ^ bits) for i in range(n_blk)])

    def over_h(arrays):
        return [over_blk(array, 4 * (i + 1)) for i, array in enumerate(arrays)]

    n_h = n_high - 1
    got_away, got_stay = over_rep(sent_away), over_rep(sent_stay)
    to_y, to_l, *to_h = in_vmem(
        first_kernel, "first", [2 * n_high * (a + d), 2 * n_high * b] + [4 * e] * n_h, kept_away, got_away
    )
    got_y, got_l, got_h = over_blk(to_y, 1), over_blk(to_l, 2), over_h(to_h)
    own_a, own_d, own_b, own_e, to_y, to_l, *to_h = in_vmem(
        functools.partial(second_kernel, n_high), "second",
        [n_high * a, 2 * d, n_high * b, 2 * e, n_high * b + 2 * e, n_high * a] + [2 * d] * n_h,
        kept_stay, got_stay, got_y, got_l, *got_h,
    )
    got_y, got_l, got_h = over_blk(to_y, 1), over_blk(to_l, 2), over_h(to_h)
    own, to_l, *to_h = in_vmem(
        functools.partial(third_kernel, n_high), "third", [a + d + b + e, d + e] + [a + b] * n_h,
        own_a, own_d, own_b, own_e, got_y, got_l, *got_h,
    )
    got_l, got_h = over_blk(to_l, 2), over_h(to_h)
    (own,) = in_vmem(last_kernel, "last", [a + d + b + e], own, got_l, *got_h)
    return apply_bank(own, over_rep(own), weight_bank)


def solution(mesh):
    placed = (
        P(("groups", "blk", "rep"), None, None, None),
        P(("groups", "blk", "rep"), None, None),
        P(("groups", "blk", "rep"), None, None),
        P(("groups", "blk", "rep"), None),
        P(("groups", "blk", "rep"), None),
        P("groups", None),
        P("groups", None),
        P(),
    )
    return jax.shard_map(
        body,
        mesh=mesh,
        in_specs=placed,
        out_specs=P(("groups", "blk"), None, None),
        check_vma=False,
    )
```

```python
import functools

import jax
import jax.numpy as jnp
from jax import lax
from jax.experimental import pallas as pl
from jax.experimental.pallas import tpu as pltpu
from jax.sharding import PartitionSpec as P

NB_DEV = 8
LANES = 128
SUB = 8
MIB = 1 << 20
UNROLL = 12
N_BUF = 4
ORDERS = ("ylh", "yhl", "lyh", "hyl")
PART_ROWS = (16, 16, 16, 16)


def position():
    here = lax.axis_index("blk")
    return lax.axis_index("rep"), here & 1, (here >> 1) & 1, here >> 2


def accumulate_kernel(
    bank_size, n_owner, n_acc,
    proj_hbm, img_hbm, tra_hbm, w_hbm, pose_hbm, blocks_hbm, tiles_hbm,
    sent_away, *rest,
):
    accs, rest = rest[:n_acc], rest[n_acc:]
    proj, img, tra, weight, pose, blocks, tiles, idx_v, idx_s, square, cross = rest[:11]
    parts = rest[11 : 11 + N_BUF]
    proj_sem, small_sem, table_sem, idx_sem = rest[11 + N_BUF :]
    n_pose, n_part = pose.shape
    n_tile, n_table = blocks.shape
    n_row = accs[0].shape[0]
    tile_rows = SUB * SUB
    part_rows = n_tile * tile_rows

    table_copies = [
        pltpu.make_async_copy(src, dst, table_sem.at[i])
        for i, (src, dst) in enumerate(((pose_hbm, pose), (blocks_hbm, blocks), (tiles_hbm, tiles)))
    ]
    small_copies = [
        pltpu.make_async_copy(img_hbm, img, small_sem.at[0]),
        pltpu.make_async_copy(tra_hbm, tra, small_sem.at[1]),
        pltpu.make_async_copy(w_hbm, weight, small_sem.at[2]),
    ]
    for copy in table_copies + small_copies:
        copy.start()

    def proj_copy(p):
        rows = pl.ds(pl.multiple_of(p * part_rows, part_rows), part_rows)
        return pltpu.make_async_copy(proj_hbm.at[rows, :], proj.at[rows, :], proj_sem.at[p])

    for p in range(n_part):
        proj_copy(p).start()

    zero = jnp.zeros((8 * SUB, LANES), jnp.float32)

    @pl.loop(0, n_row // (8 * SUB))
    def _(i):
        rows = pl.ds(pl.multiple_of(i * (8 * SUB), 8 * SUB), 8 * SUB)
        for acc in accs:
            acc[rows, :] = zero

    for copy in table_copies:
        copy.wait()
    lane = lax.broadcasted_iota(jnp.int32, (n_pose, n_table), 1)
    chosen = jnp.concatenate(
        [(pose[:, p : p + 1] == lane).astype(jnp.float32) for p in range(n_part)], axis=0
    ).astype(jnp.bfloat16)

    def look_up(table):
        return lax.dot_general(
            table[...].astype(jnp.float32).astype(jnp.bfloat16), chosen,
            (((1,), (1,)), ((), ())), preferred_element_type=jnp.float32,
        )

    idx_v[...] = ((look_up(blocks) * bank_size + look_up(tiles)) * SUB).astype(jnp.int32)
    idx_copy = pltpu.make_async_copy(idx_v, idx_s, idx_sem)
    idx_copy.start()

    for copy in small_copies:
        copy.wait()

    @pl.loop(0, square.shape[0] // tile_rows)
    def _(i):
        rows = pl.ds(pl.multiple_of(i * tile_rows, tile_rows), tile_rows)
        t = tra[rows, :].astype(jnp.float32)
        square[rows, :] = t * t
        cross[rows, :] = t * img[rows, :].astype(jnp.float32)

    def stage(p, j, part):
        first = pl.multiple_of((p * n_tile + j) * tile_rows, tile_rows)
        part[...] = proj[pl.ds(first, tile_rows), :].astype(jnp.float32)

    def staged(part):
        return [part[pl.ds(k, SUB, stride=SUB), :] for k in range(n_pose)]

    def terms(p, j, cells, weights):
        cell = pl.ds((j * (n_part // SUB) + p // SUB) * tile_rows + p % SUB, SUB, stride=SUB)
        tt, ti = square[cell, :], cross[cell, :]
        return [(tt * cells[k] - ti) * weights[k] for k in range(n_pose)]

    def add_rows(p, j, values):
        for first in range(0, n_pose, n_acc):
            group = range(first, first + n_acc)
            rows = [pl.ds(pl.multiple_of(idx_s[j, p * n_pose + k], SUB), SUB) for k in group]
            old = [accs[i][rows[i], :] for i in range(n_acc)]
            for i, k in enumerate(group):
                accs[i][rows[i], :] = old[i] + values[k]

    idx_copy.wait()

    def spread(p):
        return [jnp.full((SUB, LANES), weight[k, p], jnp.float32) for k in range(n_pose)]

    proj_copy(0).wait()
    stage(0, 0, parts[0])
    stage(0, 1, parts[1])

    @pl.loop(0, n_part, init_carry=tuple(terms(0, 0, staged(parts[0]), spread(0))))
    def _(p, carry):
        @pl.when(p + 1 < n_part)
        def _():
            proj_copy(p + 1).wait()

        weights = spread(p)

        @pl.loop(0, n_tile, step=UNROLL, init_carry=carry)
        def done(j, values):
            ends = j + UNROLL == n_tile
            next_p = jnp.where(ends, jnp.minimum(p + 1, n_part - 1), p)
            next_j = jnp.where(ends, 0, j + UNROLL)

            def tile(u):
                return (p, j + u) if u < UNROLL else (next_p, next_j + u - UNROLL)

            for u in range(UNROLL):
                stage(*tile(u + 2), parts[(u + 2) % N_BUF])
                scale = weights if u + 1 < UNROLL else spread(next_p)
                later = terms(*tile(u + 1), staged(parts[(u + 1) % N_BUF]), scale)
                add_rows(p, j + u, values)
                values = later
            return tuple(values)

        return done

    Sums(n_owner, accs).pieces_away(sent_away, sent=True)


class Sums:
    def __init__(self, n_owner, accs):
        self.accs = accs
        self.half_rows = accs[0].shape[0] // (n_owner * 2)
        self.sizes = {"y": 2, "l": 2, "h": n_owner // 4}

    def pieces(self, out, begin, part, firsts, sent):
        rep, near, low, high = position()
        order = ORDERS[part]
        n_second, n_third = self.sizes[order[1]], self.sizes[order[2]]
        size = PART_ROWS[part] * SUB
        within = sum(PART_ROWS[:part]) * SUB
        half = 1 - rep if sent else rep

        def piece(x, y, z):
            off = {order[0]: firsts[0] + x, order[1]: y, order[2]: z}
            owner = ((high ^ off["h"]) * 2 + (low ^ off["l"])) * 2 + (near ^ off["y"])
            first = pl.multiple_of((owner * 2 + half) * self.half_rows + within, SUB)
            total = self.accs[0][pl.ds(first, size), :]
            for acc in self.accs[1:]:
                total += acc[pl.ds(first, size), :]
            at = begin + ((x * n_second + y) * n_third + z) * size
            out[pl.ds(pl.multiple_of(at, SUB), size), :] = total

        @pl.loop(0, len(firsts))
        def _(x):
            @pl.loop(0, n_second)
            def _(y):
                for z in range(n_third):
                    piece(x, y, z)

        return begin + len(firsts) * n_second * n_third * size

    def pieces_away(self, out, sent):
        begin = 0
        for part, order in enumerate(ORDERS):
            begin = self.pieces(out, begin, part, range(1, self.sizes[order[0]]), sent)

    def pieces_stay(self, out, sent):
        begin = 0
        for part in range(len(ORDERS)):
            begin = self.pieces(out, begin, part, range(1), sent)


def rest_kernel(n_owner, *refs):
    accs, (kept_away, sent_stay, kept_stay) = refs[:-3], refs[-3:]
    sums = Sums(n_owner, accs)
    sums.pieces_away(kept_away, sent=False)
    sums.pieces_stay(sent_stay, sent=True)
    sums.pieces_stay(kept_stay, sent=False)


def tiles_in_order(array):
    lead = array.shape[:-2]
    rows, cells = array.shape[-2:]
    array = array.reshape(lead + (rows // SUB, SUB, cells // LANES, LANES))
    return jnp.swapaxes(array, -3, -2).reshape(-1, LANES)


def accumulate(
    projections, images, transfer, pose_weights, pose_of, pose_blocks, pose_tiles,
    bank_size, n_owner,
):
    n_part, n_pose, n_tile, n_cell = projections.shape
    assert n_cell == SUB * LANES and n_pose == SUB and n_part % SUB == 0 and n_tile % UNROLL == 0 and UNROLL % N_BUF == 0
    n_row = n_owner * NB_DEV * bank_size * SUB
    n_acc = 4 if n_row * LANES * 4 <= 4 * MIB else 2
    projections = tiles_in_order(jnp.transpose(projections, (0, 2, 1, 3)))
    images = tiles_in_order(jnp.transpose(images, (1, 0, 2)))
    transfer = tiles_in_order(jnp.transpose(transfer, (1, 0, 2)))
    stay = functools.partial(pltpu.with_memory_space_constraint, memory_space=pltpu.HBM)
    hbm = pl.BlockSpec(memory_space=pltpu.HBM)
    vmem = pl.BlockSpec(memory_space=pltpu.VMEM)
    n_high = n_owner // 4
    a, d, b, e = (rows * SUB for rows in PART_ROWS)
    assert sum(PART_ROWS) == NB_DEV // 2 * bank_size

    away = 2 * n_high * (a + d + b) + 4 * (n_high - 1) * e

    def out(rows):
        return jax.ShapeDtypeStruct((rows, LANES), jnp.float32)

    sent_away, *accs = pl.pallas_call(
        functools.partial(accumulate_kernel, bank_size, n_owner, n_acc),
        out_shape=[out(away)] + [out(n_row)] * n_acc,
        in_specs=[hbm] * 7,
        out_specs=[vmem] * (1 + n_acc),
        scratch_shapes=[
            pltpu.VMEM(projections.shape, jnp.bfloat16),
            pltpu.VMEM(images.shape, jnp.bfloat16),
            pltpu.VMEM(transfer.shape, jnp.bfloat16),
            pltpu.SMEM((n_pose, n_part), jnp.float32),
            pltpu.VMEM((n_pose, n_part), jnp.int32),
            pltpu.VMEM(pose_blocks.shape[::-1], jnp.int32),
            pltpu.VMEM(pose_tiles.shape[::-1], jnp.int32),
            pltpu.VMEM((n_tile, n_part * n_pose), jnp.int32),
            pltpu.SMEM((n_tile, n_part * n_pose), jnp.int32),
            pltpu.VMEM(transfer.shape, jnp.float32),
            pltpu.VMEM(transfer.shape, jnp.float32),
        ]
        + [pltpu.VMEM((n_pose * SUB, LANES), jnp.float32)] * N_BUF
        + [
            pltpu.SemaphoreType.DMA((n_part,)),
            pltpu.SemaphoreType.DMA((3,)),
            pltpu.SemaphoreType.DMA((3,)),
            pltpu.SemaphoreType.DMA,
        ],
        compiler_params=pltpu.CompilerParams(vmem_limit_bytes=24 * MIB),
        name="accumulate",
    )(
        stay(projections), stay(images), stay(transfer),
        stay(pose_weights.T), stay(pose_of.T), stay(pose_blocks.T), stay(pose_tiles.T),
    )
    rows = 2 * n_high * (a + d + b) + 4 * e
    return sent_away, *in_vmem(functools.partial(rest_kernel, n_owner), "rest", [away, rows, rows], *accs)


def in_vmem(kernel, name, rows, *operands):
    vmem = pl.BlockSpec(memory_space=pltpu.VMEM)
    return pl.pallas_call(
        kernel,
        out_shape=[jax.ShapeDtypeStruct((n, LANES), jnp.float32) for n in rows],
        in_specs=[vmem] * len(operands),
        out_specs=[vmem] * len(rows),
        compiler_params=pltpu.CompilerParams(vmem_limit_bytes=32 * MIB),
        name=name,
    )(*operands)


def first_kernel(kept, got, *to):
    begin = 0
    for out in to:
        rows = slice(begin, begin + out.shape[0])
        out[...] = kept[rows, :] + got[rows, :]
        begin += out.shape[0]


def second_kernel(n_high, kept, got, got_y, got_l, *rest):
    got_h, (own_a, own_d, own_b, own_e, to_y, to_l, *to_h) = rest[: n_high - 1], rest[n_high - 1 :]
    a, d, b, e = (rows * SUB for rows in PART_ROWS)

    def put(out, at, begin, size, *arrivals):
        total = kept[begin : begin + size, :] + got[begin : begin + size, :]
        for array, first in arrivals:
            total += array[first : first + size, :]
        out[at : at + size, :] = total

    n = n_high * a
    put(own_a, 0, 0, n, (got_y, 0))
    put(to_l, 0, n, n, (got_y, n))
    begin, y_begin = 2 * n, 2 * n
    put(own_d, 0, begin, 2 * d, (got_y, y_begin))
    for i, out in enumerate(to_h):
        put(out, 0, begin + 2 * d * (i + 1), 2 * d, (got_y, y_begin + 2 * d * (i + 1)))
    begin, n = begin + 2 * n_high * d, n_high * b
    put(own_b, 0, begin, n, (got_l, 0))
    put(to_y, 0, begin + n, n, (got_l, n))
    begin += 2 * n
    put(own_e, 0, begin, 2 * e, *[(array, 0) for array in got_h])
    put(to_y, n, begin + 2 * e, 2 * e, *[(array, 2 * e) for array in got_h])


def third_kernel(n_high, own_a, own_d, own_b, own_e, got_y, got_l, *rest):
    got_h, (own, to_l, *to_h) = rest[: n_high - 1], rest[n_high - 1 :]
    a, d, b, e = (rows * SUB for rows in PART_ROWS)

    def put(out, at, source, begin, size, *arrivals):
        total = source[begin : begin + size, :]
        for array, first in arrivals:
            total += array[first : first + size, :]
        out[at : at + size, :] = total

    put(own, 0, own_a, 0, a, (got_l, 0))
    put(own, a, own_d, 0, d, *[(array, 0) for array in got_h])
    put(own, a + d, own_b, 0, b, (got_y, 0))
    put(own, a + d + b, own_e, 0, e, (got_y, n_high * b))
    put(to_l, 0, own_d, d, d, *[(array, d) for array in got_h])
    put(to_l, d, own_e, e, e, (got_y, n_high * b + e))
    for i, out in enumerate(to_h):
        put(out, 0, own_a, (i + 1) * a, a, (got_l, (i + 1) * a))
        put(out, a, own_b, (i + 1) * b, b, (got_y, (i + 1) * b))


def last_kernel(before, got_l, *rest):
    got_h, (own,) = rest[:-1], rest[-1:]
    a, d, b, e = (rows * SUB for rows in PART_ROWS)
    for at, size, arrivals in (
        (0, a, [(array, 0) for array in got_h]),
        (a, d, [(got_l, 0)]),
        (a + d, b, [(array, a) for array in got_h]),
        (a + d + b, e, [(got_l, d)]),
    ):
        total = before[at : at + size, :]
        for array, first in arrivals:
            total += array[first : first + size, :]
        own[at : at + size, :] = total


def weigh(source, bank, out):
    bank_size, n_z, n_cell = bank.shape
    group = 2 * SUB

    for c in range(n_cell // LANES):
        cols = slice(c * LANES, (c + 1) * LANES)

        @pl.loop(0, n_z // group)
        def _(g):
            rows = pl.ds(pl.multiple_of(g * group, group), group)
            weights = [bank[t, rows, cols] for t in range(bank_size)]
            for b in range(out.shape[0]):
                total = None
                for t in range(bank_size):
                    value = weights[t] * source[b, t, c : c + 1, :]
                    total = value if total is None else total + value
                out[b, rows, cols] = total


def bank_rest_kernel(done, other, bank, out_hbm, block, sem):
    n_half = block.shape[0]
    rep = position()[0]
    first = pltpu.make_async_copy(done, out_hbm.at[pl.ds(rep * n_half, n_half)], sem.at[0])
    first.start()
    weigh(other, bank, block)
    second = pltpu.make_async_copy(block, out_hbm.at[pl.ds((1 - rep) * n_half, n_half)], sem.at[1])
    second.start()
    first.wait()
    second.wait()


def apply_bank(own, other, weight_bank):
    bank_size, n_z, n_cell = weight_bank.shape
    n_half = NB_DEV // 2
    vmem = pl.BlockSpec(memory_space=pltpu.VMEM)
    own, other = [array.reshape(n_half, bank_size, SUB, LANES) for array in (own, other)]
    params = pltpu.CompilerParams(vmem_limit_bytes=32 * MIB)
    done = pl.pallas_call(
        weigh,
        out_shape=jax.ShapeDtypeStruct((n_half, n_z, n_cell), jnp.float32),
        in_specs=[vmem] * 2,
        out_specs=vmem,
        compiler_params=params,
        name="bank_own",
    )(own, weight_bank)
    return pl.pallas_call(
        bank_rest_kernel,
        out_shape=jax.ShapeDtypeStruct((NB_DEV, n_z, n_cell), jnp.float32),
        in_specs=[vmem] * 3,
        out_specs=pl.BlockSpec(memory_space=pl.ANY),
        scratch_shapes=[
            pltpu.VMEM((n_half, n_z, n_cell), jnp.float32),
            pltpu.SemaphoreType.DMA((2,)),
        ],
        compiler_params=params,
        name="bank_rest",
    )(done, other, weight_bank)


def body(
    projections, images, transfer, pose_weights, pose_of, pose_blocks, pose_tiles, weight_bank
):
    bank_size = weight_bank.shape[0]
    n_blk = lax.axis_size("blk")
    n_high = n_blk // 4
    sent_away, kept_away, sent_stay, kept_stay = accumulate(
        projections, images, transfer, pose_weights, pose_of, pose_blocks, pose_tiles,
        bank_size, n_blk,
    )
    a, d, b, e = (rows * SUB for rows in PART_ROWS)

    def over_rep(array):
        return lax.ppermute(array, "rep", [(0, 1), (1, 0)])

    def over_blk(array, bits):
        return lax.ppermute(array, "blk", [(i, i ^ bits) for i in range(n_blk)])

    def over_h(arrays):
        return [over_blk(array, 4 * (i + 1)) for i, array in enumerate(arrays)]

    n_h = n_high - 1
    got_away, got_stay = over_rep(sent_away), over_rep(sent_stay)
    to_y, to_l, *to_h = in_vmem(
        first_kernel, "first", [2 * n_high * (a + d), 2 * n_high * b] + [4 * e] * n_h, kept_away, got_away
    )
    got_y, got_l, got_h = over_blk(to_y, 1), over_blk(to_l, 2), over_h(to_h)
    own_a, own_d, own_b, own_e, to_y, to_l, *to_h = in_vmem(
        functools.partial(second_kernel, n_high), "second",
        [n_high * a, 2 * d, n_high * b, 2 * e, n_high * b + 2 * e, n_high * a] + [2 * d] * n_h,
        kept_stay, got_stay, got_y, got_l, *got_h,
    )
    got_y, got_l, got_h = over_blk(to_y, 1), over_blk(to_l, 2), over_h(to_h)
    own, to_l, *to_h = in_vmem(
        functools.partial(third_kernel, n_high), "third", [a + d + b + e, d + e] + [a + b] * n_h,
        own_a, own_d, own_b, own_e, got_y, got_l, *got_h,
    )
    got_l, got_h = over_blk(to_l, 2), over_h(to_h)
    (own,) = in_vmem(last_kernel, "last", [a + d + b + e], own, got_l, *got_h)
    return apply_bank(own, over_rep(own), weight_bank)


def solution(mesh):
    placed = (
        P(("groups", "blk", "rep"), None, None, None),
        P(("groups", "blk", "rep"), None, None),
        P(("groups", "blk", "rep"), None, None),
        P(("groups", "blk", "rep"), None),
        P(("groups", "blk", "rep"), None),
        P("groups", None),
        P("groups", None),
        P(),
    )
    return jax.shard_map(
        body,
        mesh=mesh,
        in_specs=placed,
        out_specs=P(("groups", "blk"), None, None),
        check_vma=False,
    )
```

```python
import functools

import jax
import jax.numpy as jnp
from jax import lax
from jax.experimental import pallas as pl
from jax.experimental.pallas import tpu as pltpu
from jax.sharding import PartitionSpec as P

NB_DEV = 8
LANES = 128
SUB = 8
MIB = 1 << 20
UNROLL = 36
N_BUF = 4
ORDERS = ("ylh", "yhl", "lyh", "hyl")
PART_ROWS = (16, 16, 16, 16)


def position():
    here = lax.axis_index("blk")
    return lax.axis_index("rep"), here & 1, (here >> 1) & 1, here >> 2


def accumulate_kernel(
    bank_size, n_owner, n_acc,
    proj_hbm, img_hbm, tra_hbm, w_hbm, pose_hbm, blocks_hbm, tiles_hbm,
    sent_away, *rest,
):
    accs, rest = rest[:n_acc], rest[n_acc:]
    proj, img, tra, weight, pose, blocks, tiles, idx_v, idx_s, square, cross = rest[:11]
    parts = rest[11 : 11 + N_BUF]
    proj_sem, small_sem, table_sem, idx_sem = rest[11 + N_BUF :]
    n_pose, n_part = pose.shape
    n_tile, n_table = blocks.shape
    n_row = accs[0].shape[0]
    tile_rows = SUB * SUB
    part_rows = n_tile * tile_rows

    table_copies = [
        pltpu.make_async_copy(src, dst, table_sem.at[i])
        for i, (src, dst) in enumerate(((pose_hbm, pose), (blocks_hbm, blocks), (tiles_hbm, tiles)))
    ]
    small_copies = [
        pltpu.make_async_copy(img_hbm, img, small_sem.at[0]),
        pltpu.make_async_copy(tra_hbm, tra, small_sem.at[1]),
        pltpu.make_async_copy(w_hbm, weight, small_sem.at[2]),
    ]
    for copy in table_copies + small_copies:
        copy.start()

    def proj_copy(p):
        rows = pl.ds(pl.multiple_of(p * part_rows, part_rows), part_rows)
        return pltpu.make_async_copy(proj_hbm.at[rows, :], proj.at[rows, :], proj_sem.at[p])

    for p in range(n_part):
        proj_copy(p).start()

    zero = jnp.zeros((8 * SUB, LANES), jnp.float32)

    @pl.loop(0, n_row // (8 * SUB))
    def _(i):
        rows = pl.ds(pl.multiple_of(i * (8 * SUB), 8 * SUB), 8 * SUB)
        for acc in accs:
            acc[rows, :] = zero

    for copy in table_copies:
        copy.wait()
    lane = lax.broadcasted_iota(jnp.int32, (n_pose, n_table), 1)
    chosen = jnp.concatenate(
        [(pose[:, p : p + 1] == lane).astype(jnp.float32) for p in range(n_part)], axis=0
    ).astype(jnp.bfloat16)

    def look_up(table):
        return lax.dot_general(
            table[...].astype(jnp.float32).astype(jnp.bfloat16), chosen,
            (((1,), (1,)), ((), ())), preferred_element_type=jnp.float32,
        )

    idx_v[...] = ((look_up(blocks) * bank_size + look_up(tiles)) * SUB).astype(jnp.int32)
    idx_copy = pltpu.make_async_copy(idx_v, idx_s, idx_sem)
    idx_copy.start()

    for copy in small_copies:
        copy.wait()

    @pl.loop(0, square.shape[0] // tile_rows)
    def _(i):
        rows = pl.ds(pl.multiple_of(i * tile_rows, tile_rows), tile_rows)
        t = tra[rows, :].astype(jnp.float32)
        square[rows, :] = t * t
        cross[rows, :] = t * img[rows, :].astype(jnp.float32)

    def stage(p, j, part):
        first = pl.multiple_of((p * n_tile + j) * tile_rows, tile_rows)
        part[...] = proj[pl.ds(first, tile_rows), :].astype(jnp.float32)

    def staged(part):
        return [part[pl.ds(k, SUB, stride=SUB), :] for k in range(n_pose)]

    def terms(p, j, cells, weights):
        cell = pl.ds((j * (n_part // SUB) + p // SUB) * tile_rows + p % SUB, SUB, stride=SUB)
        tt, ti = square[cell, :], cross[cell, :]
        return [(tt * cells[k] - ti) * weights[k] for k in range(n_pose)]

    def add_rows(p, j, values):
        for first in range(0, n_pose, n_acc):
            group = range(first, first + n_acc)
            rows = [pl.ds(pl.multiple_of(idx_s[j, p * n_pose + k], SUB), SUB) for k in group]
            old = [accs[i][rows[i], :] for i in range(n_acc)]
            for i, k in enumerate(group):
                accs[i][rows[i], :] = old[i] + values[k]

    idx_copy.wait()

    @pl.loop(0, n_part)
    def _(p):
        proj_copy(p).wait()
        weights = [jnp.full((SUB, LANES), weight[k, p], jnp.float32) for k in range(n_pose)]

        stage(p, 0, parts[0])
        stage(p, 1, parts[1])

        @pl.loop(0, n_tile, step=UNROLL, init_carry=tuple(terms(p, 0, staged(parts[0]), weights)))
        def _(j, values):
            def tile(u):
                return jnp.minimum(j + u, n_tile - 1) if u >= UNROLL else j + u

            for u in range(UNROLL):
                stage(p, tile(u + 2), parts[(u + 2) % N_BUF])
                later = terms(p, tile(u + 1), staged(parts[(u + 1) % N_BUF]), weights)
                add_rows(p, j + u, values)
                values = later
            return tuple(values)

    Sums(n_owner, accs).pieces_away(sent_away, sent=True)


class Sums:
    def __init__(self, n_owner, accs):
        self.accs = accs
        self.half_rows = accs[0].shape[0] // (n_owner * 2)
        self.sizes = {"y": 2, "l": 2, "h": n_owner // 4}

    def pieces(self, out, begin, part, firsts, sent):
        rep, near, low, high = position()
        order = ORDERS[part]
        n_second, n_third = self.sizes[order[1]], self.sizes[order[2]]
        size = PART_ROWS[part] * SUB
        within = sum(PART_ROWS[:part]) * SUB
        half = 1 - rep if sent else rep

        def piece(x, y, z):
            off = {order[0]: firsts[0] + x, order[1]: y, order[2]: z}
            owner = ((high ^ off["h"]) * 2 + (low ^ off["l"])) * 2 + (near ^ off["y"])
            first = pl.multiple_of((owner * 2 + half) * self.half_rows + within, SUB)
            total = self.accs[0][pl.ds(first, size), :]
            for acc in self.accs[1:]:
                total += acc[pl.ds(first, size), :]
            at = begin + ((x * n_second + y) * n_third + z) * size
            out[pl.ds(pl.multiple_of(at, SUB), size), :] = total

        @pl.loop(0, len(firsts))
        def _(x):
            @pl.loop(0, n_second)
            def _(y):
                for z in range(n_third):
                    piece(x, y, z)

        return begin + len(firsts) * n_second * n_third * size

    def pieces_away(self, out, sent):
        begin = 0
        for part, order in enumerate(ORDERS):
            begin = self.pieces(out, begin, part, range(1, self.sizes[order[0]]), sent)

    def pieces_stay(self, out, sent):
        begin = 0
        for part in range(len(ORDERS)):
            begin = self.pieces(out, begin, part, range(1), sent)


def rest_kernel(n_owner, *refs):
    accs, (kept_away, sent_stay, kept_stay) = refs[:-3], refs[-3:]
    sums = Sums(n_owner, accs)
    sums.pieces_away(kept_away, sent=False)
    sums.pieces_stay(sent_stay, sent=True)
    sums.pieces_stay(kept_stay, sent=False)


def tiles_in_order(array):
    lead = array.shape[:-2]
    rows, cells = array.shape[-2:]
    array = array.reshape(lead + (rows // SUB, SUB, cells // LANES, LANES))
    return jnp.swapaxes(array, -3, -2).reshape(-1, LANES)


def accumulate(
    projections, images, transfer, pose_weights, pose_of, pose_blocks, pose_tiles,
    bank_size, n_owner,
):
    n_part, n_pose, n_tile, n_cell = projections.shape
    assert n_cell == SUB * LANES and n_pose == SUB and n_part % SUB == 0 and n_tile % UNROLL == 0 and UNROLL % N_BUF == 0
    n_row = n_owner * NB_DEV * bank_size * SUB
    n_acc = 4 if n_row * LANES * 4 <= 4 * MIB else 2
    projections = tiles_in_order(jnp.transpose(projections, (0, 2, 1, 3)))
    images = tiles_in_order(jnp.transpose(images, (1, 0, 2)))
    transfer = tiles_in_order(jnp.transpose(transfer, (1, 0, 2)))
    stay = functools.partial(pltpu.with_memory_space_constraint, memory_space=pltpu.HBM)
    hbm = pl.BlockSpec(memory_space=pltpu.HBM)
    vmem = pl.BlockSpec(memory_space=pltpu.VMEM)
    n_high = n_owner // 4
    a, d, b, e = (rows * SUB for rows in PART_ROWS)
    assert sum(PART_ROWS) == NB_DEV // 2 * bank_size

    away = 2 * n_high * (a + d + b) + 4 * (n_high - 1) * e

    def out(rows):
        return jax.ShapeDtypeStruct((rows, LANES), jnp.float32)

    sent_away, *accs = pl.pallas_call(
        functools.partial(accumulate_kernel, bank_size, n_owner, n_acc),
        out_shape=[out(away)] + [out(n_row)] * n_acc,
        in_specs=[hbm] * 7,
        out_specs=[vmem] * (1 + n_acc),
        scratch_shapes=[
            pltpu.VMEM(projections.shape, jnp.bfloat16),
            pltpu.VMEM(images.shape, jnp.bfloat16),
            pltpu.VMEM(transfer.shape, jnp.bfloat16),
            pltpu.SMEM((n_pose, n_part), jnp.float32),
            pltpu.VMEM((n_pose, n_part), jnp.int32),
            pltpu.VMEM(pose_blocks.shape[::-1], jnp.int32),
            pltpu.VMEM(pose_tiles.shape[::-1], jnp.int32),
            pltpu.VMEM((n_tile, n_part * n_pose), jnp.int32),
            pltpu.SMEM((n_tile, n_part * n_pose), jnp.int32),
            pltpu.VMEM(transfer.shape, jnp.float32),
            pltpu.VMEM(transfer.shape, jnp.float32),
        ]
        + [pltpu.VMEM((n_pose * SUB, LANES), jnp.float32)] * N_BUF
        + [
            pltpu.SemaphoreType.DMA((n_part,)),
            pltpu.SemaphoreType.DMA((3,)),
            pltpu.SemaphoreType.DMA((3,)),
            pltpu.SemaphoreType.DMA,
        ],
        compiler_params=pltpu.CompilerParams(vmem_limit_bytes=24 * MIB),
        name="accumulate",
    )(
        stay(projections), stay(images), stay(transfer),
        stay(pose_weights.T), stay(pose_of.T), stay(pose_blocks.T), stay(pose_tiles.T),
    )
    rows = 2 * n_high * (a + d + b) + 4 * e
    return sent_away, *in_vmem(functools.partial(rest_kernel, n_owner), "rest", [away, rows, rows], *accs)


def in_vmem(kernel, name, rows, *operands):
    vmem = pl.BlockSpec(memory_space=pltpu.VMEM)
    return pl.pallas_call(
        kernel,
        out_shape=[jax.ShapeDtypeStruct((n, LANES), jnp.float32) for n in rows],
        in_specs=[vmem] * len(operands),
        out_specs=[vmem] * len(rows),
        compiler_params=pltpu.CompilerParams(vmem_limit_bytes=32 * MIB),
        name=name,
    )(*operands)


def first_kernel(kept, got, *to):
    begin = 0
    for out in to:
        rows = slice(begin, begin + out.shape[0])
        out[...] = kept[rows, :] + got[rows, :]
        begin += out.shape[0]


def second_kernel(n_high, kept, got, got_y, got_l, *rest):
    got_h, (own_a, own_d, own_b, own_e, to_y, to_l, *to_h) = rest[: n_high - 1], rest[n_high - 1 :]
    a, d, b, e = (rows * SUB for rows in PART_ROWS)

    def put(out, at, begin, size, *arrivals):
        total = kept[begin : begin + size, :] + got[begin : begin + size, :]
        for array, first in arrivals:
            total += array[first : first + size, :]
        out[at : at + size, :] = total

    n = n_high * a
    put(own_a, 0, 0, n, (got_y, 0))
    put(to_l, 0, n, n, (got_y, n))
    begin, y_begin = 2 * n, 2 * n
    put(own_d, 0, begin, 2 * d, (got_y, y_begin))
    for i, out in enumerate(to_h):
        put(out, 0, begin + 2 * d * (i + 1), 2 * d, (got_y, y_begin + 2 * d * (i + 1)))
    begin, n = begin + 2 * n_high * d, n_high * b
    put(own_b, 0, begin, n, (got_l, 0))
    put(to_y, 0, begin + n, n, (got_l, n))
    begin += 2 * n
    put(own_e, 0, begin, 2 * e, *[(array, 0) for array in got_h])
    put(to_y, n, begin + 2 * e, 2 * e, *[(array, 2 * e) for array in got_h])


def third_kernel(n_high, own_a, own_d, own_b, own_e, got_y, got_l, *rest):
    got_h, (own, to_l, *to_h) = rest[: n_high - 1], rest[n_high - 1 :]
    a, d, b, e = (rows * SUB for rows in PART_ROWS)

    def put(out, at, source, begin, size, *arrivals):
        total = source[begin : begin + size, :]
        for array, first in arrivals:
            total += array[first : first + size, :]
        out[at : at + size, :] = total

    put(own, 0, own_a, 0, a, (got_l, 0))
    put(own, a, own_d, 0, d, *[(array, 0) for array in got_h])
    put(own, a + d, own_b, 0, b, (got_y, 0))
    put(own, a + d + b, own_e, 0, e, (got_y, n_high * b))
    put(to_l, 0, own_d, d, d, *[(array, d) for array in got_h])
    put(to_l, d, own_e, e, e, (got_y, n_high * b + e))
    for i, out in enumerate(to_h):
        put(out, 0, own_a, (i + 1) * a, a, (got_l, (i + 1) * a))
        put(out, a, own_b, (i + 1) * b, b, (got_y, (i + 1) * b))


def last_kernel(before, got_l, *rest):
    got_h, (own,) = rest[:-1], rest[-1:]
    a, d, b, e = (rows * SUB for rows in PART_ROWS)
    for at, size, arrivals in (
        (0, a, [(array, 0) for array in got_h]),
        (a, d, [(got_l, 0)]),
        (a + d, b, [(array, a) for array in got_h]),
        (a + d + b, e, [(got_l, d)]),
    ):
        total = before[at : at + size, :]
        for array, first in arrivals:
            total += array[first : first + size, :]
        own[at : at + size, :] = total


def weigh(source, bank, out):
    bank_size, n_z, n_cell = bank.shape
    group = 2 * SUB

    for c in range(n_cell // LANES):
        cols = slice(c * LANES, (c + 1) * LANES)

        @pl.loop(0, n_z // group)
        def _(g):
            rows = pl.ds(pl.multiple_of(g * group, group), group)
            weights = [bank[t, rows, cols] for t in range(bank_size)]
            for b in range(out.shape[0]):
                total = None
                for t in range(bank_size):
                    value = weights[t] * source[b, t, c : c + 1, :]
                    total = value if total is None else total + value
                out[b, rows, cols] = total


def bank_rest_kernel(done, other, bank, out_hbm, block, sem):
    n_half = block.shape[0]
    rep = position()[0]
    first = pltpu.make_async_copy(done, out_hbm.at[pl.ds(rep * n_half, n_half)], sem.at[0])
    first.start()
    weigh(other, bank, block)
    second = pltpu.make_async_copy(block, out_hbm.at[pl.ds((1 - rep) * n_half, n_half)], sem.at[1])
    second.start()
    first.wait()
    second.wait()


def apply_bank(own, other, weight_bank):
    bank_size, n_z, n_cell = weight_bank.shape
    n_half = NB_DEV // 2
    vmem = pl.BlockSpec(memory_space=pltpu.VMEM)
    own, other = [array.reshape(n_half, bank_size, SUB, LANES) for array in (own, other)]
    params = pltpu.CompilerParams(vmem_limit_bytes=32 * MIB)
    done = pl.pallas_call(
        weigh,
        out_shape=jax.ShapeDtypeStruct((n_half, n_z, n_cell), jnp.float32),
        in_specs=[vmem] * 2,
        out_specs=vmem,
        compiler_params=params,
        name="bank_own",
    )(own, weight_bank)
    return pl.pallas_call(
        bank_rest_kernel,
        out_shape=jax.ShapeDtypeStruct((NB_DEV, n_z, n_cell), jnp.float32),
        in_specs=[vmem] * 3,
        out_specs=pl.BlockSpec(memory_space=pl.ANY),
        scratch_shapes=[
            pltpu.VMEM((n_half, n_z, n_cell), jnp.float32),
            pltpu.SemaphoreType.DMA((2,)),
        ],
        compiler_params=params,
        name="bank_rest",
    )(done, other, weight_bank)


def body(
    projections, images, transfer, pose_weights, pose_of, pose_blocks, pose_tiles, weight_bank
):
    bank_size = weight_bank.shape[0]
    n_blk = lax.axis_size("blk")
    n_high = n_blk // 4
    sent_away, kept_away, sent_stay, kept_stay = accumulate(
        projections, images, transfer, pose_weights, pose_of, pose_blocks, pose_tiles,
        bank_size, n_blk,
    )
    a, d, b, e = (rows * SUB for rows in PART_ROWS)

    def over_rep(array):
        return lax.ppermute(array, "rep", [(0, 1), (1, 0)])

    def over_blk(array, bits):
        return lax.ppermute(array, "blk", [(i, i ^ bits) for i in range(n_blk)])

    def over_h(arrays):
        return [over_blk(array, 4 * (i + 1)) for i, array in enumerate(arrays)]

    n_h = n_high - 1
    got_away, got_stay = over_rep(sent_away), over_rep(sent_stay)
    to_y, to_l, *to_h = in_vmem(
        first_kernel, "first", [2 * n_high * (a + d), 2 * n_high * b] + [4 * e] * n_h, kept_away, got_away
    )
    got_y, got_l, got_h = over_blk(to_y, 1), over_blk(to_l, 2), over_h(to_h)
    own_a, own_d, own_b, own_e, to_y, to_l, *to_h = in_vmem(
        functools.partial(second_kernel, n_high), "second",
        [n_high * a, 2 * d, n_high * b, 2 * e, n_high * b + 2 * e, n_high * a] + [2 * d] * n_h,
        kept_stay, got_stay, got_y, got_l, *got_h,
    )
    got_y, got_l, got_h = over_blk(to_y, 1), over_blk(to_l, 2), over_h(to_h)
    own, to_l, *to_h = in_vmem(
        functools.partial(third_kernel, n_high), "third", [a + d + b + e, d + e] + [a + b] * n_h,
        own_a, own_d, own_b, own_e, got_y, got_l, *got_h,
    )
    got_l, got_h = over_blk(to_l, 2), over_h(to_h)
    (own,) = in_vmem(last_kernel, "last", [a + d + b + e], own, got_l, *got_h)
    return apply_bank(own, over_rep(own), weight_bank)


def solution(mesh):
    placed = (
        P(("groups", "blk", "rep"), None, None, None),
        P(("groups", "blk", "rep"), None, None),
        P(("groups", "blk", "rep"), None, None),
        P(("groups", "blk", "rep"), None),
        P(("groups", "blk", "rep"), None),
        P("groups", None),
        P("groups", None),
        P(),
    )
    return jax.shard_map(
        body,
        mesh=mesh,
        in_specs=placed,
        out_specs=P(("groups", "blk"), None, None),
        check_vma=False,
    )
```
